32 devices in a mesh: dp: 2 (over core), ctx: 16 (over z, y, x).
Axes of the slice: x: 2, y: 2, z: 4, core: 2. Of those that a mesh axis runs over, the one named last changes fastest.
Arguments:
- features: bfloat16 [2, 4096, 2560], P('dp', 'ctx'), may hold values from -6 to 6
- write_keys: bfloat16 [2, 4096, 128], P('dp', 'ctx'), may hold values from -0.75 to 0.75
- read_queries: bfloat16 [2, 4096, 128], P('dp', 'ctx'), may hold values from -0.75 to 0.75
- step_logits: float32 [2, 40, 4096], P('dp', None, 'ctx'), may hold values from -6 to 6
- step_bias: float32 [40], replicated, may hold values from -1 to 1
- decay_log: float32 [40], replicated, may hold values from -16 to -2
- skip_gain: float32 [40], replicated, may hold values from 0.5 to 1.5
- doc_starts: int32 [2, 4], P('dp'), may hold values from 0 to 4095, as said below
- out_grad: bfloat16 [2, 4096, 2560], P('dp', 'ctx'), may hold values from -20 to 20
Outputs:
- mixed: bfloat16 [2, 4096, 2560], P('dp', 'ctx')
- feature_grad: bfloat16 [2, 4096, 2560], P('dp', 'ctx')
- write_grad: bfloat16 [2, 4096, 128], P('dp', 'ctx')
- read_grad: bfloat16 [2, 4096, 128], P('dp', 'ctx')
- step_grad: float32 [2, 40, 4096], P('dp', None, 'ctx')
- bias_grad: float32 [40], replicated
- decay_grad: float32 [40], replicated
- skip_grad: float32 [40], replicated
The draws below stay inside these ranges and needn't reach their ends.
Inputs may be any that keep to these rules, and one draw needn't show every extreme that they name: `doc_starts`: each row is ascending with distinct entries, begins with 0 and ends with 4095; row b holds the first positions of the documents packed into sequence b.
All inputs are finite; a program needn't handle non-finite values.
Results may differ from the reference program's by a relative error of at most 0.002.
Values sent between devices are 32-bit elements; how exact they have to be, the bound alone decides.
No kernel may reach another device: no remote copies, remote signals or barrier semaphores. Data moves between devices by JAX's collectives and lax.ppermute only.
A program may use at most 128 MiB of HBM per device.

```python
import math
import jax
import jax.numpy as jnp
from jax import lax

HEADS = 40
HEAD_DIM = 64
STATE = 128
GROUP_HEADS = 2
L_DEV = 256
BATCH = 2
SEQ = 4096
DOCS = 4
N_CTX = 16


def draw_decay_log(key, part):
    key = jax.random.fold_in(key, 11)
    uniform_draw = jax.random.uniform(key, (HEADS,), jnp.float32)
    lowest = math.log(1.0 / SEQ)
    highest = math.log(0.05)
    return (lowest + uniform_draw * (highest - lowest)).astype(jnp.float32)


def draw_doc_starts(key, part):
    key = jax.random.fold_in(key, 23)
    window = SEQ // 4

    def one_row(row_key):
        side_bit = jax.random.randint(jax.random.fold_in(row_key, 1), (), 0, 2)
        window_start = jnp.where(side_bit == 1, SEQ - 1 - window, 1).astype(jnp.int32)
        chosen = jax.random.permutation(jax.random.fold_in(row_key, 2), window)[:DOCS - 2].astype(jnp.int32) + window_start
        inner = jnp.sort(chosen)
        return jnp.concatenate([jnp.zeros((1,), jnp.int32), inner, jnp.full((1,), SEQ - 1, jnp.int32)])
    return jax.vmap(one_row)(jax.random.split(key, BATCH))


def draw_out_grad(key, part):
    key = jax.random.fold_in(key, 37)
    shape_all = (BATCH, SEQ, HEADS * HEAD_DIM)
    ramp = 1.0 + 2.0 * jnp.arange(SEQ, dtype=jnp.float32) / SEQ
    values = jnp.clip(jax.random.normal(key, shape_all, jnp.float32), -6.0, 6.0) * ramp[None, :, None]
    return values.astype(jnp.bfloat16)


def block_levels(own_key, shape, cuts, low, top_value):
    level = 1.0
    for axis_at, parts in cuts:
        heights = jax.random.uniform(jax.random.fold_in(jax.random.fold_in(own_key, 6), axis_at), (parts,), jnp.float32, low / len(cuts), top_value / len(cuts))
        level = level * jnp.repeat(jnp.exp(heights), shape[axis_at] // parts).reshape((-1,) + (1,) * (len(shape) - 1 - axis_at))
    return level


def normal_values(rng, extent, spread, most, shards=(), kind=jnp.bfloat16):
    gain = block_levels(rng, extent, shards, -0.22, 0.18) if shards else 1.0
    values = jax.random.normal(rng, extent, jnp.float32) * spread * gain
    return jnp.minimum(jnp.maximum(values, -most), most).astype(kind)


def setup_inputs(seed: int = 0) -> dict:
    streams_of = jax.random.split(jax.random.key(seed), 10)
    return {
        "features": normal_values(streams_of[0], (BATCH, SEQ, HEADS * HEAD_DIM), 1.0, 6.0, ((0, 2), (1, 16))),
        "write_keys": normal_values(streams_of[1], (BATCH, SEQ, STATE), (1.0 / (4 * STATE * L_DEV) ** 0.25), 0.75, ((0, 2), (1, 16))),
        "read_queries": normal_values(streams_of[2], (BATCH, SEQ, STATE), (1.0 / (4 * STATE * L_DEV) ** 0.25), 0.75, ((0, 2), (1, 16))),
        "step_logits": normal_values(streams_of[3], (BATCH, HEADS, SEQ), 1.0, 6.0, ((0, 2), (2, 16)), jnp.float32),
        "step_bias": jnp.clip(jax.random.uniform(streams_of[4], (HEADS,), jnp.float32, -1.0, 1.0), -1.0, 1.0),
        "decay_log": draw_decay_log(jax.random.fold_in(streams_of[9], 71), 0),
        "skip_gain": jnp.clip(jax.random.uniform(streams_of[6], (HEADS,), jnp.float32, 0.5, 1.5), 0.5, 1.5),
        "doc_starts": draw_doc_starts(jax.random.fold_in(streams_of[9], 71), 0),
        "out_grad": draw_out_grad(jax.random.fold_in(streams_of[9], 71), 0),
    }


EXACT = lax.Precision.HIGHEST

def widen(values, repeat_by):
    return jnp.repeat(values, repeat_by, axis=-1)

def step_decays(logit_block, step_bias, decay_log):
    stride = jax.nn.softplus(logit_block + step_bias[:, None])
    decay_rate = -jnp.exp(decay_log)
    cumulative = jnp.cumsum(stride * decay_rate[:, None], axis=1)
    return (stride, cumulative)

def segments(doc_starts, start_pos, length):
    positions = start_pos + jnp.arange(length, dtype=jnp.int32)
    segment = lax.optimization_barrier(jnp.sum((doc_starts[None, :] <= positions[:, None]).astype(jnp.int32), axis=1))
    entry_segment = jnp.sum((doc_starts <= start_pos - 1).astype(jnp.int32))
    return (segment, entry_segment)

def block_state(feature_block, write_block, logit_block, step_bias, decay_log, own_last, linked):
    stride, cumulative = step_decays(logit_block, step_bias, decay_log)
    weights = own_last[None, :] * jnp.exp(cumulative[:, -1:] - cumulative) * stride
    head_size = feature_block.shape[1] // stride.shape[0]
    scaled = feature_block * widen(weights.T, head_size)
    state_end = jnp.dot(write_block.T, scaled, precision=EXACT, preferred_element_type=jnp.float32)
    totals = jnp.exp(cumulative[:, -1]) * linked
    return (state_end, totals)

def intra_group(cum_group, stride_group, feature_group, scores, same_doc):
    gaps = cum_group[:, :, None] - cum_group[:, None, :]
    decays = jnp.exp(jnp.where(same_doc[None], gaps, -jnp.inf))
    mixing = decays * scores[None] * stride_group[:, None, :]
    head_count = cum_group.shape[0]
    per_head = feature_group.reshape(feature_group.shape[0], head_count, -1)
    result = jnp.einsum('htu,uhp->thp', mixing, per_head, precision=EXACT)
    return result.reshape(feature_group.shape[0], -1)

def block_main(feature_block, write_block, read_block, logit_block, step_bias, decay_log, skip_gain, segment):
    stride, cumulative = step_decays(logit_block, step_bias, decay_log)
    length = feature_block.shape[0]
    head_count = stride.shape[0]
    head_size = feature_block.shape[1] // head_count
    groups = head_count // GROUP_HEADS
    ordinal = jnp.arange(length, dtype=jnp.int32)
    same_doc = (segment[:, None] == segment[None, :]) & (ordinal[:, None] >= ordinal[None, :])
    scores = jnp.dot(read_block, write_block.T, precision=EXACT, preferred_element_type=jnp.float32)
    cum_stack = cumulative.reshape(groups, GROUP_HEADS, length)
    stride_stack = stride.reshape(groups, GROUP_HEADS, length)
    feature_stack = feature_block.reshape(length, groups, GROUP_HEADS * head_size).transpose(1, 0, 2)

    def one_group(packed):
        return intra_group(packed[0], packed[1], packed[2], scores, same_doc)
    pieces = lax.map(jax.checkpoint(one_group), (cum_stack, stride_stack, feature_stack))
    inside = pieces.transpose(1, 0, 2).reshape(length, -1)
    return inside + feature_block * widen(skip_gain, head_size)

def block_carry(read_block, logit_block, step_bias, decay_log, keep_in, state_in):
    stride, cumulative = step_decays(logit_block, step_bias, decay_log)
    factor = keep_in[:, None] * jnp.exp(cumulative.T)
    head_size = state_in.shape[1] // factor.shape[1]
    return jnp.dot(read_block, state_in, precision=EXACT, preferred_element_type=jnp.float32) * widen(factor, head_size)

def sequence_forward(features, write_keys, read_queries, step_logits, step_bias, decay_log, skip_gain, doc_starts):
    head_count = step_logits.shape[0]
    feature_blocks = features.reshape(N_CTX, L_DEV, -1)
    write_blocks = write_keys.reshape(N_CTX, L_DEV, -1)
    read_blocks = read_queries.reshape(N_CTX, L_DEV, -1)
    logit_blocks = step_logits.reshape(head_count, N_CTX, L_DEV).transpose(1, 0, 2)
    offsets = jnp.arange(N_CTX, dtype=jnp.int32) * L_DEV
    head_size = features.shape[1] // head_count

    def advance(carried, packed):
        feature_block, write_block, read_block, logit_block, start_pos = packed
        segment, entry_segment = segments(doc_starts, start_pos, L_DEV)
        keep_in = (segment == entry_segment).astype(jnp.float32)
        own_last = (segment == segment[-1]).astype(jnp.float32)
        linked = (segment[-1] == entry_segment).astype(jnp.float32)
        result = block_main(feature_block, write_block, read_block, logit_block, step_bias, decay_log, skip_gain, segment)
        result = result + block_carry(read_block, logit_block, step_bias, decay_log, keep_in, carried)
        state_end, totals = block_state(feature_block, write_block, logit_block, step_bias, decay_log, own_last, linked)
        carried = carried * widen(totals, head_size)[None, :] + state_end
        return (carried, result)
    initial = jnp.zeros((write_keys.shape[1], features.shape[1]), jnp.float32)
    _, outputs = lax.scan(jax.checkpoint(advance), initial, (feature_blocks, write_blocks, read_blocks, logit_blocks, offsets))
    return outputs.reshape(features.shape[0], -1)

def reference(features, write_keys, read_queries, step_logits, step_bias, decay_log, skip_gain, doc_starts, out_grad):
    mixed_rows, feature_rows, write_rows, read_rows, step_rows = ([], [], [], [], [])
    bias_total = jnp.zeros_like(step_bias)
    decay_total = jnp.zeros_like(decay_log)
    skip_total = jnp.zeros_like(skip_gain)
    for member in range(features.shape[0]):
        starts_row = doc_starts[member]

        def sequence_fn(feat_in, write_in, read_in, logit_in, bias_in, decay_in, skip_in, starts_row=starts_row):
            return sequence_forward(feat_in, write_in, read_in, logit_in, bias_in, decay_in, skip_in, starts_row)
        mixed_out, pullback = jax.vjp(sequence_fn, features[member].astype(jnp.float32), write_keys[member].astype(jnp.float32), read_queries[member].astype(jnp.float32), step_logits[member], step_bias, decay_log, skip_gain)
        gradients = pullback(out_grad[member].astype(jnp.float32))
        mixed_rows.append(mixed_out.astype(jnp.bfloat16))
        feature_rows.append(gradients[0].astype(jnp.bfloat16))
        write_rows.append(gradients[1].astype(jnp.bfloat16))
        read_rows.append(gradients[2].astype(jnp.bfloat16))
        step_rows.append(gradients[3])
        bias_total = bias_total + gradients[4]
        decay_total = decay_total + gradients[5]
        skip_total = skip_total + gradients[6]
    return (jnp.stack(mixed_rows), jnp.stack(feature_rows), jnp.stack(write_rows), jnp.stack(read_rows), jnp.stack(step_rows), bias_total, decay_total, skip_total)
```

```python
import functools

import jax
import jax.numpy as jnp
from jax import lax
from jax.experimental import pallas as pl
from jax.experimental.pallas import tpu as pltpu
from jax.sharding import PartitionSpec as P

F32 = jnp.float32
BF16 = jnp.bfloat16
PLANE = 4
LANES = 128
LOG2E = 1.4426950408889634
FAR = -1e30
VMEM_BYTES = 56 * 1024 * 1024
VMEM = pl.BlockSpec(memory_space=pltpu.VMEM)
SMEM = pl.BlockSpec(memory_space=pltpu.SMEM)


def iota(shape, axis):
    return lax.broadcasted_iota(jnp.int32, shape, axis)


def matmul(left, right):
    return lax.dot_general(left, right, (((1,), (0,)), ((), ())), preferred_element_type=F32)


def matmul_nt(left, right):
    return lax.dot_general(left, right, (((1,), (1,)), ((), ())), preferred_element_type=F32)


def split2(value):
    high = value.astype(BF16)
    return high, (value - high.astype(F32)).astype(BF16)


def split3(value):
    high = value.astype(BF16)
    rest = value - high.astype(F32)
    middle = rest.astype(BF16)
    return high, middle, (rest - middle.astype(F32)).astype(BF16)


def column(row):
    count = row.shape[1]
    eye = iota((count, count), 0) == iota((count, count), 1)
    return jnp.sum(jnp.where(eye, row, 0.0), axis=1, keepdims=True)


def stacked_columns(rows):
    parts = [part.astype(F32) for part in split3(rows)]
    spare = LANES - 3 * rows.shape[0]
    if spare:
        parts.append(jnp.zeros((spare, rows.shape[1]), F32))
    return jnp.concatenate(parts, axis=0).T.astype(BF16)


def head_of(shape, axis, head_dim):
    return lax.div(iota(shape, axis), head_dim)


def spread_matrix(heads, first, width, head_dim):
    lane = iota((LANES, width), 0)
    head = head_of((LANES, width), 1, head_dim) + first
    hit = (lane == head) | (lane == head + heads) | (lane == head + 2 * heads)
    return jnp.where(hit, 1.0, 0.0).astype(BF16)


def gather_matrix(first, width, head_dim):
    head = head_of((width, LANES), 0, head_dim) + first
    return jnp.where(iota((width, LANES), 1) == head, 1.0, 0.0).astype(BF16)


def softplus(value):
    return jnp.maximum(value, 0.0) + jnp.log1p(jnp.exp(-jnp.abs(value)))


def document_at(starts_ref, position):
    total = jnp.zeros_like(position)
    for entry in range(starts_ref.shape[1]):
        total = total + (starts_ref[0, entry] <= position).astype(jnp.int32)
    return total


def place():
    index = lax.axis_index("ctx")
    return index, lax.rem(index, PLANE)


def states_kernel(
    head_dim, starts, logits, bias, decay, features, cotangent, writes, reads,
    send0, send1, send2, send3, weight_cols, factor_cols, cum_cols, cum_rows, stride_out, log_out,
):
    index, own = place()
    heads, length = logits.shape
    state = writes.shape[1]
    width = features.shape[1] // PLANE
    first = index * length
    stride = softplus(logits[...] + column(bias[...]))
    log_decay = stride * column(-jnp.exp(decay[...]))
    upto = jnp.where(iota((length, length), 0) <= iota((length, length), 1), 1.0, 0.0).astype(BF16)
    parts = matmul(jnp.concatenate(split3(log_decay), axis=0), upto)
    cum = parts[:heads] + parts[heads : 2 * heads] + parts[2 * heads :]
    segment = document_at(starts, first + iota((1, length), 1))
    entry = document_at(starts, jnp.full((1, 1), first - 1, jnp.int32))
    leave = document_at(starts, jnp.full((1, 1), first + length - 1, jnp.int32))
    own_last = jnp.where(segment == leave, 1.0, 0.0)
    keep_in = jnp.where(segment == entry, 1.0, 0.0)
    weight = own_last * jnp.exp(cum[:, length - 1 :] - cum) * stride
    factor = keep_in * jnp.exp(cum)
    weight_stack = stacked_columns(weight)
    factor_stack = stacked_columns(factor)
    weight_cols[...] = weight_stack
    factor_cols[...] = factor_stack
    write_t = writes[...].astype(F32).T.astype(BF16)
    read_t = reads[...].astype(F32).T.astype(BF16)
    for distance, send in enumerate((send0, send1, send2, send3)):
        quarter = own ^ distance
        cols = pl.ds(pl.multiple_of(quarter * width, LANES), width)
        spread = spread_matrix(heads, quarter * (heads // PLANE), width, head_dim)
        high, low = split2(features[:, cols].astype(F32) * matmul(weight_stack, spread))
        send[0:state] = matmul(write_t, high) + matmul(write_t, low)
        wide = matmul(factor_stack, spread)
        high, low = split2(cotangent[:, cols].astype(F32) * wide)
        send[state : 2 * state] = matmul(read_t, high) + matmul(read_t, low)
        send[2 * state :] = jnp.broadcast_to(wide[length - 1 :], (8, width))
    cum_cols[...] = stacked_columns(cum * LOG2E)
    cum_rows[...] = cum * LOG2E - jnp.log2(stride)
    stride_out[...] = stride
    log_out[...] = log_decay


def inner_kernel(
    head_dim, starts, cum_cols, cum_rows, features, cotangent, writes, reads,
    inside, feature_part, write_part, read_part, skip_part, scores_ref, mask_ref, grad_ref,
):
    index, _ = place()
    length = features.shape[0]
    heads = cum_rows.shape[0]
    pair = 2 * head_dim
    first = index * length
    segment_row = document_at(starts, first + iota((1, length), 1))
    segment_col = document_at(starts, first + iota((length, 1), 0))
    allowed = (segment_row == segment_col) & (iota((length, length), 0) >= iota((length, length), 1))
    mask_ref[...] = jnp.where(allowed, 0.0, FAR)
    scores_ref[...] = matmul_nt(reads[...], writes[...])
    grad_ref[...] = jnp.zeros_like(grad_ref)

    def one_pair(at, carry):
        cols = pl.ds(pl.multiple_of(at * pair, LANES), pair)
        feature = features[:, cols]
        grad = cotangent[:, cols]
        grad_f32 = grad.astype(F32)
        grad_t = grad_f32.T.astype(BF16)
        skip_part[:, cols] = jnp.sum(grad_f32 * feature.astype(F32), axis=0, keepdims=True)
        second = iota((length, pair), 1) >= head_dim
        values, back = [], []
        for side in range(2):
            head = at * 2 + side
            lane = iota((LANES, LANES), 0)
            pick = (lane == head) | (lane == head + heads) | (lane == head + 2 * heads)
            upper = matmul(cum_cols[...], jnp.where(pick, 1.0, 0.0).astype(BF16))
            upper = jnp.concatenate([upper] * (length // LANES), axis=1)
            weight = jnp.exp2(upper - cum_rows[pl.ds(head, 1), :] + mask_ref[...])
            high, low = split2(weight * scores_ref[...])
            values.append(matmul(high, feature) + matmul(low, feature))
            rows = grad_t[side * head_dim : (side + 1) * head_dim]
            back.append(matmul(rows, high) + matmul(rows, low))
            only = jnp.where(second == (side == 1), grad_f32, 0.0).astype(BF16)
            grad_ref[...] += matmul_nt(only, feature) * weight
        inside[:, cols] = jnp.where(second, values[1], values[0])
        feature_part[:, cols] = jnp.concatenate(back, axis=0).T
        return carry

    lax.fori_loop(0, heads // 2, one_pair, 0)
    score_grad = grad_ref[...]
    high, low = split2(score_grad)
    read_part[...] = matmul(high, writes[...]) + matmul(low, writes[...])
    high, low = split2(score_grad.T)
    write_part[...] = matmul(high, reads[...]) + matmul(low, reads[...])


def plane_kernel(state, part0, part1, part2, part3, up, down):
    _, own = place()
    parts = (part0, part1, part2, part3)
    for at in range(PLANE):

        @pl.when(own == at)
        def _(at=at):
            block = [parts[j ^ at] for j in range(PLANE)]
            keeps = [ref[2 * state : 2 * state + 1] for ref in block]
            total = block[0][0:state]
            for j in range(1, PLANE):
                total = total * keeps[j] + block[j][0:state]
            up[0:state] = total
            total = block[PLANE - 1][state : 2 * state]
            for j in reversed(range(PLANE - 1)):
                total = total * keeps[j] + block[j][state : 2 * state]
            down[0:state] = total
            keep = jnp.broadcast_to(
                keeps[0] * keeps[1] * keeps[2] * keeps[3], (8, up.shape[1])
            )
            up[state:] = keep
            down[state:] = keep


def arrived(state, came):
    total, keep = came[0][0:state], came[0][state : state + 1]
    for ref in came[1:]:
        total = total + keep * ref[0:state]
        keep = keep * ref[state : state + 1]
    return total, keep


def link_kernel(state, count, up, down, *refs):
    ups, downs, (up_out, down_out) = refs[:count], refs[count : 2 * count], refs[2 * count :]
    for own, came, out in ((up, ups, up_out), (down, downs, down_out)):
        total, keep = arrived(state, came)
        out[0:state] = own[0:state] + own[state : state + 1] * total
        out[state:] = own[state:] * keep


def spread_kernel(state, count, *refs):
    parts = refs[:PLANE]
    ups = refs[PLANE : PLANE + count]
    downs = refs[PLANE + count : PLANE + 2 * count]
    outs = refs[PLANE + 2 * count :]
    _, own = place()
    entering, returning = arrived(state, ups)[0], arrived(state, downs)[0]
    for at in range(PLANE):

        @pl.when(own == at)
        def _(at=at):
            block = [parts[j ^ at] for j in range(PLANE)]
            keeps = [ref[2 * state : 2 * state + 1] for ref in block]
            total = entering
            for j in range(PLANE):
                outs[j ^ at][0:state] = total
                if j < PLANE - 1:
                    total = total * keeps[j] + block[j][0:state]
            total = returning
            for j in reversed(range(PLANE)):
                outs[j ^ at][state:] = total
                if j > 0:
                    total = total * keeps[j] + block[j][state : 2 * state]


def finish_kernel(
    head_dim, own_ref, logits, bias, decay, skip, weight_cols, factor_cols, stride_ref, log_ref,
    features, cotangent, writes, reads, inside, feature_part, write_part, read_part, skip_part,
    part0, part1, part2, part3, have0, have1, have2, have3,
    mixed, feature_grad, write_grad, read_grad, step_grad, sums, row_acc, col_acc, last_acc, read_acc, write_acc, skip_acc,
):
    heads, length = logits.shape
    state = writes.shape[1]
    width = features.shape[1]
    step = pl.program_id(0)
    quarter = own_ref[0] ^ step
    first = quarter * (heads // PLANE)

    @pl.when(step == 0)
    def _():
        for ref in (row_acc, col_acc, last_acc, read_acc, write_acc, skip_acc):
            ref[...] = jnp.zeros_like(ref)

    spread = spread_matrix(heads, first, width, head_dim)
    gather = gather_matrix(first, width, head_dim)
    skip_stack = stacked_columns(jnp.broadcast_to(column(skip[...]), (heads, LANES)))
    skip_wide = matmul(skip_stack[0:16], spread)[0:1]
    factor = matmul(factor_cols[...], spread)
    weight = matmul(weight_cols[...], spread)
    feature = features[...].astype(F32)
    grad = cotangent[...].astype(F32)
    writes2 = jnp.concatenate([writes[...]] * 2, axis=1)
    reads2 = jnp.concatenate([reads[...]] * 2, axis=1)

    def add_heads(ref, value):
        high, low = split2(value)
        ref[...] += matmul(high, gather) + matmul(low, gather)

    for distance, (part, have) in enumerate(
        zip((part0, part1, part2, part3), (have0, have1, have2, have3))
    ):

        @pl.when(step == distance)
        def _(part=part, have=have):
            entering = have[0:state]
            stack = jnp.concatenate(split2(entering), axis=0)
            total = inside[...] + factor * matmul(reads2, stack)
            mixed[...] = (total + skip_wide * feature).astype(BF16)
            add_heads(row_acc, grad * total)
            high, low = split2(factor * grad)
            read_acc[...] += matmul_nt(high, stack) + matmul_nt(low, stack)
            returning = have[state:]
            keep = part[2 * state : 2 * state + 1]
            leaving = keep * entering + part[0:state]
            add_heads(last_acc, jnp.sum((returning * leaving).reshape(state // 8, 8, width), axis=0))
            stack = jnp.concatenate(split2(returning), axis=0)
            total = feature_part[...] + weight * matmul(writes2, stack)
            feature_grad[...] = (total + skip_wide * grad).astype(BF16)
            add_heads(col_acc, feature * total)
            high, low = split2(weight * feature)
            write_acc[...] += matmul_nt(high, stack) + matmul_nt(low, stack)

    add_heads(skip_acc, jnp.broadcast_to(skip_part[...], (8, width)))

    @pl.when(step == PLANE - 1)
    def _():
        read_grad[...] = (read_part[...] + read_acc[:, :state] + read_acc[:, state:]).astype(BF16)
        write_grad[...] = (write_part[...] + write_acc[:, :state] + write_acc[:, state:]).astype(BF16)
        rows = row_acc[...].T[:heads]
        cols = col_acc[...].T[:heads]
        last = column(jnp.sum(last_acc[...], axis=0, keepdims=True))[:heads]
        stride = stride_ref[...]
        gap_grad = rows - cols + jnp.where(iota((heads, length), 1) == length - 1, last, 0.0)
        onward = jnp.where(iota((length, length), 0) >= iota((length, length), 1), 1.0, 0.0).astype(BF16)
        parts = matmul(jnp.concatenate(split3(gap_grad), axis=0), onward)
        log_grad = parts[:heads] + parts[heads : 2 * heads] + parts[2 * heads :]
        rate = column(-jnp.exp(decay[...]))
        slope = 1.0 / (1.0 + jnp.exp(-(logits[...] + column(bias[...]))))
        step_value = (cols / stride + rate * log_grad) * slope
        step_grad[...] = step_value
        bias_sum = jnp.sum(step_value, axis=1, keepdims=True)
        decay_sum = jnp.sum(log_grad * log_ref[...], axis=1, keepdims=True)
        lane = iota((heads, LANES), 1)
        table = jnp.where(lane == 0, bias_sum, jnp.where(lane == 1, decay_sum, 0.0))
        table = jnp.concatenate([table, jnp.zeros((LANES - heads, LANES), F32)], axis=0).T[0:8]
        sums[...] = jnp.where(iota((8, LANES), 0) == 2, skip_acc[...], table)


def params(**more):
    return pltpu.CompilerParams(vmem_limit_bytes=VMEM_BYTES, **more)


def cost(flops, size):
    return pl.CostEstimate(flops=flops, bytes_accessed=size, transcendentals=0)


def struct(shape, dtype=F32):
    return jax.ShapeDtypeStruct(shape, dtype)


def local(
    features, write_keys, read_queries, step_logits, step_bias, decay_log, skip_gain, doc_starts, out_grad
):
    features, writes, reads, logits, cotangent = (
        features[0], write_keys[0], read_queries[0], step_logits[0], out_grad[0]
    )
    length, wide = features.shape
    heads = logits.shape[0]
    state = writes.shape[1]
    head_dim = wide // heads
    width = wide // PLANE
    bias, decay, skip = step_bias[None], decay_log[None], skip_gain[None]
    blocks = lax.axis_size("ctx")

    def exchange(value, distance):
        return lax.ppermute(value, "ctx", [(k, k ^ distance) for k in range(blocks)])

    def shift(value, distance):
        pairs = [(k, k + distance) for k in range(blocks) if 0 <= k + distance < blocks]
        return lax.ppermute(value, "ctx", pairs)

    stack = struct((length, LANES), BF16)
    small = struct((heads, length))
    message = struct((2 * state + 8, width))
    *sent, weight_cols, factor_cols, cum_cols, cum_rows, stride, log_decay = pl.pallas_call(
        functools.partial(states_kernel, head_dim),
        out_shape=[message] * PLANE + [stack] * 3 + [small] * 3,
        in_specs=[SMEM] + [VMEM] * 7,
        out_specs=[VMEM] * (PLANE + 6),
        compiler_params=params(),
        cost_estimate=cost(4 * 10**9, 6 * 10**6),
        name="states",
    )(doc_starts, logits, bias, decay, features, cotangent, writes, reads)
    parts = [sent[0]] + [exchange(sent[d], d) for d in range(1, PLANE)]

    inside, feature_part, write_part, read_part, skip_part = pl.pallas_call(
        functools.partial(inner_kernel, head_dim),
        out_shape=[
            struct((length, wide)),
            struct((length, wide)),
            struct((length, state)),
            struct((length, state)),
            struct((1, wide)),
        ],
        in_specs=[SMEM] + [VMEM] * 6,
        out_specs=[VMEM] * 5,
        scratch_shapes=[pltpu.VMEM((length, length), F32)] * 3,
        compiler_params=params(),
        cost_estimate=cost(2 * 10**10, 10**7),
        name="inner",
    )(doc_starts, cum_cols, cum_rows, features, cotangent, writes, reads)

    sums_shape = struct((state + 8, width))
    up, down = pl.pallas_call(
        functools.partial(plane_kernel, state),
        out_shape=[sums_shape] * 2,
        in_specs=[VMEM] * PLANE,
        out_specs=[VMEM] * 2,
        compiler_params=params(),
        cost_estimate=cost(10**6, 4 * 10**6),
        name="plane",
    )(*parts)
    planes = blocks // PLANE
    ups, downs = [], []
    near_up, near_down = up, down
    reach = 1
    while reach < planes:
        ups.append(shift(near_up, PLANE * reach))
        downs.append(shift(near_down, -PLANE * reach))
        reach *= 2
        if reach < planes:
            near_up, near_down = pl.pallas_call(
                functools.partial(link_kernel, state, len(ups)),
                out_shape=[sums_shape] * 2,
                in_specs=[VMEM] * (2 + 2 * len(ups)),
                out_specs=[VMEM] * 2,
                compiler_params=params(),
                cost_estimate=cost(10**6, 2 * 10**6),
                name="link",
            )(up, down, *ups, *downs)
    haves = pl.pallas_call(
        functools.partial(spread_kernel, state, len(ups)),
        out_shape=[struct((2 * state, width))] * PLANE,
        in_specs=[VMEM] * (PLANE + 2 * len(ups)),
        out_specs=[VMEM] * PLANE,
        compiler_params=params(),
        cost_estimate=cost(10**6, 6 * 10**6),
        name="spread",
    )(*parts, *ups, *downs)
    haves = [haves[0]] + [exchange(haves[d], d) for d in range(1, PLANE)]

    def whole(shape):
        return pl.BlockSpec(shape, lambda step, own: (0,) * len(shape))

    by_quarter = pl.BlockSpec((length, width), lambda step, own: (0, own[0] ^ step))
    row_quarter = pl.BlockSpec((1, width), lambda step, own: (0, own[0] ^ step))
    row_small = whole((1, heads))
    tokens = whole((length, state))
    own = jnp.reshape(lax.rem(lax.axis_index("ctx"), PLANE), (1,))
    mixed, feature_grad, write_grad, read_grad, step_grad, sums = pl.pallas_call(
        functools.partial(finish_kernel, head_dim),
        out_shape=[
            struct((length, wide), BF16),
            struct((length, wide), BF16),
            struct((length, state), BF16),
            struct((length, state), BF16),
            small,
            struct((8, LANES)),
        ],
        grid_spec=pltpu.PrefetchScalarGridSpec(
            num_scalar_prefetch=1,
            grid=(PLANE,),
            in_specs=[whole((heads, length))]
            + [row_small] * 3
            + [whole((length, LANES))] * 2
            + [whole((heads, length))] * 2
            + [by_quarter] * 2
            + [tokens] * 2
            + [by_quarter] * 2
            + [tokens] * 2
            + [row_quarter]
            + [whole((2 * state + 8, width))] * PLANE
            + [whole((2 * state, width))] * PLANE,
            out_specs=[
                by_quarter,
                by_quarter,
                tokens,
                tokens,
                whole((heads, length)),
                whole((8, LANES)),
            ],
            scratch_shapes=[
                pltpu.VMEM((length, LANES), F32),
                pltpu.VMEM((length, LANES), F32),
                pltpu.VMEM((8, LANES), F32),
                pltpu.VMEM((length, 2 * state), F32),
                pltpu.VMEM((length, 2 * state), F32),
                pltpu.VMEM((8, LANES), F32),
            ],
        ),
        compiler_params=params(dimension_semantics=("arbitrary",)),
        cost_estimate=cost(10**10, 2 * 10**7),
        name="finish",
    )(
        own, logits, bias, decay, skip, weight_cols, factor_cols, stride, log_decay, features, cotangent,
        writes, reads, inside, feature_part, write_part, read_part, skip_part, *sent, *haves,
    )
    for distance in [2**bit for bit in range(blocks.bit_length() - 1)]:
        sums = sums + exchange(sums, distance)
    members = lax.axis_size("dp")
    for distance in [2**bit for bit in range(members.bit_length() - 1)]:
        sums = sums + lax.ppermute(sums, "dp", [(k, k ^ distance) for k in range(members)])
    return (
        mixed[None],
        feature_grad[None],
        write_grad[None],
        read_grad[None],
        step_grad[None],
        sums[0, :heads],
        sums[1, :heads],
        sums[2, :heads],
    )


def solution(mesh):
    by_tokens = P("dp", "ctx", None)
    by_heads = P("dp", None, "ctx")
    in_specs = (by_tokens, by_tokens, by_tokens, by_heads, P(), P(), P(), P("dp", None), by_tokens)
    out_specs = (by_tokens, by_tokens, by_tokens, by_tokens, by_heads, P(), P(), P())
    return jax.shard_map(local, mesh=mesh, in_specs=in_specs, out_specs=out_specs, check_vma=False)
```

```python
import functools

import jax
import jax.numpy as jnp
import numpy as np
from jax import lax
from jax.experimental import pallas as pl
from jax.experimental.pallas import tpu as pltpu
from jax.sharding import PartitionSpec as P

F32 = jnp.float32
BF16 = jnp.bfloat16
QUARTERS = 4
HALVES = 2
GROUP = QUARTERS * HALVES
LANES = 128
LOG2E = 1.4426950408889634
FAR = -1e30
VMEM = pl.BlockSpec(memory_space=pltpu.VMEM)
SMEM = pl.BlockSpec(memory_space=pltpu.SMEM)
ANY = pl.BlockSpec(memory_space=pl.ANY)


def iota(shape, axis):
    return lax.broadcasted_iota(jnp.int32, shape, axis)


def matmul(left, right):
    return lax.dot_general(left, right, (((1,), (0,)), ((), ())), preferred_element_type=F32)


def matmul_nt(left, right):
    return lax.dot_general(left, right, (((1,), (1,)), ((), ())), preferred_element_type=F32)


def split2(value):
    high = value.astype(BF16)
    return high, (value - high.astype(F32)).astype(BF16)


def split3(value):
    high = value.astype(BF16)
    rest = value - high.astype(F32)
    middle = rest.astype(BF16)
    return high, middle, (rest - middle.astype(F32)).astype(BF16)


def column(row):
    count = row.shape[1]
    eye = iota((count, count), 0) == iota((count, count), 1)
    return jnp.sum(jnp.where(eye, row, 0.0), axis=1, keepdims=True)


def stacked_columns(rows):
    parts = [part.astype(F32) for part in split3(rows)]
    spare = LANES - 3 * rows.shape[0]
    if spare:
        parts.append(jnp.zeros((spare, rows.shape[1]), F32))
    return jnp.concatenate(parts, axis=0).T.astype(BF16)


def spread_table(heads, head_dim):
    table = np.zeros((LANES, heads * head_dim), np.float32)
    for head in range(heads):
        for part in range(3):
            table[part * heads + head, head * head_dim : (head + 1) * head_dim] = 1.0
    return jnp.asarray(table, BF16)


def softplus(value):
    return jnp.maximum(value, 0.0) + jnp.log1p(jnp.exp(-jnp.abs(value)))


def document_at(starts_ref, position):
    total = jnp.zeros_like(position)
    for entry in range(starts_ref.shape[1]):
        total = total + (starts_ref[0, entry] <= position).astype(jnp.int32)
    return total


def group_place():
    return lax.rem(lax.axis_index("ctx"), GROUP)


def share_out(own, quarter_of_state, sends, scratch, part):
    mine = lax.div(own, QUARTERS)
    for distance in range(QUARTERS):
        scratch[...] = quarter_of_state(lax.rem(own ^ distance, QUARTERS))
        for half in range(HALVES):
            rows = pl.ds(pl.multiple_of((mine ^ half) * part, part), part)
            sends[half * QUARTERS + distance][0:part] = scratch[rows]


def states_kernel(starts, logits, bias, decay, spread_ref, features, writes, *refs):
    sends = refs[:GROUP]
    weight_cols, factor_cols, cum_cols, cum_rows, stride_out, log_out, scratch = refs[GROUP:]
    heads, length = logits.shape
    state = writes.shape[1]
    width = features.shape[1] // QUARTERS
    part = state // HALVES
    first = lax.axis_index("ctx") * length
    own = group_place()
    stride = softplus(logits[...] + column(bias[...]))
    log_decay = stride * column(-jnp.exp(decay[...]))
    upto = jnp.where(iota((length, length), 0) <= iota((length, length), 1), 1.0, 0.0).astype(BF16)
    parts = matmul(jnp.concatenate(split3(log_decay), axis=0), upto)
    cum = parts[:heads] + parts[heads : 2 * heads] + parts[2 * heads :]
    segment = document_at(starts, first + iota((1, length), 1))
    entry = document_at(starts, jnp.full((1, 1), first - 1, jnp.int32))
    leave = document_at(starts, jnp.full((1, 1), first + length - 1, jnp.int32))
    own_last = jnp.where(segment == leave, 1.0, 0.0)
    keep_in = jnp.where(segment == entry, 1.0, 0.0)
    weight_stack = stacked_columns(own_last * jnp.exp(cum[:, length - 1 :] - cum) * stride)
    factor_stack = stacked_columns(keep_in * jnp.exp(cum))
    write_t = writes[...].astype(F32).T.astype(BF16)

    def quarter_of_state(quarter):
        cols = pl.ds(pl.multiple_of(quarter * width, LANES), width)
        high, low = split2(features[:, cols].astype(F32) * matmul(weight_stack, spread_ref[:, cols]))
        return matmul(write_t, high) + matmul(write_t, low)

    share_out(own, quarter_of_state, sends, scratch, part)
    for distance in range(QUARTERS):
        cols = pl.ds(pl.multiple_of(lax.rem(own ^ distance, QUARTERS) * width, LANES), width)
        keep = matmul(factor_stack[length - 16 :], spread_ref[:, cols])[15:16]
        for half in range(HALVES):
            sends[half * QUARTERS + distance][part:] = jnp.broadcast_to(keep, (8, width))
    weight_cols[...] = weight_stack
    factor_cols[...] = factor_stack
    cum_cols[...] = stacked_columns(cum * LOG2E)
    cum_rows[...] = cum * LOG2E - jnp.log2(stride)
    stride_out[...] = stride
    log_out[...] = log_decay


def back_states_kernel(factor_cols, spread_ref, cotangent, reads, *refs):
    scratch = refs[-1]
    state = reads.shape[1]
    width = cotangent.shape[1] // QUARTERS
    read_t = reads[...].astype(F32).T.astype(BF16)

    def quarter_of_state(quarter):
        cols = pl.ds(pl.multiple_of(quarter * width, LANES), width)
        high, low = split2(cotangent[:, cols].astype(F32) * matmul(factor_cols[...], spread_ref[:, cols]))
        return matmul(read_t, high) + matmul(read_t, low)

    share_out(group_place(), quarter_of_state, refs[:GROUP], scratch, state // HALVES)


def inner_kernel(offset, last, starts, cum_cols, cum_rows, features, cotangent, writes, reads, *refs):
    if last:
        refs = refs[:1] + refs[5:]
    else:
        refs = refs[1:]
    if last:
        before, inside, feature_part, skip_part, write_part, read_part = refs[:6]
    else:
        inside, feature_part, skip_part, grad_out = refs[:4]
    scores_ref, mask_ref, grad_ref = refs[-3:]
    length, width = features.shape
    heads = cum_rows.shape[0]
    here = heads // QUARTERS
    head_dim = width // here
    pair = 2 * head_dim
    step = pl.program_id(0)

    @pl.when(step == 0)
    def _():
        first = lax.axis_index("ctx") * length
        segment_row = document_at(starts, first + iota((1, length), 1))
        segment_col = document_at(starts, first + iota((length, 1), 0))
        causal = iota((length, length), 0) >= iota((length, length), 1)
        mask_ref[...] = jnp.where((segment_row == segment_col) & causal, 0.0, FAR)
        scores_ref[...] = matmul_nt(reads[...], writes[...])
        grad_ref[...] = before[...] if last else jnp.zeros_like(grad_ref)

    def one_pair(at, carry):
        cols = pl.ds(pl.multiple_of(at * pair, LANES), pair)
        feature = features[:, cols]
        grad = cotangent[:, cols]
        grad_f32 = grad.astype(F32)
        grad_t = grad_f32.T.astype(BF16)
        skip_part[:, cols] = jnp.sum(grad_f32 * feature.astype(F32), axis=0, keepdims=True)
        head = (offset + step) * here + at * 2
        lane = iota((LANES, 2 * LANES), 0)
        wanted = head + lax.div(iota((LANES, 2 * LANES), 1), LANES)
        pick = (lane == wanted) | (lane == wanted + heads) | (lane == wanted + 2 * heads)
        upper = matmul(cum_cols[...], jnp.where(pick, 1.0, 0.0).astype(BF16))
        second = iota((LANES, pair), 1) >= head_dim
        back = [None, None]
        for block in range(length // LANES):
            rows = slice(block * LANES, (block + 1) * LANES)
            reach = (block + 1) * LANES
            values = []
            for side in range(2):
                high_row = jnp.concatenate([upper[rows, side * LANES : (side + 1) * LANES]] * (block + 1), axis=1)
                low_row = cum_rows[pl.ds(head + side, 1), :][:, 0:reach]
                weight = jnp.exp2(high_row - low_row + mask_ref[rows, 0:reach])
                high, low = split2(weight * scores_ref[rows, 0:reach])
                values.append(matmul(high, feature[0:reach]) + matmul(low, feature[0:reach]))
                grad_rows = grad_t[side * head_dim : (side + 1) * head_dim, rows]
                found = matmul(grad_rows, high) + matmul(grad_rows, low)
                if block:
                    found = jnp.concatenate([found[:, : reach - LANES] + back[side], found[:, reach - LANES :]], axis=1)
                back[side] = found
                only = jnp.where(second == (side == 1), grad_f32[rows], 0.0).astype(BF16)
                grad_ref[rows, 0:reach] += matmul_nt(only, feature[0:reach]) * weight
            inside[rows, cols] = jnp.where(second, values[1], values[0])
        feature_part[:, cols] = jnp.concatenate(back, axis=0).T
        return carry

    lax.fori_loop(0, here // 2, one_pair, 0)

    @pl.when(step == pl.num_programs(0) - 1)
    def _():
        score_grad = grad_ref[...]
        if last:
            high, low = split2(score_grad)
            read_part[...] = matmul(high, writes[...]) + matmul(low, writes[...])
            high, low = split2(score_grad.T)
            write_part[...] = matmul(high, reads[...]) + matmul(low, reads[...])
        else:
            grad_out[...] = score_grad


def in_order(refs, scratch):
    own = group_place()
    for distance, ref in enumerate(refs):
        scratch[own ^ distance] = ref[...]


def group_kernel(part, *refs):
    up, keeps, came = refs[-3:]
    in_order(refs[:GROUP], came)
    total = came[0, 0:part]
    keep = came[0, part:]
    for j in range(1, GROUP):
        total = total * came[j, part : part + 1] + came[j, 0:part]
        keep = keep * came[j, part:]
    up[0:part] = total
    up[part:] = keep
    for j in range(GROUP):
        keeps[j : j + 1] = came[j, part : part + 1]


def back_group_kernel(part, *refs):
    keeps, up = refs[GROUP : GROUP + 2]
    down, came = refs[-2:]
    in_order(refs[:GROUP], came)
    total = came[GROUP - 1]
    for j in reversed(range(GROUP - 1)):
        total = total * keeps[j : j + 1] + came[j]
    down[0:part] = total
    down[part:] = up[part:]


def arrived(part, came):
    total, keep = came[0][0:part], came[0][part : part + 1]
    for ref in came[1:]:
        total = total + keep * ref[0:part]
        keep = keep * ref[part : part + 1]
    return total, keep


def link_kernel(part, own, *refs):
    total, keep = arrived(part, refs[:-1])
    refs[-1][0:part] = own[0:part] + own[part : part + 1] * total
    refs[-1][part:] = own[part:] * keep


def give_out(outs, scratch):
    own = group_place()
    for distance, out in enumerate(outs):
        out[...] = scratch[own ^ distance]


def spread_kernel(part, count, *refs):
    came, out = refs[-2:]
    in_order(refs[:GROUP], came)
    total = arrived(part, refs[GROUP : GROUP + count])[0]
    for j in range(GROUP):
        out[j] = total
        if j < GROUP - 1:
            total = total * came[j, part : part + 1] + came[j, 0:part]
    give_out(refs[-2 - GROUP : -2], out)


def back_spread_kernel(part, count, *refs):
    keeps = refs[GROUP]
    came, out = refs[-2:]
    in_order(refs[:GROUP], came)
    total = arrived(part, refs[GROUP + 1 : GROUP + 1 + count])[0]
    for j in reversed(range(GROUP)):
        out[j] = total
        if j > 0:
            total = total * keeps[j : j + 1] + came[j]
    give_out(refs[-2 - GROUP : -2], out)


def head_sums(ref, value, spread):
    high, low = split2(value)
    ref[...] += matmul_nt(high, spread) + matmul_nt(low, spread)


def wide_skip(skip, heads, spread):
    stack = stacked_columns(jnp.broadcast_to(column(skip[...]), (heads, LANES)))
    return matmul(stack[0:16], spread)[0:1]


def quarter_rows(scratch):
    step = pl.program_id(0)
    return jnp.concatenate([scratch[half * QUARTERS + step] for half in range(HALVES)], axis=0)


def finish_kernel(skip, factor_cols, spread_ref, features, cotangent, reads, inside, read_part, *refs):
    haves = refs[:GROUP]
    mixed, read_grad, rows, kept, read_acc, have = refs[GROUP + 1 :]
    length, state = reads.shape
    heads = skip.shape[1]
    step = pl.program_id(0)

    @pl.when(step == 0)
    def _():
        rows[...] = jnp.zeros_like(rows)
        read_acc[...] = jnp.zeros_like(read_acc)
        in_order(haves, have)

    spread = spread_ref[...]
    factor = matmul(factor_cols[...], spread)
    grad = cotangent[...].astype(F32)
    entering = quarter_rows(have)
    kept[...] = entering * factor[length - 1 :]
    stack = jnp.concatenate(split2(entering), axis=0)
    reads2 = jnp.concatenate([reads[...]] * 2, axis=1)
    total = inside[...] + factor * matmul(reads2, stack)
    mixed[...] = (total + wide_skip(skip, heads, spread) * features[...].astype(F32)).astype(BF16)
    head_sums(rows, grad * total, spread)
    high, low = split2(factor * grad)
    read_acc[...] += matmul_nt(high, stack) + matmul_nt(low, stack)

    @pl.when(step == QUARTERS - 1)
    def _():
        read_grad[...] = (read_part[...] + read_acc[:, :state] + read_acc[:, state:]).astype(BF16)


def back_finish_kernel(
    logits, bias, decay, skip, weight_cols, stride_ref, log_ref, spread_ref,
    features, cotangent, writes, feature_part, skip_part, row_ref, kept, *refs,
):
    haves = refs[:GROUP]
    feature_grad, step_grad, sums, col_acc, last_acc, skip_acc, have = refs[GROUP:]
    heads, length = logits.shape
    state = writes.shape[1]
    width = features.shape[1]
    step = pl.program_id(0)

    @pl.when(step == 0)
    def _():
        for ref in (col_acc, last_acc, skip_acc):
            ref[...] = jnp.zeros_like(ref)
        in_order(haves, have)

    spread = spread_ref[...]
    weight = matmul(weight_cols[...], spread)
    feature = features[...].astype(F32)
    returning = quarter_rows(have)
    stack = jnp.concatenate(split2(returning), axis=0)
    writes2 = jnp.concatenate([writes[...]] * 2, axis=1)
    carried = weight * matmul(writes2, stack)
    total = feature_part[...] + carried
    feature_grad[...] = (total + wide_skip(skip, heads, spread) * cotangent[...].astype(F32)).astype(BF16)
    head_sums(col_acc, feature * total, spread)
    leaving = jnp.sum((returning * kept[...]).reshape(state // 8, 8, width), axis=0)
    leaving = leaving + jnp.sum((feature * carried).reshape(length // 8, 8, width), axis=0)
    head_sums(last_acc, leaving, spread)
    head_sums(skip_acc, jnp.broadcast_to(skip_part[...], (8, width)), spread)

    @pl.when(step == QUARTERS - 1)
    def _():
        rows = row_ref[...].T[:heads]
        cols = col_acc[...].T[:heads]
        last = column(jnp.sum(last_acc[...], axis=0, keepdims=True))[:heads]
        stride = stride_ref[...]
        gap_grad = rows - cols + jnp.where(iota((heads, length), 1) == length - 1, last, 0.0)
        onward = jnp.where(iota((length, length), 0) >= iota((length, length), 1), 1.0, 0.0).astype(BF16)
        parts = matmul(jnp.concatenate(split3(gap_grad), axis=0), onward)
        log_grad = parts[:heads] + parts[heads : 2 * heads] + parts[2 * heads :]
        rate = column(-jnp.exp(decay[...]))
        slope = 1.0 / (1.0 + jnp.exp(-(logits[...] + column(bias[...]))))
        step_value = (cols / stride + rate * log_grad) * slope
        step_grad[...] = step_value
        bias_sum = jnp.sum(step_value, axis=1, keepdims=True)
        decay_sum = jnp.sum(log_grad * log_ref[...], axis=1, keepdims=True)
        skip_sum = column(skip_acc[0:1])[:heads]
        spare = jnp.zeros((LANES - 3 * heads, 1), F32)
        table = jnp.concatenate([bias_sum, decay_sum, skip_sum, spare], axis=0)
        eye = iota((LANES, LANES), 0) == iota((LANES, LANES), 1)
        table = jnp.sum(jnp.where(eye, table, 0.0), axis=0, keepdims=True)
        sums[...] = jnp.broadcast_to(table[None], sums.shape)


def write_kernel(weight_cols, spread_ref, features, write_part, *refs):
    write_grad, write_acc, have = refs[GROUP + 1 :]
    state = write_part.shape[1]
    step = pl.program_id(0)

    @pl.when(step == 0)
    def _():
        write_acc[...] = jnp.zeros_like(write_acc)
        in_order(refs[:GROUP], have)

    weight = matmul(weight_cols[...], spread_ref[...])
    stack = jnp.concatenate(split2(quarter_rows(have)), axis=0)
    high, low = split2(weight * features[...].astype(F32))
    write_acc[...] += matmul_nt(high, stack) + matmul_nt(low, stack)

    @pl.when(step == QUARTERS - 1)
    def _():
        write_grad[...] = (write_part[...] + write_acc[:, :state] + write_acc[:, state:]).astype(BF16)


def call(kernel, name, outs, in_specs, work, mib, **more):
    return pl.pallas_call(
        kernel,
        out_shape=outs,
        in_specs=in_specs,
        out_specs=more.pop("out_specs", [VMEM] * len(outs)),
        compiler_params=pltpu.CompilerParams(vmem_limit_bytes=mib * 2**20),
        cost_estimate=pl.CostEstimate(flops=work * 10**9, bytes_accessed=10**6, transcendentals=0),
        name=name,
        **more,
    )


def struct(shape, dtype=F32):
    return jax.ShapeDtypeStruct(shape, dtype)


def local(
    features, write_keys, read_queries, step_logits, step_bias, decay_log, skip_gain, doc_starts, out_grad
):
    features, writes, reads, logits, cotangent = (
        features[0], write_keys[0], read_queries[0], step_logits[0], out_grad[0]
    )
    length, wide = features.shape
    heads = logits.shape[0]
    state = writes.shape[1]
    head_dim = wide // heads
    width = wide // QUARTERS
    part = state // HALVES
    bias, decay, skip = step_bias[None], decay_log[None], skip_gain[None]
    blocks, members = lax.axis_size("ctx"), lax.axis_size("dp")
    spread = spread_table(heads, head_dim)

    def swap(values):
        pairs = [[(k, k ^ d) for k in range(blocks)] for d in range(GROUP)]
        return [values[0]] + [lax.ppermute(values[d], "ctx", pairs[d]) for d in range(1, GROUP)]

    def shift(value, distance):
        pairs = [(k, k + distance) for k in range(blocks) if 0 <= k + distance < blocks]
        return lax.ppermute(value, "ctx", pairs)

    def scan(own, sign):
        came, near, reach = [], own, 1
        while reach < blocks // GROUP:
            came.append(shift(near, sign * GROUP * reach))
            reach *= 2
            if reach < blocks // GROUP:
                near = call(
                    functools.partial(link_kernel, part), "link", [group_sum], [VMEM] * (1 + len(came)), 1, 8
                )(own, *came)[0]
        return came

    def all_of(*shape):
        return pl.BlockSpec(shape, lambda step: (0,) * len(shape))

    def quarter_of(rows, offset=0):
        return pl.BlockSpec((rows, width), lambda step: (0, step + offset))

    stack = struct((length, LANES), BF16)
    small = struct((heads, length))
    result = struct((length, wide), BF16)
    tokens_result = struct((length, state), BF16)
    group_sum = struct((part + 8, width))
    share = struct((part, width))
    tokens = all_of(length, state)
    columns = all_of(length, LANES)
    by_heads = all_of(heads, length)
    row = all_of(1, heads)
    whole_share = all_of(part, width)
    by_quarter = quarter_of(length)
    spread_quarter = quarter_of(LANES)
    shares = pltpu.VMEM((GROUP, part, width), F32)
    long_shares = pltpu.VMEM((GROUP, part + 8, width), F32)

    out = call(
        states_kernel,
        "states",
        [group_sum] * GROUP + [stack] * 3 + [small] * 3,
        [SMEM] + [VMEM] * 6,
        3,
        24,
        scratch_shapes=[pltpu.VMEM((state, width), F32)],
    )(doc_starts, logits, bias, decay, spread, features, writes)
    send, (weight_cols, factor_cols, cum_cols, cum_rows, stride, log_decay) = out[:GROUP], out[GROUP:]
    came = swap(send)
    back_send = call(
        back_states_kernel,
        "back_states",
        [share] * GROUP,
        [VMEM] * 4,
        3,
        24,
        scratch_shapes=[pltpu.VMEM((state, width), F32)],
    )(factor_cols, spread, cotangent, reads)
    back_came = swap(back_send)

    half = QUARTERS // 2
    started = struct((length, wide)), struct((length, wide)), struct((1, wide))
    square = all_of(length, length)
    inner_args = (doc_starts, cum_cols, cum_rows, features, cotangent, writes, reads)
    score_scratch = [pltpu.VMEM((length, length), F32)] * 3

    def inner_specs(offset):
        mine = quarter_of(length, offset)
        return [SMEM, columns, by_heads, mine, mine, tokens, tokens], [mine, mine, quarter_of(1, offset)]

    specs, out_specs = inner_specs(0)
    *begun, score_grad = call(
        functools.partial(inner_kernel, 0, False),
        "inner_first",
        [*started, struct((length, length))],
        specs + [ANY],
        10,
        24,
        grid=(half,),
        out_specs=out_specs + [square],
        scratch_shapes=score_scratch,
    )(*inner_args, back_send[0])
    up, keeps = call(
        functools.partial(group_kernel, part),
        "group",
        [group_sum, struct((GROUP, width))],
        [VMEM] * GROUP + [ANY],
        2,
        8,
        scratch_shapes=[long_shares],
    )(*came, score_grad)
    ups = scan(up, 1)
    specs, out_specs = inner_specs(half)
    inside, feature_part, skip_part, write_part, read_part = call(
        functools.partial(inner_kernel, half, True),
        "inner_second",
        [*started, struct((length, state)), struct((length, state))],
        specs + [square] + [ANY] * 4,
        10,
        24,
        grid=(half,),
        out_specs=out_specs + [tokens, tokens],
        scratch_shapes=score_scratch,
        input_output_aliases={8: 0, 9: 1, 10: 2},
    )(*inner_args, score_grad, *begun, up)
    (down,) = call(
        functools.partial(back_group_kernel, part),
        "back_group",
        [group_sum],
        [VMEM] * (GROUP + 2) + [ANY],
        2,
        8,
        scratch_shapes=[shares],
    )(*back_came, keeps, up, write_part)
    downs = scan(down, -1)
    give = call(
        functools.partial(spread_kernel, part, len(ups)),
        "spread",
        [share] * GROUP,
        [VMEM] * (GROUP + len(ups)) + [ANY],
        2,
        12,
        scratch_shapes=[long_shares, shares],
    )(*came, *ups, down)
    have = swap(give)
    back_give = call(
        functools.partial(back_spread_kernel, part, len(downs)),
        "back_spread",
        [share] * GROUP,
        [VMEM] * (GROUP + 1 + len(downs)) + [ANY],
        2,
        12,
        scratch_shapes=[shares, shares],
    )(*back_came, keeps, *downs, give[0])
    back_have = swap(back_give)

    mixed, read_grad, rows, kept = call(
        finish_kernel,
        "finish",
        [result, tokens_result, struct((length, LANES)), struct((state, wide))],
        [row, columns, spread_quarter, by_quarter, by_quarter, tokens, by_quarter, tokens]
        + [whole_share] * GROUP
        + [ANY],
        8,
        24,
        grid=(QUARTERS,),
        out_specs=[by_quarter, tokens, columns, quarter_of(state)],
        scratch_shapes=[pltpu.VMEM((length, 2 * state), F32), shares],
    )(skip, factor_cols, spread, features, cotangent, reads, inside, read_part, *have, back_give[0])
    devices = blocks * members
    feature_grad, step_grad, sums = call(
        back_finish_kernel,
        "back_finish",
        [result, small, struct((devices, 1, LANES))],
        [by_heads, row, row, row, columns, by_heads, by_heads, spread_quarter]
        + [by_quarter, by_quarter, tokens, by_quarter]
        + [quarter_of(1), columns, quarter_of(state)]
        + [whole_share] * GROUP,
        8,
        24,
        grid=(QUARTERS,),
        out_specs=[by_quarter, by_heads, all_of(devices, 1, LANES)],
        scratch_shapes=[
            pltpu.VMEM((length, LANES), F32),
            pltpu.VMEM((8, LANES), F32),
            pltpu.VMEM((8, LANES), F32),
            shares,
        ],
    )(
        logits, bias, decay, skip, weight_cols, stride, log_decay, spread, features, cotangent, writes,
        feature_part, skip_part, rows, kept, *back_have,
    )
    (write_grad,) = call(
        write_kernel,
        "write_grad",
        [tokens_result],
        [columns, spread_quarter, by_quarter, tokens] + [whole_share] * GROUP + [ANY],
        4,
        24,
        grid=(QUARTERS,),
        out_specs=[tokens],
        scratch_shapes=[pltpu.VMEM((length, 2 * state), F32), shares],
    )(weight_cols, spread, features, write_part, *back_have, step_grad)
    sums = jnp.sum(lax.all_to_all(sums, ("dp", "ctx"), 0, 0), axis=(0, 1))
    return (
        mixed[None],
        feature_grad[None],
        write_grad[None],
        read_grad[None],
        step_grad[None],
        sums[:heads],
        sums[heads : 2 * heads],
        sums[2 * heads : 3 * heads],
    )


def solution(mesh):
    by_tokens = P("dp", "ctx", None)
    by_heads = P("dp", None, "ctx")
    in_specs = (by_tokens, by_tokens, by_tokens, by_heads, P(), P(), P(), P("dp", None), by_tokens)
    out_specs = (by_tokens, by_tokens, by_tokens, by_tokens, by_heads, P(), P(), P())
    return jax.shard_map(local, mesh=mesh, in_specs=in_specs, out_specs=out_specs, check_vma=False)
```

```python
import functools

import jax
import jax.numpy as jnp
import numpy as np
from jax import lax
from jax.experimental import pallas as pl
from jax.experimental.pallas import tpu as pltpu
from jax.sharding import PartitionSpec as P

F32 = jnp.float32
BF16 = jnp.bfloat16
QUARTERS = 4
HALVES = 2
GROUP = QUARTERS * HALVES
LANES = 128
LOG2E = 1.4426950408889634
FAR = -1e30
VMEM = pl.BlockSpec(memory_space=pltpu.VMEM)
SMEM = pl.BlockSpec(memory_space=pltpu.SMEM)
ANY = pl.BlockSpec(memory_space=pl.ANY)


def iota(shape, axis):
    return lax.broadcasted_iota(jnp.int32, shape, axis)


def matmul(left, right):
    return lax.dot_general(left, right, (((1,), (0,)), ((), ())), preferred_element_type=F32)


def matmul_nt(left, right):
    return lax.dot_general(left, right, (((1,), (1,)), ((), ())), preferred_element_type=F32)


def split2(value):
    high = value.astype(BF16)
    return high, (value - high.astype(F32)).astype(BF16)


def split3(value):
    high = value.astype(BF16)
    rest = value - high.astype(F32)
    middle = rest.astype(BF16)
    return high, middle, (rest - middle.astype(F32)).astype(BF16)


def column(row):
    count = row.shape[1]
    eye = iota((count, count), 0) == iota((count, count), 1)
    return jnp.sum(jnp.where(eye, row, 0.0), axis=1, keepdims=True)


def stacked_columns(rows):
    parts = [part.astype(F32) for part in split3(rows)]
    spare = LANES - 3 * rows.shape[0]
    if spare:
        parts.append(jnp.zeros((spare, rows.shape[1]), F32))
    return jnp.concatenate(parts, axis=0).T.astype(BF16)


def spread_table(heads, head_dim):
    table = np.zeros((LANES, heads * head_dim), np.float32)
    for head in range(heads):
        for part in range(3):
            table[part * heads + head, head * head_dim : (head + 1) * head_dim] = 1.0
    return jnp.asarray(table, BF16)


def softplus(value):
    return jnp.maximum(value, 0.0) + jnp.log1p(jnp.exp(-jnp.abs(value)))


def document_at(starts_ref, position):
    total = jnp.zeros_like(position)
    for entry in range(starts_ref.shape[1]):
        total = total + (starts_ref[0, entry] <= position).astype(jnp.int32)
    return total


def group_place():
    return lax.rem(lax.axis_index("ctx"), GROUP)


def share_out(own, quarter_of_state, sends, scratch, part):
    mine = lax.div(own, QUARTERS)
    for distance in range(QUARTERS):
        scratch[...] = quarter_of_state(lax.rem(own ^ distance, QUARTERS))
        for half in range(HALVES):
            rows = pl.ds(pl.multiple_of((mine ^ half) * part, part), part)
            sends[half * QUARTERS + distance][0:part] = scratch[rows]


def states_kernel(starts, logits, bias, decay, spread_ref, features, writes, *refs):
    sends = refs[:GROUP]
    weight_cols, factor_cols, cum_cols, cum_rows, stride_out, log_out, scratch = refs[GROUP:]
    heads, length = logits.shape
    state = writes.shape[1]
    width = features.shape[1] // QUARTERS
    part = state // HALVES
    first = lax.axis_index("ctx") * length
    own = group_place()
    stride = softplus(logits[...] + column(bias[...]))
    log_decay = stride * column(-jnp.exp(decay[...]))
    upto = jnp.where(iota((length, length), 0) <= iota((length, length), 1), 1.0, 0.0).astype(BF16)
    parts = matmul(jnp.concatenate(split3(log_decay), axis=0), upto)
    cum = parts[:heads] + parts[heads : 2 * heads] + parts[2 * heads :]
    segment = document_at(starts, first + iota((1, length), 1))
    entry = document_at(starts, jnp.full((1, 1), first - 1, jnp.int32))
    leave = document_at(starts, jnp.full((1, 1), first + length - 1, jnp.int32))
    own_last = jnp.where(segment == leave, 1.0, 0.0)
    keep_in = jnp.where(segment == entry, 1.0, 0.0)
    weight_stack = stacked_columns(own_last * jnp.exp(cum[:, length - 1 :] - cum) * stride)
    factor_stack = stacked_columns(keep_in * jnp.exp(cum))
    write_t = writes[...].astype(F32).T.astype(BF16)

    def quarter_of_state(quarter):
        cols = pl.ds(pl.multiple_of(quarter * width, LANES), width)
        high, low = split2(features[:, cols].astype(F32) * matmul(weight_stack, spread_ref[:, cols]))
        return matmul(write_t, high) + matmul(write_t, low)

    share_out(own, quarter_of_state, sends, scratch, part)
    for distance in range(QUARTERS):
        cols = pl.ds(pl.multiple_of(lax.rem(own ^ distance, QUARTERS) * width, LANES), width)
        keep = matmul(factor_stack[length - 16 :], spread_ref[:, cols])[15:16]
        for half in range(HALVES):
            sends[half * QUARTERS + distance][part:] = jnp.broadcast_to(keep, (8, width))
    weight_cols[...] = weight_stack
    factor_cols[...] = factor_stack
    cum_cols[...] = stacked_columns(cum * LOG2E)
    cum_rows[...] = cum * LOG2E - jnp.log2(stride)
    stride_out[...] = stride
    log_out[...] = log_decay


def back_states_kernel(factor_cols, spread_ref, cotangent, reads, send):
    state = reads.shape[1]
    width = cotangent.shape[1] // QUARTERS
    part = state // HALVES
    read_t = reads[...].astype(F32).T.astype(BF16)
    for quarter in range(QUARTERS):
        cols = slice(quarter * width, (quarter + 1) * width)
        high, low = split2(cotangent[:, cols].astype(F32) * matmul(factor_cols[...], spread_ref[:, cols]))
        total = matmul(read_t, high) + matmul(read_t, low)
        for half in range(HALVES):
            send[half * QUARTERS + quarter] = total[half * part : (half + 1) * part]


def inner_kernel(offset, last, starts, cum_cols, cum_rows, features, cotangent, writes, reads, *refs):
    if last:
        refs = refs[:1] + refs[5:]
    else:
        refs = refs[1:]
    if last:
        before, inside, feature_part, skip_part, write_part, read_part = refs[:6]
    else:
        inside, feature_part, skip_part, grad_out = refs[:4]
    scores_ref, mask_ref, grad_ref = refs[-3:]
    length, width = features.shape
    heads = cum_rows.shape[0]
    here = heads // QUARTERS
    head_dim = width // here
    pair = 2 * head_dim
    step = pl.program_id(0)

    @pl.when(step == 0)
    def _():
        first = lax.axis_index("ctx") * length
        segment_row = document_at(starts, first + iota((1, length), 1))
        segment_col = document_at(starts, first + iota((length, 1), 0))
        causal = iota((length, length), 0) >= iota((length, length), 1)
        mask_ref[...] = jnp.where((segment_row == segment_col) & causal, 0.0, FAR)
        scores_ref[...] = matmul_nt(reads[...], writes[...])
        grad_ref[...] = before[...] if last else jnp.zeros_like(grad_ref)

    def one_pair(at, carry):
        cols = pl.ds(pl.multiple_of(at * pair, LANES), pair)
        feature = features[:, cols]
        grad = cotangent[:, cols]
        grad_f32 = grad.astype(F32)
        grad_t = grad_f32.T.astype(BF16)
        skip_part[:, cols] = jnp.sum(grad_f32 * feature.astype(F32), axis=0, keepdims=True)
        head = (offset + step) * here + at * 2
        lane = iota((LANES, 2 * LANES), 0)
        wanted = head + lax.div(iota((LANES, 2 * LANES), 1), LANES)
        pick = (lane == wanted) | (lane == wanted + heads) | (lane == wanted + 2 * heads)
        upper = matmul(cum_cols[...], jnp.where(pick, 1.0, 0.0).astype(BF16))
        second = iota((LANES, pair), 1) >= head_dim
        back = [None, None]
        for block in range(length // LANES):
            rows = slice(block * LANES, (block + 1) * LANES)
            reach = (block + 1) * LANES
            values = []
            for side in range(2):
                high_row = jnp.concatenate([upper[rows, side * LANES : (side + 1) * LANES]] * (block + 1), axis=1)
                low_row = cum_rows[pl.ds(head + side, 1), :][:, 0:reach]
                weight = jnp.exp2(high_row - low_row + mask_ref[rows, 0:reach])
                high, low = split2(weight * scores_ref[rows, 0:reach])
                values.append(matmul(high, feature[0:reach]) + matmul(low, feature[0:reach]))
                grad_rows = grad_t[side * head_dim : (side + 1) * head_dim, rows]
                found = matmul(grad_rows, high) + matmul(grad_rows, low)
                if block:
                    found = jnp.concatenate([found[:, : reach - LANES] + back[side], found[:, reach - LANES :]], axis=1)
                back[side] = found
                only = jnp.where(second == (side == 1), grad_f32[rows], 0.0).astype(BF16)
                grad_ref[rows, 0:reach] += matmul_nt(only, feature[0:reach]) * weight
            inside[rows, cols] = jnp.where(second, values[1], values[0])
        feature_part[:, cols] = jnp.concatenate(back, axis=0).T
        return carry

    lax.fori_loop(0, here // 2, one_pair, 0)

    @pl.when(step == pl.num_programs(0) - 1)
    def _():
        score_grad = grad_ref[...]
        if last:
            high, low = split2(score_grad)
            read_part[...] = matmul(high, writes[...]) + matmul(low, writes[...])
            high, low = split2(score_grad.T)
            write_part[...] = matmul(high, reads[...]) + matmul(low, reads[...])
        else:
            grad_out[...] = score_grad


def in_order(refs, scratch):
    own = group_place()
    for distance, ref in enumerate(refs):
        scratch[own ^ distance] = ref[...]


def group_kernel(part, *refs):
    up, keeps, came = refs[-3:]
    in_order(refs[:GROUP], came)
    total = came[0, 0:part]
    keep = came[0, part:]
    for j in range(1, GROUP):
        total = total * came[j, part : part + 1] + came[j, 0:part]
        keep = keep * came[j, part:]
    up[0:part] = total
    up[part:] = keep
    for j in range(GROUP):
        keeps[j : j + 1] = came[j, part : part + 1]


def back_group_kernel(part, came, keeps, up, _, down):
    total = came[GROUP - 1]
    for j in reversed(range(GROUP - 1)):
        total = total * keeps[j : j + 1] + came[j]
    down[0:part] = total
    down[part:] = up[part:]


def arrived(part, came):
    total, keep = came[0][0:part], came[0][part : part + 1]
    for ref in came[1:]:
        total = total + keep * ref[0:part]
        keep = keep * ref[part : part + 1]
    return total, keep


def link_kernel(part, own, *refs):
    total, keep = arrived(part, refs[:-1])
    refs[-1][0:part] = own[0:part] + own[part : part + 1] * total
    refs[-1][part:] = own[part:] * keep


def give_out(outs, scratch):
    own = group_place()
    for distance, out in enumerate(outs):
        out[...] = scratch[own ^ distance]


def spread_kernel(part, count, *refs):
    came, out = refs[-2:]
    in_order(refs[:GROUP], came)
    total = arrived(part, refs[GROUP : GROUP + count])[0]
    for j in range(GROUP):
        out[j] = total
        if j < GROUP - 1:
            total = total * came[j, part : part + 1] + came[j, 0:part]
    give_out(refs[-2 - GROUP : -2], out)


def back_spread_kernel(part, count, came, keeps, *refs):
    out = refs[-1]
    total = arrived(part, refs[:count])[0]
    for j in reversed(range(GROUP)):
        out[j] = total
        if j > 0:
            total = total * keeps[j : j + 1] + came[j]


def head_sums(ref, value, spread):
    high, low = split2(value)
    ref[...] += matmul_nt(high, spread) + matmul_nt(low, spread)


def wide_skip(skip, heads, spread):
    stack = stacked_columns(jnp.broadcast_to(column(skip[...]), (heads, LANES)))
    return matmul(stack[0:16], spread)[0:1]


def quarter_rows(scratch):
    step = pl.program_id(0)
    return jnp.concatenate([scratch[half * QUARTERS + step] for half in range(HALVES)], axis=0)


def finish_kernel(skip, factor_cols, spread_ref, features, cotangent, reads, inside, read_part, *refs):
    haves = refs[:GROUP]
    mixed, read_grad, rows, kept, read_acc, have = refs[GROUP + 1 :]
    length, state = reads.shape
    heads = skip.shape[1]
    step = pl.program_id(0)

    @pl.when(step == 0)
    def _():
        rows[...] = jnp.zeros_like(rows)
        read_acc[...] = jnp.zeros_like(read_acc)
        in_order(haves, have)

    spread = spread_ref[...]
    factor = matmul(factor_cols[...], spread)
    grad = cotangent[...].astype(F32)
    entering = quarter_rows(have)
    kept[...] = entering * factor[length - 1 :]
    stack = jnp.concatenate(split2(entering), axis=0)
    reads2 = jnp.concatenate([reads[...]] * 2, axis=1)
    total = inside[...] + factor * matmul(reads2, stack)
    mixed[...] = (total + wide_skip(skip, heads, spread) * features[...].astype(F32)).astype(BF16)
    head_sums(rows, grad * total, spread)
    high, low = split2(factor * grad)
    read_acc[...] += matmul_nt(high, stack) + matmul_nt(low, stack)

    @pl.when(step == QUARTERS - 1)
    def _():
        read_grad[...] = (read_part[...] + read_acc[:, :state] + read_acc[:, state:]).astype(BF16)


def back_finish_kernel(
    logits, bias, decay, weight_cols, stride_ref, log_ref, spread_ref,
    features, writes, feature_part, skip_part, row_ref, kept, have,
    step_grad, sums, col_acc, last_acc, skip_acc,
):
    heads, length = logits.shape
    state = writes.shape[1]
    width = features.shape[1]
    step = pl.program_id(0)

    @pl.when(step == 0)
    def _():
        for ref in (col_acc, last_acc, skip_acc):
            ref[...] = jnp.zeros_like(ref)

    spread = spread_ref[...]
    weight = matmul(weight_cols[...], spread)
    feature = features[...].astype(F32)
    returning = quarter_rows(have)
    stack = jnp.concatenate(split2(returning), axis=0)
    writes2 = jnp.concatenate([writes[...]] * 2, axis=1)
    carried = weight * matmul(writes2, stack)
    total = feature_part[...] + carried
    head_sums(col_acc, feature * total, spread)
    leaving = jnp.sum((returning * kept[...]).reshape(state // 8, 8, width), axis=0)
    leaving = leaving + jnp.sum((feature * carried).reshape(length // 8, 8, width), axis=0)
    head_sums(last_acc, leaving, spread)
    head_sums(skip_acc, jnp.broadcast_to(skip_part[...], (8, width)), spread)

    @pl.when(step == QUARTERS - 1)
    def _():
        rows = row_ref[...].T[:heads]
        cols = col_acc[...].T[:heads]
        last = column(jnp.sum(last_acc[...], axis=0, keepdims=True))[:heads]
        stride = stride_ref[...]
        gap_grad = rows - cols + jnp.where(iota((heads, length), 1) == length - 1, last, 0.0)
        onward = jnp.where(iota((length, length), 0) >= iota((length, length), 1), 1.0, 0.0).astype(BF16)
        parts = matmul(jnp.concatenate(split3(gap_grad), axis=0), onward)
        log_grad = parts[:heads] + parts[heads : 2 * heads] + parts[2 * heads :]
        rate = column(-jnp.exp(decay[...]))
        slope = 1.0 / (1.0 + jnp.exp(-(logits[...] + column(bias[...]))))
        step_value = (cols / stride + rate * log_grad) * slope
        step_grad[...] = step_value
        bias_sum = jnp.sum(step_value, axis=1, keepdims=True)
        decay_sum = jnp.sum(log_grad * log_ref[...], axis=1, keepdims=True)
        skip_sum = column(skip_acc[0:1])[:heads]
        spare = jnp.zeros((LANES - 3 * heads, 1), F32)
        table = jnp.concatenate([bias_sum, decay_sum, skip_sum, spare], axis=0)
        eye = iota((LANES, LANES), 0) == iota((LANES, LANES), 1)
        table = jnp.sum(jnp.where(eye, table, 0.0), axis=0, keepdims=True)
        sums[...] = jnp.broadcast_to(table[None], sums.shape)


def write_kernel(
    skip, weight_cols, spread_ref, features, cotangent, writes, feature_part, write_part, have, _,
    feature_grad, write_grad, write_acc,
):
    state = write_part.shape[1]
    step = pl.program_id(0)

    @pl.when(step == 0)
    def _():
        write_acc[...] = jnp.zeros_like(write_acc)

    spread = spread_ref[...]
    weight = matmul(weight_cols[...], spread)
    stack = jnp.concatenate(split2(quarter_rows(have)), axis=0)
    writes2 = jnp.concatenate([writes[...]] * 2, axis=1)
    total = feature_part[...] + weight * matmul(writes2, stack)
    skips = wide_skip(skip, skip.shape[1], spread) * cotangent[...].astype(F32)
    feature_grad[...] = (total + skips).astype(BF16)
    high, low = split2(weight * features[...].astype(F32))
    write_acc[...] += matmul_nt(high, stack) + matmul_nt(low, stack)

    @pl.when(step == QUARTERS - 1)
    def _():
        write_grad[...] = (write_part[...] + write_acc[:, :state] + write_acc[:, state:]).astype(BF16)


def call(kernel, name, outs, in_specs, work, mib, **more):
    return pl.pallas_call(
        kernel,
        out_shape=outs,
        in_specs=in_specs,
        out_specs=more.pop("out_specs", [VMEM] * len(outs)),
        compiler_params=pltpu.CompilerParams(vmem_limit_bytes=mib * 2**20),
        cost_estimate=pl.CostEstimate(flops=work * 10**9, bytes_accessed=10**6, transcendentals=0),
        name=name,
        **more,
    )


def struct(shape, dtype=F32):
    return jax.ShapeDtypeStruct(shape, dtype)


def local(
    features, write_keys, read_queries, step_logits, step_bias, decay_log, skip_gain, doc_starts, out_grad
):
    features, writes, reads, logits, cotangent = (
        features[0], write_keys[0], read_queries[0], step_logits[0], out_grad[0]
    )
    length, wide = features.shape
    heads = logits.shape[0]
    state = writes.shape[1]
    head_dim = wide // heads
    width = wide // QUARTERS
    part = state // HALVES
    bias, decay, skip = step_bias[None], decay_log[None], skip_gain[None]
    blocks, members = lax.axis_size("ctx"), lax.axis_size("dp")
    spread = spread_table(heads, head_dim)

    def swap(values):
        came = dict.fromkeys(range(GROUP), values[0])
        for d in (1, 2, 4, 7, 3, 5, 6):
            came[d] = lax.ppermute(values[d], "ctx", [(k, k ^ d) for k in range(blocks)])
        return [came[d] for d in range(GROUP)]

    def swap_stacked(value):
        groups = [list(range(k, k + GROUP)) for k in range(0, blocks, GROUP)]
        return lax.all_to_all(value, "ctx", 0, 0, axis_index_groups=groups)

    def shift(value, distance):
        pairs = [(k, k + distance) for k in range(blocks) if 0 <= k + distance < blocks]
        return lax.ppermute(value, "ctx", pairs)

    def scan(own, sign):
        came, near, reach = [], own, 1
        while reach < blocks // GROUP:
            came.append(shift(near, sign * GROUP * reach))
            reach *= 2
            if reach < blocks // GROUP:
                near = call(
                    functools.partial(link_kernel, part), "link", [group_sum], [VMEM] * (1 + len(came)), 1, 8
                )(own, *came)[0]
        return came

    def all_of(*shape):
        return pl.BlockSpec(shape, lambda step: (0,) * len(shape))

    def quarter_of(rows, offset=0):
        return pl.BlockSpec((rows, width), lambda step: (0, step + offset))

    stack = struct((length, LANES), BF16)
    small = struct((heads, length))
    result = struct((length, wide), BF16)
    tokens_result = struct((length, state), BF16)
    group_sum = struct((part + 8, width))
    share = struct((part, width))
    tokens = all_of(length, state)
    columns = all_of(length, LANES)
    by_heads = all_of(heads, length)
    row = all_of(1, heads)
    whole_share = all_of(part, width)
    by_quarter = quarter_of(length)
    spread_quarter = quarter_of(LANES)
    shares = pltpu.VMEM((GROUP, part, width), F32)
    shares_out = struct((GROUP, part, width))
    whole_shares = all_of(GROUP, part, width)
    long_shares = pltpu.VMEM((GROUP, part + 8, width), F32)

    out = call(
        states_kernel,
        "states",
        [group_sum] * GROUP + [stack] * 3 + [small] * 3,
        [SMEM] + [VMEM] * 6,
        3,
        60,
        scratch_shapes=[pltpu.VMEM((state, width), F32)],
    )(doc_starts, logits, bias, decay, spread, features, writes)
    send, (weight_cols, factor_cols, cum_cols, cum_rows, stride, log_decay) = out[:GROUP], out[GROUP:]
    came = swap(send)
    (back_send,) = call(back_states_kernel, "back_states", [shares_out], [VMEM] * 4, 3, 24)(
        factor_cols, spread, cotangent, reads
    )
    back_came = swap_stacked(back_send)

    half = QUARTERS // 2
    started = struct((length, wide)), struct((length, wide)), struct((1, wide))
    square = all_of(length, length)
    inner_args = (doc_starts, cum_cols, cum_rows, features, cotangent, writes, reads)
    score_scratch = [pltpu.VMEM((length, length), F32)] * 3

    def inner_specs(offset):
        mine = quarter_of(length, offset)
        return [SMEM, columns, by_heads, mine, mine, tokens, tokens], [mine, mine, quarter_of(1, offset)]

    specs, out_specs = inner_specs(0)
    *begun, score_grad = call(
        functools.partial(inner_kernel, 0, False),
        "inner_first",
        [*started, struct((length, length))],
        specs + [ANY],
        10,
        24,
        grid=(half,),
        out_specs=out_specs + [square],
        scratch_shapes=score_scratch,
    )(*inner_args, back_send)
    up, keeps = call(
        functools.partial(group_kernel, part),
        "group",
        [group_sum, struct((GROUP, width))],
        [VMEM] * GROUP + [ANY],
        2,
        8,
        scratch_shapes=[long_shares],
    )(*came, score_grad)
    ups = scan(up, 1)
    specs, out_specs = inner_specs(half)
    inside, feature_part, skip_part, write_part, read_part = call(
        functools.partial(inner_kernel, half, True),
        "inner_second",
        [*started, struct((length, state)), struct((length, state))],
        specs + [square] + [ANY] * 4,
        10,
        24,
        grid=(half,),
        out_specs=out_specs + [tokens, tokens],
        scratch_shapes=score_scratch,
        input_output_aliases={8: 0, 9: 1, 10: 2},
    )(*inner_args, score_grad, *begun, up)
    (down,) = call(
        functools.partial(back_group_kernel, part),
        "back_group",
        [group_sum],
        [VMEM] * 3 + [ANY],
        2,
        8,
    )(back_came, keeps, up, write_part)
    downs = scan(down, -1)
    give = call(
        functools.partial(spread_kernel, part, len(ups)),
        "spread",
        [share] * GROUP,
        [VMEM] * (GROUP + len(ups)) + [ANY],
        2,
        12,
        scratch_shapes=[long_shares, shares],
    )(*came, *ups, down)
    have = swap(give)
    (back_give,) = call(
        functools.partial(back_spread_kernel, part, len(downs)),
        "back_spread",
        [shares_out],
        [VMEM] * (2 + len(downs)) + [ANY],
        2,
        12,
    )(back_came, keeps, *downs, give[0])
    back_have = swap_stacked(back_give)

    mixed, read_grad, rows, kept = call(
        finish_kernel,
        "finish",
        [result, tokens_result, struct((length, LANES)), struct((state, wide))],
        [row, columns, spread_quarter, by_quarter, by_quarter, tokens, by_quarter, tokens]
        + [whole_share] * GROUP
        + [ANY],
        8,
        24,
        grid=(QUARTERS,),
        out_specs=[by_quarter, tokens, columns, quarter_of(state)],
        scratch_shapes=[pltpu.VMEM((length, 2 * state), F32), shares],
    )(skip, factor_cols, spread, features, cotangent, reads, inside, read_part, *have, back_give)
    devices = blocks * members
    step_grad, sums = call(
        back_finish_kernel,
        "back_finish",
        [small, struct((devices, 1, LANES))],
        [by_heads, row, row, columns, by_heads, by_heads, spread_quarter]
        + [by_quarter, tokens, by_quarter]
        + [quarter_of(1), columns, quarter_of(state), whole_shares],
        8,
        24,
        grid=(QUARTERS,),
        out_specs=[by_heads, all_of(devices, 1, LANES)],
        scratch_shapes=[pltpu.VMEM((length, LANES), F32), pltpu.VMEM((8, LANES), F32), pltpu.VMEM((8, LANES), F32)],
    )(
        logits, bias, decay, weight_cols, stride, log_decay, spread, features, writes,
        feature_part, skip_part, rows, kept, back_have,
    )
    feature_grad, write_grad = call(
        write_kernel,
        "write_grad",
        [result, tokens_result],
        [row, columns, spread_quarter, by_quarter, by_quarter, tokens, by_quarter, tokens, whole_shares, ANY],
        6,
        24,
        grid=(QUARTERS,),
        out_specs=[by_quarter, tokens],
        scratch_shapes=[pltpu.VMEM((length, 2 * state), F32)],
    )(skip, weight_cols, spread, features, cotangent, writes, feature_part, write_part, back_have, step_grad)
    sums = jnp.sum(lax.all_to_all(sums, ("dp", "ctx"), 0, 0), axis=(0, 1))
    return (
        mixed[None],
        feature_grad[None],
        write_grad[None],
        read_grad[None],
        step_grad[None],
        sums[:heads],
        sums[heads : 2 * heads],
        sums[2 * heads : 3 * heads],
    )


def solution(mesh):
    by_tokens = P("dp", "ctx", None)
    by_heads = P("dp", None, "ctx")
    in_specs = (by_tokens, by_tokens, by_tokens, by_heads, P(), P(), P(), P("dp", None), by_tokens)
    out_specs = (by_tokens, by_tokens, by_tokens, by_tokens, by_heads, P(), P(), P())
    return jax.shard_map(local, mesh=mesh, in_specs=in_specs, out_specs=out_specs, check_vma=False)
```

```python
import functools

import jax
import jax.numpy as jnp
import numpy as np
from jax import lax
from jax.experimental import pallas as pl
from jax.experimental.pallas import tpu as pltpu
from jax.sharding import PartitionSpec as P

F32 = jnp.float32
BF16 = jnp.bfloat16
QUARTERS = 4
HALVES = 2
GROUP = QUARTERS * HALVES
EARLY, LATE = (1, 2, 4, 7), (3, 5, 6)
LANES = 128
LOG2E = 1.4426950408889634
FAR = -1e30
VMEM = pl.BlockSpec(memory_space=pltpu.VMEM)
SMEM = pl.BlockSpec(memory_space=pltpu.SMEM)
ANY = pl.BlockSpec(memory_space=pl.ANY)


def iota(shape, axis):
    return lax.broadcasted_iota(jnp.int32, shape, axis)


def matmul(left, right):
    return lax.dot_general(left, right, (((1,), (0,)), ((), ())), preferred_element_type=F32)


def matmul_nt(left, right):
    return lax.dot_general(left, right, (((1,), (1,)), ((), ())), preferred_element_type=F32)


def split2(value):
    high = value.astype(BF16)
    return high, (value - high.astype(F32)).astype(BF16)


def split3(value):
    high = value.astype(BF16)
    rest = value - high.astype(F32)
    middle = rest.astype(BF16)
    return high, middle, (rest - middle.astype(F32)).astype(BF16)


def column(row):
    count = row.shape[1]
    eye = iota((count, count), 0) == iota((count, count), 1)
    return jnp.sum(jnp.where(eye, row, 0.0), axis=1, keepdims=True)


def stacked_columns(rows):
    parts = [part.astype(F32) for part in split3(rows)]
    spare = LANES - 3 * rows.shape[0]
    if spare:
        parts.append(jnp.zeros((spare, rows.shape[1]), F32))
    return jnp.concatenate(parts, axis=0).T.astype(BF16)


def spread_table(heads, head_dim):
    table = np.zeros((LANES, heads * head_dim), np.float32)
    for head in range(heads):
        for part in range(3):
            table[part * heads + head, head * head_dim : (head + 1) * head_dim] = 1.0
    return jnp.asarray(table, BF16)


def softplus(value):
    return jnp.maximum(value, 0.0) + jnp.log1p(jnp.exp(-jnp.abs(value)))


def document_at(starts_ref, position):
    total = jnp.zeros_like(position)
    for entry in range(starts_ref.shape[1]):
        total = total + (starts_ref[0, entry] <= position).astype(jnp.int32)
    return total


def group_place():
    return lax.rem(lax.axis_index("ctx"), GROUP)


def share_out(own, quarter_of_state, places, scratch):
    mine = lax.div(own, QUARTERS)
    part = scratch.shape[0] // HALVES
    for distance in range(QUARTERS):
        scratch[...] = quarter_of_state(lax.rem(own ^ distance, QUARTERS))
        for half in range(HALVES):
            rows = pl.ds(pl.multiple_of((mine ^ half) * part, part), part)
            places[half * QUARTERS + distance][...] = scratch[rows]


def states_kernel(starts, logits, bias, decay, spread_ref, features, writes, cotangent, reads, *refs):
    sends = refs[:GROUP]
    late = refs[GROUP : GROUP + len(LATE)]
    weight_cols, factor_cols, cum_cols, cum_rows, stride_out, log_out, scratch = refs[GROUP + len(LATE) :]
    heads, length = logits.shape
    state = writes.shape[1]
    width = features.shape[1] // QUARTERS
    part = state // HALVES
    first = lax.axis_index("ctx") * length
    own = group_place()
    stride = softplus(logits[...] + column(bias[...]))
    log_decay = stride * column(-jnp.exp(decay[...]))
    upto = jnp.where(iota((length, length), 0) <= iota((length, length), 1), 1.0, 0.0).astype(BF16)
    parts = matmul(jnp.concatenate(split3(log_decay), axis=0), upto)
    cum = parts[:heads] + parts[heads : 2 * heads] + parts[2 * heads :]
    segment = document_at(starts, first + iota((1, length), 1))
    entry = document_at(starts, jnp.full((1, 1), first - 1, jnp.int32))
    leave = document_at(starts, jnp.full((1, 1), first + length - 1, jnp.int32))
    own_last = jnp.where(segment == leave, 1.0, 0.0)
    keep_in = jnp.where(segment == entry, 1.0, 0.0)
    weight_stack = stacked_columns(own_last * jnp.exp(cum[:, length - 1 :] - cum) * stride)
    factor_stack = stacked_columns(keep_in * jnp.exp(cum))
    write_t = writes[...].astype(F32).T.astype(BF16)

    def quarter_of_state(quarter):
        cols = pl.ds(pl.multiple_of(quarter * width, LANES), width)
        high, low = split2(features[:, cols].astype(F32) * matmul(weight_stack, spread_ref[:, cols]))
        return matmul(write_t, high) + matmul(write_t, low)

    share_out(own, quarter_of_state, [send.at[0:part] for send in sends], scratch)
    read_t = reads[...].astype(F32).T.astype(BF16)

    keeps = []

    def back_quarter(quarter):
        cols = pl.ds(pl.multiple_of(quarter * width, LANES), width)
        wide = matmul(factor_stack, spread_ref[:, cols])
        keeps.append(jnp.broadcast_to(wide[length - 1 :], (8, width)))
        high, low = split2(cotangent[:, cols].astype(F32) * wide)
        return matmul(read_t, high) + matmul(read_t, low)

    places = [
        late[LATE.index(distance)] if distance in LATE else send.at[part + 8 :]
        for distance, send in enumerate(sends)
    ]
    share_out(own, back_quarter, places, scratch)
    for distance, send in enumerate(sends):
        send[part : part + 8] = keeps[distance % QUARTERS]
    weight_cols[...] = weight_stack
    factor_cols[...] = factor_stack
    cum_cols[...] = stacked_columns(cum * LOG2E)
    cum_rows[...] = cum * LOG2E - jnp.log2(stride)
    stride_out[...] = stride
    log_out[...] = log_decay


def inner_kernel(offset, last, starts, cum_cols, cum_rows, features, cotangent, writes, reads, *refs):
    if last:
        refs = refs[:1] + refs[5:]
    else:
        refs = refs[1:]
    if last:
        before, inside, feature_part, skip_part, write_part, read_part = refs[:6]
    else:
        inside, feature_part, skip_part, grad_out = refs[:4]
    scores_ref, mask_ref, grad_ref = refs[-3:]
    length, width = features.shape
    heads = cum_rows.shape[0]
    here = heads // QUARTERS
    head_dim = width // here
    pair = 2 * head_dim
    step = pl.program_id(0)

    @pl.when(step == 0)
    def _():
        first = lax.axis_index("ctx") * length
        segment_row = document_at(starts, first + iota((1, length), 1))
        segment_col = document_at(starts, first + iota((length, 1), 0))
        causal = iota((length, length), 0) >= iota((length, length), 1)
        mask_ref[...] = jnp.where((segment_row == segment_col) & causal, 0.0, FAR)
        scores_ref[...] = matmul_nt(reads[...], writes[...])
        grad_ref[...] = before[...] if last else jnp.zeros_like(grad_ref)

    def one_pair(at, carry):
        cols = pl.ds(pl.multiple_of(at * pair, LANES), pair)
        feature = features[:, cols]
        grad = cotangent[:, cols]
        grad_f32 = grad.astype(F32)
        grad_t = grad_f32.T.astype(BF16)
        skip_part[:, cols] = jnp.sum(grad_f32 * feature.astype(F32), axis=0, keepdims=True)
        head = (offset + step) * here + at * 2
        lane = iota((LANES, 2 * LANES), 0)
        wanted = head + lax.div(iota((LANES, 2 * LANES), 1), LANES)
        pick = (lane == wanted) | (lane == wanted + heads) | (lane == wanted + 2 * heads)
        upper = matmul(cum_cols[...], jnp.where(pick, 1.0, 0.0).astype(BF16))
        second = iota((LANES, pair), 1) >= head_dim
        back = [None, None]
        for block in range(length // LANES):
            rows = slice(block * LANES, (block + 1) * LANES)
            reach = (block + 1) * LANES
            values = []
            for side in range(2):
                high_row = jnp.concatenate([upper[rows, side * LANES : (side + 1) * LANES]] * (block + 1), axis=1)
                low_row = cum_rows[pl.ds(head + side, 1), :][:, 0:reach]
                weight = jnp.exp2(high_row - low_row + mask_ref[rows, 0:reach])
                high, low = split2(weight * scores_ref[rows, 0:reach])
                values.append(matmul(high, feature[0:reach]) + matmul(low, feature[0:reach]))
                grad_rows = grad_t[side * head_dim : (side + 1) * head_dim, rows]
                found = matmul(grad_rows, high) + matmul(grad_rows, low)
                if block:
                    found = jnp.concatenate([found[:, : reach - LANES] + back[side], found[:, reach - LANES :]], axis=1)
                back[side] = found
                only = jnp.where(second == (side == 1), grad_f32[rows], 0.0).astype(BF16)
                grad_ref[rows, 0:reach] += matmul_nt(only, feature[0:reach]) * weight
            inside[rows, cols] = jnp.where(second, values[1], values[0])
        feature_part[:, cols] = jnp.concatenate(back, axis=0).T
        return carry

    lax.fori_loop(0, here // 2, one_pair, 0)

    @pl.when(step == pl.num_programs(0) - 1)
    def _():
        score_grad = grad_ref[...]
        if last:
            high, low = split2(score_grad)
            read_part[...] = matmul(high, writes[...]) + matmul(low, writes[...])
            high, low = split2(score_grad.T)
            write_part[...] = matmul(high, reads[...]) + matmul(low, reads[...])
        else:
            grad_out[...] = score_grad


def in_order(refs, scratch, back=False):
    own = group_place()
    rows = scratch.shape[1]
    for distance, ref in enumerate(refs):
        first = ref.shape[0] - rows if back else 0
        scratch[own ^ distance] = ref[first : first + rows]


def hold_kernel(*refs):
    count = len(LATE)
    for value, out in zip(refs[:count], refs[count + 1 :]):
        out[...] = value[...]


def group_kernel(part, *refs):
    up, keeps, came = refs[-3:]
    in_order(refs[:GROUP], came)
    total = came[0, 0:part]
    keep = came[0, part:]
    for j in range(1, GROUP):
        total = total * came[j, part : part + 1] + came[j, 0:part]
        keep = keep * came[j, part:]
    up[0:part] = total
    up[part:] = keep
    for j in range(GROUP):
        keeps[j : j + 1] = came[j, part : part + 1]


def back_group_kernel(part, *refs):
    keeps, up = refs[GROUP : GROUP + 2]
    down, came = refs[-2:]
    in_order(refs[:GROUP], came, back=True)
    total = came[GROUP - 1]
    for j in reversed(range(GROUP - 1)):
        total = total * keeps[j : j + 1] + came[j]
    down[0:part] = total
    down[part:] = up[part:]


def arrived(part, came):
    total, keep = came[0][0:part], came[0][part : part + 1]
    for ref in came[1:]:
        total = total + keep * ref[0:part]
        keep = keep * ref[part : part + 1]
    return total, keep


def link_kernel(part, own, *refs):
    total, keep = arrived(part, refs[:-1])
    refs[-1][0:part] = own[0:part] + own[part : part + 1] * total
    refs[-1][part:] = own[part:] * keep


def give_out(outs, scratch):
    own = group_place()
    for distance, out in enumerate(outs):
        out[...] = scratch[own ^ distance]


def spread_kernel(part, count, *refs):
    came, out = refs[-2:]
    in_order(refs[:GROUP], came)
    total = arrived(part, refs[GROUP : GROUP + count])[0]
    for j in range(GROUP):
        out[j] = total
        if j < GROUP - 1:
            total = total * came[j, part : part + 1] + came[j, 0:part]
    give_out(refs[-2 - GROUP : -2], out)


def back_spread_kernel(part, count, *refs):
    keeps = refs[GROUP]
    came, out = refs[-2:]
    in_order(refs[:GROUP], came, back=True)
    total = arrived(part, refs[GROUP + 1 : GROUP + 1 + count])[0]
    for j in reversed(range(GROUP)):
        out[j] = total
        if j > 0:
            total = total * keeps[j : j + 1] + came[j]
    give_out(refs[-2 - GROUP : -2], out)


def head_sums(ref, value, spread):
    high, low = split2(value)
    ref[...] += matmul_nt(high, spread) + matmul_nt(low, spread)


def wide_skip(skip, heads, spread):
    stack = stacked_columns(jnp.broadcast_to(column(skip[...]), (heads, LANES)))
    return matmul(stack[0:16], spread)[0:1]


def quarter_rows(scratch):
    step = pl.program_id(0)
    return jnp.concatenate([scratch[half * QUARTERS + step] for half in range(HALVES)], axis=0)


def finish_kernel(skip, factor_cols, spread_ref, features, cotangent, reads, inside, read_part, *refs):
    haves = refs[:GROUP]
    mixed, read_grad, rows, kept, read_acc, have = refs[GROUP + 1 :]
    length, state = reads.shape
    heads = skip.shape[1]
    step = pl.program_id(0)

    @pl.when(step == 0)
    def _():
        rows[...] = jnp.zeros_like(rows)
        read_acc[...] = jnp.zeros_like(read_acc)
        in_order(haves, have)

    spread = spread_ref[...]
    factor = matmul(factor_cols[...], spread)
    grad = cotangent[...].astype(F32)
    entering = quarter_rows(have)
    kept[...] = entering * factor[length - 1 :]
    stack = jnp.concatenate(split2(entering), axis=0)
    reads2 = jnp.concatenate([reads[...]] * 2, axis=1)
    total = inside[...] + factor * matmul(reads2, stack)
    mixed[...] = (total + wide_skip(skip, heads, spread) * features[...].astype(F32)).astype(BF16)
    head_sums(rows, grad * total, spread)
    high, low = split2(factor * grad)
    read_acc[...] += matmul_nt(high, stack) + matmul_nt(low, stack)

    @pl.when(step == QUARTERS - 1)
    def _():
        read_grad[...] = (read_part[...] + read_acc[:, :state] + read_acc[:, state:]).astype(BF16)


def back_finish_kernel(
    logits, bias, decay, weight_cols, stride_ref, log_ref, spread_ref,
    features, writes, feature_part, skip_part, row_ref, kept, *refs,
):
    haves = refs[:GROUP]
    step_grad, sums, col_acc, last_acc, skip_acc, have = refs[GROUP:]
    heads, length = logits.shape
    state = writes.shape[1]
    width = features.shape[1]
    step = pl.program_id(0)

    @pl.when(step == 0)
    def _():
        for ref in (col_acc, last_acc, skip_acc):
            ref[...] = jnp.zeros_like(ref)
        in_order(haves, have)

    spread = spread_ref[...]
    weight = matmul(weight_cols[...], spread)
    feature = features[...].astype(F32)
    returning = quarter_rows(have)
    stack = jnp.concatenate(split2(returning), axis=0)
    writes2 = jnp.concatenate([writes[...]] * 2, axis=1)
    carried = weight * matmul(writes2, stack)
    total = feature_part[...] + carried
    head_sums(col_acc, feature * total, spread)
    leaving = jnp.sum((returning * kept[...]).reshape(state // 8, 8, width), axis=0)
    leaving = leaving + jnp.sum((feature * carried).reshape(length // 8, 8, width), axis=0)
    head_sums(last_acc, leaving, spread)
    head_sums(skip_acc, jnp.broadcast_to(skip_part[...], (8, width)), spread)

    @pl.when(step == QUARTERS - 1)
    def _():
        rows = row_ref[...].T[:heads]
        cols = col_acc[...].T[:heads]
        last = column(jnp.sum(last_acc[...], axis=0, keepdims=True))[:heads]
        stride = stride_ref[...]
        gap_grad = rows - cols + jnp.where(iota((heads, length), 1) == length - 1, last, 0.0)
        onward = jnp.where(iota((length, length), 0) >= iota((length, length), 1), 1.0, 0.0).astype(BF16)
        parts = matmul(jnp.concatenate(split3(gap_grad), axis=0), onward)
        log_grad = parts[:heads] + parts[heads : 2 * heads] + parts[2 * heads :]
        rate = column(-jnp.exp(decay[...]))
        slope = 1.0 / (1.0 + jnp.exp(-(logits[...] + column(bias[...]))))
        step_value = (cols / stride + rate * log_grad) * slope
        step_grad[...] = step_value
        bias_sum = jnp.sum(step_value, axis=1, keepdims=True)
        decay_sum = jnp.sum(log_grad * log_ref[...], axis=1, keepdims=True)
        skip_sum = column(skip_acc[0:1])[:heads]
        spare = jnp.zeros((LANES - 3 * heads, 1), F32)
        table = jnp.concatenate([bias_sum, decay_sum, skip_sum, spare], axis=0)
        eye = iota((LANES, LANES), 0) == iota((LANES, LANES), 1)
        table = jnp.sum(jnp.where(eye, table, 0.0), axis=0, keepdims=True)
        sums[...] = jnp.broadcast_to(table[None], sums.shape)


def write_kernel(
    skip, weight_cols, spread_ref, features, cotangent, writes, feature_part, write_part, *refs,
):
    feature_grad, write_grad, write_acc, have = refs[GROUP + 1 :]
    state = write_part.shape[1]
    step = pl.program_id(0)

    @pl.when(step == 0)
    def _():
        write_acc[...] = jnp.zeros_like(write_acc)
        in_order(refs[:GROUP], have)

    spread = spread_ref[...]
    weight = matmul(weight_cols[...], spread)
    stack = jnp.concatenate(split2(quarter_rows(have)), axis=0)
    writes2 = jnp.concatenate([writes[...]] * 2, axis=1)
    total = feature_part[...] + weight * matmul(writes2, stack)
    skips = wide_skip(skip, skip.shape[1], spread) * cotangent[...].astype(F32)
    feature_grad[...] = (total + skips).astype(BF16)
    high, low = split2(weight * features[...].astype(F32))
    write_acc[...] += matmul_nt(high, stack) + matmul_nt(low, stack)

    @pl.when(step == QUARTERS - 1)
    def _():
        write_grad[...] = (write_part[...] + write_acc[:, :state] + write_acc[:, state:]).astype(BF16)


def call(kernel, name, outs, in_specs, work, mib, **more):
    return pl.pallas_call(
        kernel,
        out_shape=outs,
        in_specs=in_specs,
        out_specs=more.pop("out_specs", [VMEM] * len(outs)),
        compiler_params=pltpu.CompilerParams(vmem_limit_bytes=mib * 2**20),
        cost_estimate=pl.CostEstimate(flops=work * 10**9, bytes_accessed=10**6, transcendentals=0),
        name=name,
        **more,
    )


def struct(shape, dtype=F32):
    return jax.ShapeDtypeStruct(shape, dtype)


def local(
    features, write_keys, read_queries, step_logits, step_bias, decay_log, skip_gain, doc_starts, out_grad
):
    features, writes, reads, logits, cotangent = (
        features[0], write_keys[0], read_queries[0], step_logits[0], out_grad[0]
    )
    length, wide = features.shape
    heads = logits.shape[0]
    state = writes.shape[1]
    head_dim = wide // heads
    width = wide // QUARTERS
    part = state // HALVES
    bias, decay, skip = step_bias[None], decay_log[None], skip_gain[None]
    blocks, members = lax.axis_size("ctx"), lax.axis_size("dp")
    spread = spread_table(heads, head_dim)

    def exchange(value, distance):
        return lax.ppermute(value, "ctx", [(k, k ^ distance) for k in range(blocks)])

    def swap(values):
        came = {d: exchange(values[d], d) for d in EARLY + LATE}
        return [came.get(d, values[0]) for d in range(GROUP)]

    def shift(value, distance):
        pairs = [(k, k + distance) for k in range(blocks) if 0 <= k + distance < blocks]
        return lax.ppermute(value, "ctx", pairs)

    def scan(own, sign):
        came, near, reach = [], own, 1
        while reach < blocks // GROUP:
            came.append(shift(near, sign * GROUP * reach))
            reach *= 2
            if reach < blocks // GROUP:
                near = call(
                    functools.partial(link_kernel, part), "link", [group_sum], [VMEM] * (1 + len(came)), 1, 8
                )(own, *came)[0]
        return came

    def all_of(*shape):
        return pl.BlockSpec(shape, lambda step: (0,) * len(shape))

    def quarter_of(rows, offset=0):
        return pl.BlockSpec((rows, width), lambda step: (0, step + offset))

    stack = struct((length, LANES), BF16)
    small = struct((heads, length))
    result = struct((length, wide), BF16)
    tokens_result = struct((length, state), BF16)
    group_sum = struct((part + 8, width))
    share = struct((part, width))
    tokens = all_of(length, state)
    columns = all_of(length, LANES)
    by_heads = all_of(heads, length)
    row = all_of(1, heads)
    whole_share = all_of(part, width)
    by_quarter = quarter_of(length)
    spread_quarter = quarter_of(LANES)
    shares = pltpu.VMEM((GROUP, part, width), F32)
    long_shares = pltpu.VMEM((GROUP, part + 8, width), F32)

    both = struct((2 * part + 8, width))
    out = call(
        states_kernel,
        "states",
        [group_sum if d in LATE else both for d in range(GROUP)] + [share] * len(LATE) + [stack] * 3 + [small] * 3,
        [SMEM] + [VMEM] * 8,
        4,
        60,
        scratch_shapes=[pltpu.VMEM((state, width), F32)],
    )(doc_starts, logits, bias, decay, spread, features, writes, cotangent, reads)
    send, late_send = out[:GROUP], out[GROUP : GROUP + len(LATE)]
    weight_cols, factor_cols, cum_cols, cum_rows, stride, log_decay = out[GROUP + len(LATE) :]
    came = swap(send)

    half = QUARTERS // 2
    started = struct((length, wide)), struct((length, wide)), struct((1, wide))
    square = all_of(length, length)
    inner_args = (doc_starts, cum_cols, cum_rows, features, cotangent, writes, reads)
    score_scratch = [pltpu.VMEM((length, length), F32)] * 3

    def inner_specs(offset):
        mine = quarter_of(length, offset)
        return [SMEM, columns, by_heads, mine, mine, tokens, tokens], [mine, mine, quarter_of(1, offset)]

    specs, out_specs = inner_specs(0)
    *begun, score_grad = call(
        functools.partial(inner_kernel, 0, False),
        "inner_first",
        [*started, struct((length, length))],
        specs + [ANY],
        1,
        24,
        grid=(half,),
        out_specs=out_specs + [square],
        scratch_shapes=score_scratch,
    )(*inner_args, cum_rows)
    specs, out_specs = inner_specs(half)
    inside, feature_part, skip_part, write_part, read_part = call(
        functools.partial(inner_kernel, half, True),
        "inner_second",
        [*started, struct((length, state)), struct((length, state))],
        specs + [square] + [ANY] * 4,
        10,
        24,
        grid=(half,),
        out_specs=out_specs + [tokens, tokens],
        scratch_shapes=score_scratch,
        input_output_aliases={8: 0, 9: 1, 10: 2},
    )(*inner_args, score_grad, *begun, cum_rows)
    up, keeps = call(
        functools.partial(group_kernel, part),
        "group",
        [group_sum, struct((GROUP, width))],
        [VMEM] * GROUP + [ANY],
        2,
        8,
        scratch_shapes=[long_shares],
    )(*came, write_part)
    ups = scan(up, 1)
    held = call(hold_kernel, "hold", [share] * len(LATE), [VMEM] * len(LATE) + [ANY], 1, 8)(*late_send, up)
    late_came = [exchange(value, d) for value, d in zip(held, LATE)]
    back_came = [late_came[LATE.index(d)] if d in LATE else came[d] for d in range(GROUP)]

    give = call(
        functools.partial(spread_kernel, part, len(ups)),
        "spread",
        [share] * GROUP,
        [VMEM] * (GROUP + len(ups)) + [ANY],
        2,
        12,
        scratch_shapes=[long_shares, shares],
    )(*came, *ups, up)
    (down,) = call(
        functools.partial(back_group_kernel, part),
        "back_group",
        [group_sum],
        [VMEM] * (GROUP + 2) + [ANY],
        2,
        8,
        scratch_shapes=[shares],
    )(*back_came, keeps, up, give[0])
    downs = scan(down, -1)
    have = swap(give)
    back_give = call(
        functools.partial(back_spread_kernel, part, len(downs)),
        "back_spread",
        [share] * GROUP,
        [VMEM] * (GROUP + 1 + len(downs)) + [ANY],
        2,
        12,
        scratch_shapes=[shares, shares],
    )(*back_came, keeps, *downs, give[0])
    back_have = swap(back_give)

    mixed, read_grad, rows, kept = call(
        finish_kernel,
        "finish",
        [result, tokens_result, struct((length, LANES)), struct((state, wide))],
        [row, columns, spread_quarter, by_quarter, by_quarter, tokens, by_quarter, tokens]
        + [whole_share] * GROUP
        + [ANY],
        8,
        24,
        grid=(QUARTERS,),
        out_specs=[by_quarter, tokens, columns, quarter_of(state)],
        scratch_shapes=[pltpu.VMEM((length, 2 * state), F32), shares],
    )(skip, factor_cols, spread, features, cotangent, reads, inside, read_part, *have, back_give[0])
    devices = blocks * members
    step_grad, sums = call(
        back_finish_kernel,
        "back_finish",
        [small, struct((devices, 1, LANES))],
        [by_heads, row, row, columns, by_heads, by_heads, spread_quarter]
        + [by_quarter, tokens, by_quarter]
        + [quarter_of(1), columns, quarter_of(state)]
        + [whole_share] * GROUP,
        8,
        24,
        grid=(QUARTERS,),
        out_specs=[by_heads, all_of(devices, 1, LANES)],
        scratch_shapes=[
            pltpu.VMEM((length, LANES), F32),
            pltpu.VMEM((8, LANES), F32),
            pltpu.VMEM((8, LANES), F32),
            shares,
        ],
    )(
        logits, bias, decay, weight_cols, stride, log_decay, spread, features, writes,
        feature_part, skip_part, rows, kept, *back_have,
    )
    feature_grad, write_grad = call(
        write_kernel,
        "write_grad",
        [result, tokens_result],
        [row, columns, spread_quarter, by_quarter, by_quarter, tokens, by_quarter, tokens]
        + [whole_share] * GROUP
        + [ANY],
        6,
        24,
        grid=(QUARTERS,),
        out_specs=[by_quarter, tokens],
        scratch_shapes=[pltpu.VMEM((length, 2 * state), F32), shares],
    )(skip, weight_cols, spread, features, cotangent, writes, feature_part, write_part, *back_have, step_grad)
    sums = jnp.sum(lax.all_to_all(sums, ("dp", "ctx"), 0, 0), axis=(0, 1))
    return (
        mixed[None],
        feature_grad[None],
        write_grad[None],
        read_grad[None],
        step_grad[None],
        sums[:heads],
        sums[heads : 2 * heads],
        sums[2 * heads : 3 * heads],
    )


def solution(mesh):
    by_tokens = P("dp", "ctx", None)
    by_heads = P("dp", None, "ctx")
    in_specs = (by_tokens, by_tokens, by_tokens, by_heads, P(), P(), P(), P("dp", None), by_tokens)
    out_specs = (by_tokens, by_tokens, by_tokens, by_tokens, by_heads, P(), P(), P())
    return jax.shard_map(local, mesh=mesh, in_specs=in_specs, out_specs=out_specs, check_vma=False)
```

```python
import functools

import jax
import jax.numpy as jnp
import numpy as np
from jax import lax
from jax.experimental import pallas as pl
from jax.experimental.pallas import tpu as pltpu
from jax.sharding import PartitionSpec as P

F32 = jnp.float32
BF16 = jnp.bfloat16
QUARTERS = 4
HALVES = 2
GROUP = QUARTERS * HALVES
DISTANCES = (1, 2, 4, 7, 3, 5, 6)
LANES = 128
LOG2E = 1.4426950408889634
FAR = -1e30
VMEM = pl.BlockSpec(memory_space=pltpu.VMEM)
SMEM = pl.BlockSpec(memory_space=pltpu.SMEM)
ANY = pl.BlockSpec(memory_space=pl.ANY)


def iota(shape, axis):
    return lax.broadcasted_iota(jnp.int32, shape, axis)


def matmul(left, right):
    return lax.dot_general(left, right, (((1,), (0,)), ((), ())), preferred_element_type=F32)


def matmul_nt(left, right):
    return lax.dot_general(left, right, (((1,), (1,)), ((), ())), preferred_element_type=F32)


def split2(value):
    high = value.astype(BF16)
    return high, (value - high.astype(F32)).astype(BF16)


def split3(value):
    high = value.astype(BF16)
    rest = value - high.astype(F32)
    middle = rest.astype(BF16)
    return high, middle, (rest - middle.astype(F32)).astype(BF16)


def column(row):
    count = row.shape[1]
    eye = iota((count, count), 0) == iota((count, count), 1)
    return jnp.sum(jnp.where(eye, row, 0.0), axis=1, keepdims=True)


def stacked_columns(rows):
    parts = [part.astype(F32) for part in split3(rows)]
    spare = LANES - 3 * rows.shape[0]
    if spare:
        parts.append(jnp.zeros((spare, rows.shape[1]), F32))
    return jnp.concatenate(parts, axis=0).T.astype(BF16)


def spread_table(heads, head_dim):
    table = np.zeros((LANES, heads * head_dim), np.float32)
    for head in range(heads):
        for part in range(3):
            table[part * heads + head, head * head_dim : (head + 1) * head_dim] = 1.0
    return jnp.asarray(table, BF16)


def softplus(value):
    return jnp.maximum(value, 0.0) + jnp.log1p(jnp.exp(-jnp.abs(value)))


def document_at(starts_ref, position):
    total = jnp.zeros_like(position)
    for entry in range(starts_ref.shape[1]):
        total = total + (starts_ref[0, entry] <= position).astype(jnp.int32)
    return total


def group_place():
    return lax.rem(lax.axis_index("ctx"), GROUP)


def share_out(own, quarter_of_state, places, scratch):
    mine = lax.div(own, QUARTERS)
    part = scratch.shape[0] // HALVES
    for distance in range(QUARTERS):
        scratch[...] = quarter_of_state(lax.rem(own ^ distance, QUARTERS))
        for half in range(HALVES):
            rows = pl.ds(pl.multiple_of((mine ^ half) * part, part), part)
            places[half * QUARTERS + distance][...] = scratch[rows]


def states_kernel(starts, logits, bias, decay, spread_ref, features, writes, cotangent, reads, *refs):
    sends = refs[:GROUP]
    weight_cols, factor_cols, cum_cols, cum_rows, stride_out, log_out, scratch = refs[GROUP:]
    heads, length = logits.shape
    state = writes.shape[1]
    width = features.shape[1] // QUARTERS
    part = state // HALVES
    first = lax.axis_index("ctx") * length
    own = group_place()
    stride = softplus(logits[...] + column(bias[...]))
    log_decay = stride * column(-jnp.exp(decay[...]))
    upto = jnp.where(iota((length, length), 0) <= iota((length, length), 1), 1.0, 0.0).astype(BF16)
    parts = matmul(jnp.concatenate(split3(log_decay), axis=0), upto)
    cum = parts[:heads] + parts[heads : 2 * heads] + parts[2 * heads :]
    segment = document_at(starts, first + iota((1, length), 1))
    entry = document_at(starts, jnp.full((1, 1), first - 1, jnp.int32))
    leave = document_at(starts, jnp.full((1, 1), first + length - 1, jnp.int32))
    own_last = jnp.where(segment == leave, 1.0, 0.0)
    keep_in = jnp.where(segment == entry, 1.0, 0.0)
    weight_stack = stacked_columns(own_last * jnp.exp(cum[:, length - 1 :] - cum) * stride)
    factor_stack = stacked_columns(keep_in * jnp.exp(cum))
    write_t = writes[...].astype(F32).T.astype(BF16)

    def quarter_of_state(quarter):
        cols = pl.ds(pl.multiple_of(quarter * width, LANES), width)
        high, low = split2(features[:, cols].astype(F32) * matmul(weight_stack, spread_ref[:, cols]))
        return matmul(write_t, high) + matmul(write_t, low)

    share_out(own, quarter_of_state, [send.at[0:part] for send in sends], scratch)
    read_t = reads[...].astype(F32).T.astype(BF16)

    keeps = []

    def back_quarter(quarter):
        cols = pl.ds(pl.multiple_of(quarter * width, LANES), width)
        wide = matmul(factor_stack, spread_ref[:, cols])
        keeps.append(jnp.broadcast_to(wide[length - 1 :], (8, width)))
        high, low = split2(cotangent[:, cols].astype(F32) * wide)
        return matmul(read_t, high) + matmul(read_t, low)

    share_out(own, back_quarter, [send.at[part + 8 :] for send in sends], scratch)
    for distance, send in enumerate(sends):
        send[part : part + 8] = keeps[distance % QUARTERS]
    weight_cols[...] = weight_stack
    factor_cols[...] = factor_stack
    cum_cols[...] = stacked_columns(cum * LOG2E)
    cum_rows[...] = cum * LOG2E - jnp.log2(stride)
    stride_out[...] = stride
    log_out[...] = log_decay


def inner_kernel(offset, last, starts, cum_cols, cum_rows, features, cotangent, writes, reads, *refs):
    if last:
        refs = refs[:1] + refs[5:]
    else:
        refs = refs[1:]
    if last:
        before, inside, feature_part, skip_part, write_part, read_part = refs[:6]
    else:
        inside, feature_part, skip_part, grad_out = refs[:4]
    scores_ref, mask_ref, grad_ref = refs[-3:]
    length, width = features.shape
    heads = cum_rows.shape[0]
    here = heads // QUARTERS
    head_dim = width // here
    pair = 2 * head_dim
    step = pl.program_id(0)

    @pl.when(step == 0)
    def _():
        first = lax.axis_index("ctx") * length
        segment_row = document_at(starts, first + iota((1, length), 1))
        segment_col = document_at(starts, first + iota((length, 1), 0))
        causal = iota((length, length), 0) >= iota((length, length), 1)
        mask_ref[...] = jnp.where((segment_row == segment_col) & causal, 0.0, FAR)
        scores_ref[...] = matmul_nt(reads[...], writes[...])
        grad_ref[...] = before[...] if last else jnp.zeros_like(grad_ref)

    def one_pair(at, carry):
        cols = pl.ds(pl.multiple_of(at * pair, LANES), pair)
        feature = features[:, cols]
        grad = cotangent[:, cols]
        grad_f32 = grad.astype(F32)
        grad_t = grad_f32.T.astype(BF16)
        skip_part[:, cols] = jnp.sum(grad_f32 * feature.astype(F32), axis=0, keepdims=True)
        head = (offset + step) * here + at * 2
        lane = iota((LANES, 2 * LANES), 0)
        wanted = head + lax.div(iota((LANES, 2 * LANES), 1), LANES)
        pick = (lane == wanted) | (lane == wanted + heads) | (lane == wanted + 2 * heads)
        upper = matmul(cum_cols[...], jnp.where(pick, 1.0, 0.0).astype(BF16))
        second = iota((LANES, pair), 1) >= head_dim
        back = [None, None]
        for block in range(length // LANES):
            rows = slice(block * LANES, (block + 1) * LANES)
            reach = (block + 1) * LANES
            values = []
            for side in range(2):
                high_row = jnp.concatenate([upper[rows, side * LANES : (side + 1) * LANES]] * (block + 1), axis=1)
                low_row = cum_rows[pl.ds(head + side, 1), :][:, 0:reach]
                weight = jnp.exp2(high_row - low_row + mask_ref[rows, 0:reach])
                high, low = split2(weight * scores_ref[rows, 0:reach])
                values.append(matmul(high, feature[0:reach]) + matmul(low, feature[0:reach]))
                grad_rows = grad_t[side * head_dim : (side + 1) * head_dim, rows]
                found = matmul(grad_rows, high) + matmul(grad_rows, low)
                if block:
                    found = jnp.concatenate([found[:, : reach - LANES] + back[side], found[:, reach - LANES :]], axis=1)
                back[side] = found
                only = jnp.where(second == (side == 1), grad_f32[rows], 0.0).astype(BF16)
                grad_ref[rows, 0:reach] += matmul_nt(only, feature[0:reach]) * weight
            inside[rows, cols] = jnp.where(second, values[1], values[0])
        feature_part[:, cols] = jnp.concatenate(back, axis=0).T
        return carry

    lax.fori_loop(0, here // 2, one_pair, 0)

    @pl.when(step == pl.num_programs(0) - 1)
    def _():
        score_grad = grad_ref[...]
        if last:
            high, low = split2(score_grad)
            read_part[...] = matmul(high, writes[...]) + matmul(low, writes[...])
            high, low = split2(score_grad.T)
            write_part[...] = matmul(high, reads[...]) + matmul(low, reads[...])
        else:
            grad_out[...] = score_grad


def in_order(refs, scratch, back=False):
    own = group_place()
    rows = scratch.shape[1]
    for distance, ref in enumerate(refs):
        first = ref.shape[0] - rows if back else 0
        scratch[own ^ distance] = ref[first : first + rows]


def group_kernel(part, *refs):
    up, keeps, came = refs[-3:]
    in_order(refs[:GROUP], came)
    total = came[0, 0:part]
    keep = came[0, part:]
    for j in range(1, GROUP):
        total = total * came[j, part : part + 1] + came[j, 0:part]
        keep = keep * came[j, part:]
    up[0:part] = total
    up[part:] = keep
    for j in range(GROUP):
        keeps[j : j + 1] = came[j, part : part + 1]


def back_group_kernel(part, *refs):
    keeps, up = refs[GROUP : GROUP + 2]
    down, came = refs[-2:]
    in_order(refs[:GROUP], came, back=True)
    total = came[GROUP - 1]
    for j in reversed(range(GROUP - 1)):
        total = total * keeps[j : j + 1] + came[j]
    down[0:part] = total
    down[part:] = up[part:]


def arrived(part, came):
    total, keep = came[0][0:part], came[0][part : part + 1]
    for ref in came[1:]:
        total = total + keep * ref[0:part]
        keep = keep * ref[part : part + 1]
    return total, keep


def link_kernel(part, own, *refs):
    total, keep = arrived(part, refs[:-1])
    refs[-1][0:part] = own[0:part] + own[part : part + 1] * total
    refs[-1][part:] = own[part:] * keep


def give_out(outs, scratch):
    own = group_place()
    for distance, out in enumerate(outs):
        out[...] = scratch[own ^ distance]


def spread_kernel(part, count, *refs):
    came, out = refs[-2:]
    in_order(refs[:GROUP], came)
    total = arrived(part, refs[GROUP : GROUP + count])[0]
    for j in range(GROUP):
        out[j] = total
        if j < GROUP - 1:
            total = total * came[j, part : part + 1] + came[j, 0:part]
    give_out(refs[-2 - GROUP : -2], out)


def back_spread_kernel(part, count, *refs):
    keeps = refs[GROUP]
    came, out = refs[-2:]
    in_order(refs[:GROUP], came, back=True)
    total = arrived(part, refs[GROUP + 1 : GROUP + 1 + count])[0]
    for j in reversed(range(GROUP)):
        out[j] = total
        if j > 0:
            total = total * keeps[j : j + 1] + came[j]
    give_out(refs[-2 - GROUP : -2], out)


def head_sums(ref, value, spread):
    high, low = split2(value)
    ref[...] += matmul_nt(high, spread) + matmul_nt(low, spread)


def wide_skip(skip, heads, spread):
    stack = stacked_columns(jnp.broadcast_to(column(skip[...]), (heads, LANES)))
    return matmul(stack[0:16], spread)[0:1]


def quarter_rows(scratch):
    step = pl.program_id(0)
    return jnp.concatenate([scratch[half * QUARTERS + step] for half in range(HALVES)], axis=0)


def finish_kernel(skip, factor_cols, spread_ref, features, cotangent, reads, inside, read_part, *refs):
    haves = refs[:GROUP]
    mixed, read_grad, rows, kept, read_acc, have = refs[GROUP + 1 :]
    length, state = reads.shape
    heads = skip.shape[1]
    step = pl.program_id(0)

    @pl.when(step == 0)
    def _():
        rows[...] = jnp.zeros_like(rows)
        read_acc[...] = jnp.zeros_like(read_acc)
        in_order(haves, have)

    spread = spread_ref[...]
    factor = matmul(factor_cols[...], spread)
    grad = cotangent[...].astype(F32)
    entering = quarter_rows(have)
    kept[...] = entering * factor[length - 1 :]
    stack = jnp.concatenate(split2(entering), axis=0)
    reads2 = jnp.concatenate([reads[...]] * 2, axis=1)
    total = inside[...] + factor * matmul(reads2, stack)
    mixed[...] = (total + wide_skip(skip, heads, spread) * features[...].astype(F32)).astype(BF16)
    head_sums(rows, grad * total, spread)
    high, low = split2(factor * grad)
    read_acc[...] += matmul_nt(high, stack) + matmul_nt(low, stack)

    @pl.when(step == QUARTERS - 1)
    def _():
        read_grad[...] = (read_part[...] + read_acc[:, :state] + read_acc[:, state:]).astype(BF16)


def back_finish_kernel(
    logits, bias, decay, weight_cols, stride_ref, log_ref, spread_ref,
    features, writes, feature_part, skip_part, row_ref, kept, *refs,
):
    haves = refs[:GROUP]
    step_grad, sums, col_acc, last_acc, skip_acc, have = refs[GROUP:]
    heads, length = logits.shape
    state = writes.shape[1]
    width = features.shape[1]
    step = pl.program_id(0)

    @pl.when(step == 0)
    def _():
        for ref in (col_acc, last_acc, skip_acc):
            ref[...] = jnp.zeros_like(ref)
        in_order(haves, have)

    spread = spread_ref[...]
    weight = matmul(weight_cols[...], spread)
    feature = features[...].astype(F32)
    returning = quarter_rows(have)
    stack = jnp.concatenate(split2(returning), axis=0)
    writes2 = jnp.concatenate([writes[...]] * 2, axis=1)
    carried = weight * matmul(writes2, stack)
    total = feature_part[...] + carried
    head_sums(col_acc, feature * total, spread)
    leaving = jnp.sum((returning * kept[...]).reshape(state // 8, 8, width), axis=0)
    leaving = leaving + jnp.sum((feature * carried).reshape(length // 8, 8, width), axis=0)
    head_sums(last_acc, leaving, spread)
    head_sums(skip_acc, jnp.broadcast_to(skip_part[...], (8, width)), spread)

    @pl.when(step == QUARTERS - 1)
    def _():
        rows = row_ref[...].T[:heads]
        cols = col_acc[...].T[:heads]
        last = column(jnp.sum(last_acc[...], axis=0, keepdims=True))[:heads]
        stride = stride_ref[...]
        gap_grad = rows - cols + jnp.where(iota((heads, length), 1) == length - 1, last, 0.0)
        onward = jnp.where(iota((length, length), 0) >= iota((length, length), 1), 1.0, 0.0).astype(BF16)
        parts = matmul(jnp.concatenate(split3(gap_grad), axis=0), onward)
        log_grad = parts[:heads] + parts[heads : 2 * heads] + parts[2 * heads :]
        rate = column(-jnp.exp(decay[...]))
        slope = 1.0 / (1.0 + jnp.exp(-(logits[...] + column(bias[...]))))
        step_value = (cols / stride + rate * log_grad) * slope
        step_grad[...] = step_value
        bias_sum = jnp.sum(step_value, axis=1, keepdims=True)
        decay_sum = jnp.sum(log_grad * log_ref[...], axis=1, keepdims=True)
        skip_sum = column(skip_acc[0:1])[:heads]
        spare = jnp.zeros((LANES - 3 * heads, 1), F32)
        table = jnp.concatenate([bias_sum, decay_sum, skip_sum, spare], axis=0)
        eye = iota((LANES, LANES), 0) == iota((LANES, LANES), 1)
        table = jnp.sum(jnp.where(eye, table, 0.0), axis=0, keepdims=True)
        sums[...] = jnp.broadcast_to(table[None], sums.shape)


def write_kernel(
    skip, weight_cols, spread_ref, features, cotangent, writes, feature_part, write_part, *refs,
):
    feature_grad, write_grad, write_acc, have = refs[GROUP + 1 :]
    state = write_part.shape[1]
    step = pl.program_id(0)

    @pl.when(step == 0)
    def _():
        write_acc[...] = jnp.zeros_like(write_acc)
        in_order(refs[:GROUP], have)

    spread = spread_ref[...]
    weight = matmul(weight_cols[...], spread)
    stack = jnp.concatenate(split2(quarter_rows(have)), axis=0)
    writes2 = jnp.concatenate([writes[...]] * 2, axis=1)
    total = feature_part[...] + weight * matmul(writes2, stack)
    skips = wide_skip(skip, skip.shape[1], spread) * cotangent[...].astype(F32)
    feature_grad[...] = (total + skips).astype(BF16)
    high, low = split2(weight * features[...].astype(F32))
    write_acc[...] += matmul_nt(high, stack) + matmul_nt(low, stack)

    @pl.when(step == QUARTERS - 1)
    def _():
        write_grad[...] = (write_part[...] + write_acc[:, :state] + write_acc[:, state:]).astype(BF16)


def call(kernel, name, outs, in_specs, work, mib, **more):
    return pl.pallas_call(
        kernel,
        out_shape=outs,
        in_specs=in_specs,
        out_specs=more.pop("out_specs", [VMEM] * len(outs)),
        compiler_params=pltpu.CompilerParams(vmem_limit_bytes=mib * 2**20),
        cost_estimate=pl.CostEstimate(flops=work * 10**9, bytes_accessed=10**6, transcendentals=0),
        name=name,
        **more,
    )


def struct(shape, dtype=F32):
    return jax.ShapeDtypeStruct(shape, dtype)


def local(
    features, write_keys, read_queries, step_logits, step_bias, decay_log, skip_gain, doc_starts, out_grad
):
    features, writes, reads, logits, cotangent = (
        features[0], write_keys[0], read_queries[0], step_logits[0], out_grad[0]
    )
    length, wide = features.shape
    heads = logits.shape[0]
    state = writes.shape[1]
    head_dim = wide // heads
    width = wide // QUARTERS
    part = state // HALVES
    bias, decay, skip = step_bias[None], decay_log[None], skip_gain[None]
    blocks, members = lax.axis_size("ctx"), lax.axis_size("dp")
    spread = spread_table(heads, head_dim)

    def exchange(value, distance):
        return lax.ppermute(value, "ctx", [(k, k ^ distance) for k in range(blocks)])

    def swap(values):
        came = {d: exchange(values[d], d) for d in DISTANCES}
        return [came.get(d, values[0]) for d in range(GROUP)]

    def shift(value, distance):
        pairs = [(k, k + distance) for k in range(blocks) if 0 <= k + distance < blocks]
        return lax.ppermute(value, "ctx", pairs)

    def scan(own, sign):
        came, near, reach = [], own, 1
        while reach < blocks // GROUP:
            came.append(shift(near, sign * GROUP * reach))
            reach *= 2
            if reach < blocks // GROUP:
                near = call(
                    functools.partial(link_kernel, part), "link", [group_sum], [VMEM] * (1 + len(came)), 1, 8
                )(own, *came)[0]
        return came

    def all_of(*shape):
        return pl.BlockSpec(shape, lambda step: (0,) * len(shape))

    def quarter_of(rows, offset=0):
        return pl.BlockSpec((rows, width), lambda step: (0, step + offset))

    stack = struct((length, LANES), BF16)
    small = struct((heads, length))
    result = struct((length, wide), BF16)
    tokens_result = struct((length, state), BF16)
    group_sum = struct((part + 8, width))
    share = struct((part, width))
    tokens = all_of(length, state)
    columns = all_of(length, LANES)
    by_heads = all_of(heads, length)
    row = all_of(1, heads)
    whole_share = all_of(part, width)
    by_quarter = quarter_of(length)
    spread_quarter = quarter_of(LANES)
    shares = pltpu.VMEM((GROUP, part, width), F32)
    long_shares = pltpu.VMEM((GROUP, part + 8, width), F32)

    both = struct((2 * part + 8, width))
    out = call(
        states_kernel,
        "states",
        [both] * GROUP + [stack] * 3 + [small] * 3,
        [SMEM] + [VMEM] * 8,
        4,
        60,
        scratch_shapes=[pltpu.VMEM((state, width), F32)],
    )(doc_starts, logits, bias, decay, spread, features, writes, cotangent, reads)
    came = swap(out[:GROUP])
    weight_cols, factor_cols, cum_cols, cum_rows, stride, log_decay = out[GROUP:]

    half = QUARTERS // 2
    started = struct((length, wide)), struct((length, wide)), struct((1, wide))
    square = all_of(length, length)
    inner_args = (doc_starts, cum_cols, cum_rows, features, cotangent, writes, reads)
    score_scratch = [pltpu.VMEM((length, length), F32)] * 3

    def inner_specs(offset):
        mine = quarter_of(length, offset)
        return [SMEM, columns, by_heads, mine, mine, tokens, tokens], [mine, mine, quarter_of(1, offset)]

    specs, out_specs = inner_specs(0)
    *begun, score_grad = call(
        functools.partial(inner_kernel, 0, False),
        "inner_first",
        [*started, struct((length, length))],
        specs + [ANY],
        1,
        24,
        grid=(half,),
        out_specs=out_specs + [square],
        scratch_shapes=score_scratch,
    )(*inner_args, cum_rows)
    specs, out_specs = inner_specs(half)
    inside, feature_part, skip_part, write_part, read_part = call(
        functools.partial(inner_kernel, half, True),
        "inner_second",
        [*started, struct((length, state)), struct((length, state))],
        specs + [square] + [ANY] * 4,
        10,
        24,
        grid=(half,),
        out_specs=out_specs + [tokens, tokens],
        scratch_shapes=score_scratch,
        input_output_aliases={8: 0, 9: 1, 10: 2},
    )(*inner_args, score_grad, *begun, cum_rows)
    up, keeps = call(
        functools.partial(group_kernel, part),
        "group",
        [group_sum, struct((GROUP, width))],
        [VMEM] * GROUP + [ANY],
        2,
        8,
        scratch_shapes=[long_shares],
    )(*came, write_part)
    ups = scan(up, 1)
    (down,) = call(
        functools.partial(back_group_kernel, part),
        "back_group",
        [group_sum],
        [VMEM] * (GROUP + 2),
        2,
        8,
        scratch_shapes=[shares],
    )(*came, keeps, up)
    downs = scan(down, -1)
    give = call(
        functools.partial(spread_kernel, part, len(ups)),
        "spread",
        [share] * GROUP,
        [VMEM] * (GROUP + len(ups)) + [ANY],
        2,
        12,
        scratch_shapes=[long_shares, shares],
    )(*came, *ups, down)
    have = swap(give)
    back_give = call(
        functools.partial(back_spread_kernel, part, len(downs)),
        "back_spread",
        [share] * GROUP,
        [VMEM] * (GROUP + 1 + len(downs)) + [ANY],
        2,
        12,
        scratch_shapes=[shares, shares],
    )(*came, keeps, *downs, give[0])
    back_have = swap(back_give)

    mixed, read_grad, rows, kept = call(
        finish_kernel,
        "finish",
        [result, tokens_result, struct((length, LANES)), struct((state, wide))],
        [row, columns, spread_quarter, by_quarter, by_quarter, tokens, by_quarter, tokens]
        + [whole_share] * GROUP
        + [ANY],
        8,
        24,
        grid=(QUARTERS,),
        out_specs=[by_quarter, tokens, columns, quarter_of(state)],
        scratch_shapes=[pltpu.VMEM((length, 2 * state), F32), shares],
    )(skip, factor_cols, spread, features, cotangent, reads, inside, read_part, *have, back_give[0])
    devices = blocks * members
    step_grad, sums = call(
        back_finish_kernel,
        "back_finish",
        [small, struct((devices, 1, LANES))],
        [by_heads, row, row, columns, by_heads, by_heads, spread_quarter]
        + [by_quarter, tokens, by_quarter]
        + [quarter_of(1), columns, quarter_of(state)]
        + [whole_share] * GROUP,
        8,
        24,
        grid=(QUARTERS,),
        out_specs=[by_heads, all_of(devices, 1, LANES)],
        scratch_shapes=[
            pltpu.VMEM((length, LANES), F32),
            pltpu.VMEM((8, LANES), F32),
            pltpu.VMEM((8, LANES), F32),
            shares,
        ],
    )(
        logits, bias, decay, weight_cols, stride, log_decay, spread, features, writes,
        feature_part, skip_part, rows, kept, *back_have,
    )
    feature_grad, write_grad = call(
        write_kernel,
        "write_grad",
        [result, tokens_result],
        [row, columns, spread_quarter, by_quarter, by_quarter, tokens, by_quarter, tokens]
        + [whole_share] * GROUP
        + [ANY],
        6,
        60,
        grid=(QUARTERS,),
        out_specs=[by_quarter, tokens],
        scratch_shapes=[pltpu.VMEM((length, 2 * state), F32), shares],
    )(skip, weight_cols, spread, features, cotangent, writes, feature_part, write_part, *back_have, step_grad)
    sums = jnp.sum(lax.all_to_all(sums, ("dp", "ctx"), 0, 0), axis=(0, 1))
    return (
        mixed[None],
        feature_grad[None],
        write_grad[None],
        read_grad[None],
        step_grad[None],
        sums[:heads],
        sums[heads : 2 * heads],
        sums[2 * heads : 3 * heads],
    )


def solution(mesh):
    by_tokens = P("dp", "ctx", None)
    by_heads = P("dp", None, "ctx")
    in_specs = (by_tokens, by_tokens, by_tokens, by_heads, P(), P(), P(), P("dp", None), by_tokens)
    out_specs = (by_tokens, by_tokens, by_tokens, by_tokens, by_heads, P(), P(), P())
    return jax.shard_map(local, mesh=mesh, in_specs=in_specs, out_specs=out_specs, check_vma=False)
```

```python
import functools

import jax
import jax.numpy as jnp
import numpy as np
from jax import lax
from jax.experimental import pallas as pl
from jax.experimental.pallas import tpu as pltpu
from jax.sharding import PartitionSpec as P

F32 = jnp.float32
BF16 = jnp.bfloat16
QUARTERS = 4
HALVES = 2
GROUP = QUARTERS * HALVES
DISTANCES = (4, 2, 1, 7, 3, 5, 6)
LANES = 128
LOG2E = 1.4426950408889634
FAR = -1e30
VMEM = pl.BlockSpec(memory_space=pltpu.VMEM)
SMEM = pl.BlockSpec(memory_space=pltpu.SMEM)
ANY = pl.BlockSpec(memory_space=pl.ANY)
INNER_AFTER = 2


def iota(shape, axis):
    return lax.broadcasted_iota(jnp.int32, shape, axis)


def matmul(left, right):
    return lax.dot_general(left, right, (((1,), (0,)), ((), ())), preferred_element_type=F32)


def matmul_nt(left, right):
    return lax.dot_general(left, right, (((1,), (1,)), ((), ())), preferred_element_type=F32)


def split2(value):
    high = value.astype(BF16)
    return high, (value - high.astype(F32)).astype(BF16)


def split3(value):
    high = value.astype(BF16)
    rest = value - high.astype(F32)
    middle = rest.astype(BF16)
    return high, middle, (rest - middle.astype(F32)).astype(BF16)


def column(row):
    count = row.shape[1]
    eye = iota((count, count), 0) == iota((count, count), 1)
    return jnp.sum(jnp.where(eye, row, 0.0), axis=1, keepdims=True)


def stacked_columns(rows):
    parts = [part.astype(F32) for part in split3(rows)]
    spare = LANES - 3 * rows.shape[0]
    if spare:
        parts.append(jnp.zeros((spare, rows.shape[1]), F32))
    return jnp.concatenate(parts, axis=0).T.astype(BF16)


def spread_table(heads, head_dim):
    table = np.zeros((LANES, heads * head_dim), np.float32)
    for head in range(heads):
        for part in range(3):
            table[part * heads + head, head * head_dim : (head + 1) * head_dim] = 1.0
    return jnp.asarray(table, BF16)


def softplus(value):
    return jnp.maximum(value, 0.0) + jnp.log1p(jnp.exp(-jnp.abs(value)))


def document_at(starts_ref, position):
    total = jnp.zeros_like(position)
    for entry in range(starts_ref.shape[1]):
        total = total + (starts_ref[0, entry] <= position).astype(jnp.int32)
    return total


def group_place():
    return lax.rem(lax.axis_index("ctx"), GROUP)


def share_out(own, quarter_of_state, places, scratch):
    mine = lax.div(own, QUARTERS)
    part = scratch.shape[0] // HALVES
    for distance in range(QUARTERS):
        scratch[...] = quarter_of_state(lax.rem(own ^ distance, QUARTERS))
        for half in range(HALVES):
            rows = pl.ds(pl.multiple_of((mine ^ half) * part, part), part)
            places[half * QUARTERS + distance][...] = scratch[rows]


def states_kernel(starts, logits, bias, decay, spread_ref, features, writes, cotangent, reads, *refs):
    sends = refs[:GROUP]
    weight_cols, factor_cols, cum_cols, cum_rows, stride_out, log_out, scratch = refs[GROUP:]
    heads, length = logits.shape
    state = writes.shape[1]
    width = features.shape[1] // QUARTERS
    part = state // HALVES
    first = lax.axis_index("ctx") * length
    own = group_place()
    stride = softplus(logits[...] + column(bias[...]))
    log_decay = stride * column(-jnp.exp(decay[...]))
    upto = jnp.where(iota((length, length), 0) <= iota((length, length), 1), 1.0, 0.0).astype(BF16)
    parts = matmul(jnp.concatenate(split3(log_decay), axis=0), upto)
    cum = parts[:heads] + parts[heads : 2 * heads] + parts[2 * heads :]
    segment = document_at(starts, first + iota((1, length), 1))
    entry = document_at(starts, jnp.full((1, 1), first - 1, jnp.int32))
    leave = document_at(starts, jnp.full((1, 1), first + length - 1, jnp.int32))
    own_last = jnp.where(segment == leave, 1.0, 0.0)
    keep_in = jnp.where(segment == entry, 1.0, 0.0)
    weight_stack = stacked_columns(own_last * jnp.exp(cum[:, length - 1 :] - cum) * stride)
    factor_stack = stacked_columns(keep_in * jnp.exp(cum))
    write_t = writes[...].astype(F32).T.astype(BF16)

    def quarter_of_state(quarter):
        cols = pl.ds(pl.multiple_of(quarter * width, LANES), width)
        high, low = split2(features[:, cols].astype(F32) * matmul(weight_stack, spread_ref[:, cols]))
        return matmul(write_t, high) + matmul(write_t, low)

    share_out(own, quarter_of_state, [send.at[0:part] for send in sends], scratch)
    read_t = reads[...].astype(F32).T.astype(BF16)

    keeps = []

    def back_quarter(quarter):
        cols = pl.ds(pl.multiple_of(quarter * width, LANES), width)
        wide = matmul(factor_stack, spread_ref[:, cols])
        keeps.append(jnp.broadcast_to(wide[length - 1 :], (8, width)))
        high, low = split2(cotangent[:, cols].astype(F32) * wide)
        return matmul(read_t, high) + matmul(read_t, low)

    share_out(own, back_quarter, [send.at[part + 8 :] for send in sends], scratch)
    for distance, send in enumerate(sends):
        send[part : part + 8] = keeps[distance % QUARTERS]
    weight_cols[...] = weight_stack
    factor_cols[...] = factor_stack
    cum_cols[...] = stacked_columns(cum * LOG2E)
    cum_rows[...] = cum * LOG2E - jnp.log2(stride)
    stride_out[...] = stride
    log_out[...] = log_decay


def inner_kernel(
    starts, cum_cols, cum_rows, features, cotangent, writes, reads, weight_cols, factor_cols, spread_ref, *refs
):
    refs = refs[INNER_AFTER:]
    inside, feature_part, skip_part, write_part, read_part, write_high, write_low, read_high, read_low = refs[:9]
    scores_ref, mask_ref, grad_ref = refs[9:]
    length, width = features.shape
    heads = cum_rows.shape[0]
    here = heads // QUARTERS
    head_dim = width // here
    pair = 2 * head_dim
    step = pl.program_id(0)

    @pl.when(step == 0)
    def _():
        first = lax.axis_index("ctx") * length
        segment_row = document_at(starts, first + iota((1, length), 1))
        segment_col = document_at(starts, first + iota((length, 1), 0))
        causal = iota((length, length), 0) >= iota((length, length), 1)
        mask_ref[...] = jnp.where((segment_row == segment_col) & causal, 0.0, FAR)
        scores_ref[...] = matmul_nt(reads[...], writes[...])
        grad_ref[...] = jnp.zeros_like(grad_ref)

    write_high[...], write_low[...] = split2(matmul(weight_cols[...], spread_ref[...]) * features[...].astype(F32))
    read_high[...], read_low[...] = split2(matmul(factor_cols[...], spread_ref[...]) * cotangent[...].astype(F32))

    def one_pair(at, carry):
        cols = pl.ds(pl.multiple_of(at * pair, LANES), pair)
        feature = features[:, cols]
        grad = cotangent[:, cols]
        grad_f32 = grad.astype(F32)
        grad_t = grad_f32.T.astype(BF16)
        skip_part[:, cols] = jnp.sum(grad_f32 * feature.astype(F32), axis=0, keepdims=True)
        head = step * here + at * 2
        lane = iota((LANES, 2 * LANES), 0)
        wanted = head + lax.div(iota((LANES, 2 * LANES), 1), LANES)
        pick = (lane == wanted) | (lane == wanted + heads) | (lane == wanted + 2 * heads)
        upper = matmul(cum_cols[...], jnp.where(pick, 1.0, 0.0).astype(BF16))
        second = iota((LANES, pair), 1) >= head_dim
        back = [None, None]
        for block in range(length // LANES):
            rows = slice(block * LANES, (block + 1) * LANES)
            reach = (block + 1) * LANES
            values = []
            for side in range(2):
                high_row = jnp.concatenate([upper[rows, side * LANES : (side + 1) * LANES]] * (block + 1), axis=1)
                low_row = cum_rows[pl.ds(head + side, 1), :][:, 0:reach]
                weight = jnp.exp2(high_row - low_row + mask_ref[rows, 0:reach])
                high, low = split2(weight * scores_ref[rows, 0:reach])
                values.append(matmul(high, feature[0:reach]) + matmul(low, feature[0:reach]))
                grad_rows = grad_t[side * head_dim : (side + 1) * head_dim, rows]
                found = matmul(grad_rows, high) + matmul(grad_rows, low)
                if block:
                    found = jnp.concatenate([found[:, : reach - LANES] + back[side], found[:, reach - LANES :]], axis=1)
                back[side] = found
                only = jnp.where(second == (side == 1), grad_f32[rows], 0.0).astype(BF16)
                grad_ref[rows, 0:reach] += matmul_nt(only, feature[0:reach]) * weight
            inside[rows, cols] = jnp.where(second, values[1], values[0])
        feature_part[:, cols] = jnp.concatenate(back, axis=0).T
        return carry

    lax.fori_loop(0, here // 2, one_pair, 0)

    @pl.when(step == QUARTERS - 1)
    def _():
        score_grad = grad_ref[...]
        high, low = split2(score_grad)
        read_part[...] = matmul(high, writes[...]) + matmul(low, writes[...])
        high, low = split2(score_grad.T)
        write_part[...] = matmul(high, reads[...]) + matmul(low, reads[...])


def in_order(refs, scratch, back=False):
    own = group_place()
    rows = scratch.shape[1]
    for distance, ref in enumerate(refs):
        first = ref.shape[0] - rows if back else 0
        scratch[own ^ distance] = ref[first : first + rows]


def group_kernel(part, *refs):
    up, down, keeps, came, back_came = refs[-5:]
    in_order(refs[:GROUP], came)
    total = came[0, 0:part]
    keep = came[0, part:]
    for j in range(1, GROUP):
        total = total * came[j, part : part + 1] + came[j, 0:part]
        keep = keep * came[j, part:]
    up[0:part] = total
    up[part:] = keep
    for j in range(GROUP):
        keeps[j : j + 1] = came[j, part : part + 1]
    in_order(refs[:GROUP], back_came, back=True)
    total = back_came[GROUP - 1]
    for j in reversed(range(GROUP - 1)):
        total = total * keeps[j : j + 1] + back_came[j]
    down[0:part] = total
    down[part:] = keep


def arrived(part, came):
    total, keep = came[0][0:part], came[0][part : part + 1]
    for ref in came[1:]:
        total = total + keep * ref[0:part]
        keep = keep * ref[part : part + 1]
    return total, keep


def link_kernel(part, own, *refs):
    total, keep = arrived(part, refs[:-1])
    refs[-1][0:part] = own[0:part] + own[part : part + 1] * total
    refs[-1][part:] = own[part:] * keep


def spread_kernel(part, count, *refs):
    ups, downs = refs[GROUP : GROUP + count], refs[GROUP + count : GROUP + 2 * count]
    keeps = refs[GROUP + 2 * count]
    outs = refs[GROUP + 2 * count + 1 : -3]
    came, back_came, give = refs[-3:]
    in_order(refs[:GROUP], came)
    total = arrived(part, ups)[0]
    for j in range(GROUP):
        give[j, 0:part] = total
        if j < GROUP - 1:
            total = total * keeps[j : j + 1] + came[j, 0:part]
    in_order(refs[:GROUP], back_came, back=True)
    total = arrived(part, downs)[0]
    for j in reversed(range(GROUP)):
        give[j, part:] = total
        if j > 0:
            total = total * keeps[j : j + 1] + back_came[j]
    own = group_place()
    for distance, out in enumerate(outs):
        out[...] = give[own ^ distance]


def head_sums(ref, value, spread):
    high, low = split2(value)
    ref[...] += matmul_nt(high, spread) + matmul_nt(low, spread)


def wide_skip(skip, heads, spread):
    stack = stacked_columns(jnp.broadcast_to(column(skip[...]), (heads, LANES)))
    return matmul(stack[0:16], spread)[0:1]


def quarter_rows(have, step, back):
    part = have.shape[1] // 2
    return jnp.concatenate([have[half * QUARTERS + step, back * part : (back + 1) * part] for half in range(HALVES)], axis=0)


def finish_kernel(
    logits, bias, decay, skip, weight_cols, factor_cols, stride_ref, log_ref, spread_ref,
    features, cotangent, writes, reads, inside, feature_part, skip_part, *refs,
):
    haves = refs[:GROUP]
    mixed, feature_grad, step_grad, sums, row_acc, col_acc, last_acc, skip_acc, have = refs[GROUP:]
    heads, length = logits.shape
    state = writes.shape[1]
    width = features.shape[1]
    step = pl.program_id(0)

    @pl.when(step == 0)
    def _():
        for ref in (row_acc, col_acc, last_acc, skip_acc):
            ref[...] = jnp.zeros_like(ref)
        in_order(haves, have)

    spread = spread_ref[...]
    skips = wide_skip(skip, heads, spread)
    feature = features[...].astype(F32)
    grad = cotangent[...].astype(F32)
    factor = matmul(factor_cols[...], spread)
    entering = quarter_rows(have, step, 0)
    stack = jnp.concatenate(split2(entering), axis=0)
    total = inside[...] + factor * matmul(jnp.concatenate([reads[...]] * 2, axis=1), stack)
    mixed[...] = (total + skips * feature).astype(BF16)
    head_sums(row_acc, grad * total, spread)
    returning = quarter_rows(have, step, 1)
    stack = jnp.concatenate(split2(returning), axis=0)
    carried = matmul(weight_cols[...], spread) * matmul(jnp.concatenate([writes[...]] * 2, axis=1), stack)
    total = feature_part[...] + carried
    feature_grad[...] = (total + skips * grad).astype(BF16)
    head_sums(col_acc, feature * total, spread)
    leaving = jnp.sum((returning * entering).reshape(state // 8, 8, width), axis=0) * factor[length - 1 :]
    leaving = leaving + jnp.sum((feature * carried).reshape(length // 8, 8, width), axis=0)
    head_sums(last_acc, leaving, spread)
    head_sums(skip_acc, jnp.broadcast_to(skip_part[...], (8, width)), spread)

    @pl.when(step == QUARTERS - 1)
    def _():
        rows = row_acc[...].T[:heads]
        cols = col_acc[...].T[:heads]
        last = column(jnp.sum(last_acc[...], axis=0, keepdims=True))[:heads]
        stride = stride_ref[...]
        gap_grad = rows - cols + jnp.where(iota((heads, length), 1) == length - 1, last, 0.0)
        onward = jnp.where(iota((length, length), 0) >= iota((length, length), 1), 1.0, 0.0).astype(BF16)
        parts = matmul(jnp.concatenate(split3(gap_grad), axis=0), onward)
        log_grad = parts[:heads] + parts[heads : 2 * heads] + parts[2 * heads :]
        rate = column(-jnp.exp(decay[...]))
        slope = 1.0 / (1.0 + jnp.exp(-(logits[...] + column(bias[...]))))
        step_value = (cols / stride + rate * log_grad) * slope
        step_grad[...] = step_value
        bias_sum = jnp.sum(step_value, axis=1, keepdims=True)
        decay_sum = jnp.sum(log_grad * log_ref[...], axis=1, keepdims=True)
        skip_sum = column(skip_acc[0:1])[:heads]
        spare = jnp.zeros((LANES - 3 * heads, 1), F32)
        table = jnp.concatenate([bias_sum, decay_sum, skip_sum, spare], axis=0)
        eye = iota((LANES, LANES), 0) == iota((LANES, LANES), 1)
        table = jnp.sum(jnp.where(eye, table, 0.0), axis=0, keepdims=True)
        sums[...] = jnp.broadcast_to(table[None], sums.shape)


def keys_kernel(write_part, read_part, write_high, write_low, read_high, read_low, *refs):
    write_grad, read_grad, write_acc, read_acc, have = refs[GROUP + 1 :]
    state = write_part.shape[1]
    step = pl.program_id(0)

    @pl.when(step == 0)
    def _():
        write_acc[...] = jnp.zeros_like(write_acc)
        read_acc[...] = jnp.zeros_like(read_acc)
        in_order(refs[:GROUP], have)

    for back, high, low, acc in ((0, read_high, read_low, read_acc), (1, write_high, write_low, write_acc)):
        stack = jnp.concatenate(split2(quarter_rows(have, step, back)), axis=0)
        acc[...] += matmul_nt(high[...], stack) + matmul_nt(low[...], stack)

    @pl.when(step == QUARTERS - 1)
    def _():
        write_grad[...] = (write_part[...] + write_acc[:, :state] + write_acc[:, state:]).astype(BF16)
        read_grad[...] = (read_part[...] + read_acc[:, :state] + read_acc[:, state:]).astype(BF16)


def call(kernel, name, outs, in_specs, work, mib, **more):
    return pl.pallas_call(
        kernel,
        out_shape=outs,
        in_specs=in_specs,
        out_specs=more.pop("out_specs", [VMEM] * len(outs)),
        compiler_params=pltpu.CompilerParams(vmem_limit_bytes=mib * 2**20),
        cost_estimate=pl.CostEstimate(flops=work * 10**9, bytes_accessed=10**6, transcendentals=0),
        name=name,
        **more,
    )


def struct(shape, dtype=F32):
    return jax.ShapeDtypeStruct(shape, dtype)


def local(
    features, write_keys, read_queries, step_logits, step_bias, decay_log, skip_gain, doc_starts, out_grad
):
    features, writes, reads, logits, cotangent = (
        features[0], write_keys[0], read_queries[0], step_logits[0], out_grad[0]
    )
    length, wide = features.shape
    heads = logits.shape[0]
    state = writes.shape[1]
    head_dim = wide // heads
    width = wide // QUARTERS
    part = state // HALVES
    bias, decay, skip = step_bias[None], decay_log[None], skip_gain[None]
    blocks, members = lax.axis_size("ctx"), lax.axis_size("dp")
    spread = spread_table(heads, head_dim)

    def exchange(value, distance):
        return lax.ppermute(value, "ctx", [(k, k ^ distance) for k in range(blocks)])

    def swap(values):
        came = {d: exchange(values[d], d) for d in DISTANCES}
        return [came.get(d, values[0]) for d in range(GROUP)]

    def shift(value, distance):
        pairs = [(k, k + distance) for k in range(blocks) if 0 <= k + distance < blocks]
        return lax.ppermute(value, "ctx", pairs)

    def scan(own, sign):
        came, near, reach = [], own, 1
        while reach < blocks // GROUP:
            came.append(shift(near, sign * GROUP * reach))
            reach *= 2
            if reach < blocks // GROUP:
                near = call(
                    functools.partial(link_kernel, part), "link", [group_sum], [VMEM] * (1 + len(came)), 1, 8
                )(own, *came)[0]
        return came

    def all_of(*shape):
        return pl.BlockSpec(shape, lambda step: (0,) * len(shape))

    def quarter_of(rows, offset=0):
        return pl.BlockSpec((rows, width), lambda step: (0, step + offset))

    stack = struct((length, LANES), BF16)
    small = struct((heads, length))
    result = struct((length, wide), BF16)
    tokens_result = struct((length, state), BF16)
    group_sum = struct((part + 8, width))
    tokens = all_of(length, state)
    columns = all_of(length, LANES)
    by_heads = all_of(heads, length)
    row = all_of(1, heads)
    by_quarter = quarter_of(length)
    spread_quarter = quarter_of(LANES)
    shares = pltpu.VMEM((GROUP, part, width), F32)
    long_shares = pltpu.VMEM((GROUP, part + 8, width), F32)
    both_shares = pltpu.VMEM((GROUP, 2 * part, width), F32)

    both = struct((2 * part + 8, width))
    out = call(
        states_kernel,
        "states",
        [both] * GROUP + [stack] * 3 + [small] * 3,
        [SMEM] + [VMEM] * 8,
        4,
        60,
        scratch_shapes=[pltpu.VMEM((state, width), F32)],
    )(doc_starts, logits, bias, decay, spread, features, writes, cotangent, reads)
    came = swap(out[:GROUP])
    weight_cols, factor_cols, cum_cols, cum_rows, stride, log_decay = out[GROUP:]

    wide_part, wide_piece = struct((length, wide)), struct((length, wide), BF16)
    inside, feature_part, skip_part, write_part, read_part, *pieces = call(
        inner_kernel,
        "inner",
        [wide_part] * 2 + [struct((1, wide))] + [struct((length, state))] * 2 + [wide_piece] * 4,
        [SMEM, columns, by_heads, by_quarter, by_quarter, tokens, tokens, columns, columns, spread_quarter]
        + [ANY] * INNER_AFTER,
        10,
        24,
        grid=(QUARTERS,),
        out_specs=[by_quarter, by_quarter, quarter_of(1), tokens, tokens] + [by_quarter] * 4,
        scratch_shapes=[pltpu.VMEM((length, length), F32)] * 3,
    )(
        doc_starts, cum_cols, cum_rows, features, cotangent, writes, reads, weight_cols, factor_cols, spread,
        *[came[d] for d in DISTANCES[:INNER_AFTER]],
    )
    up, down, keeps = call(
        functools.partial(group_kernel, part),
        "group",
        [group_sum, group_sum, struct((GROUP, width))],
        [VMEM] * GROUP + [ANY],
        2,
        12,
        scratch_shapes=[long_shares, shares],
    )(*came, write_part)
    ups, downs = scan(up, 1), scan(down, -1)
    give = call(
        functools.partial(spread_kernel, part, len(ups)),
        "spread",
        [struct((2 * part, width))] * GROUP,
        [VMEM] * (GROUP + 2 * len(ups) + 1),
        2,
        16,
        scratch_shapes=[long_shares, shares, both_shares],
    )(*came, *ups, *downs, keeps)
    have = swap(give)
    devices = blocks * members
    whole_shares = [all_of(2 * part, width)] * GROUP
    mixed, feature_grad, step_grad, sums = call(
        finish_kernel,
        "finish",
        [result, result, small, struct((devices, 1, LANES))],
        [by_heads, row, row, row, columns, columns, by_heads, by_heads, spread_quarter]
        + [by_quarter, by_quarter, tokens, tokens, by_quarter, by_quarter, quarter_of(1)]
        + whole_shares,
        8,
        24,
        grid=(QUARTERS,),
        out_specs=[by_quarter, by_quarter, by_heads, all_of(devices, 1, LANES)],
        scratch_shapes=[pltpu.VMEM((length, LANES), F32)] * 2 + [pltpu.VMEM((8, LANES), F32)] * 2 + [both_shares],
    )(
        logits, bias, decay, skip, weight_cols, factor_cols, stride, log_decay, spread,
        features, cotangent, writes, reads, inside, feature_part, skip_part, *have,
    )
    write_grad, read_grad = call(
        keys_kernel,
        "keys",
        [tokens_result] * 2,
        [tokens] * 2 + [by_quarter] * 4 + whole_shares + [ANY],
        6,
        60,
        grid=(QUARTERS,),
        out_specs=[tokens] * 2,
        scratch_shapes=[pltpu.VMEM((length, 2 * state), F32)] * 2 + [both_shares],
    )(write_part, read_part, *pieces, *have, step_grad)
    sums = jnp.sum(lax.all_to_all(sums, ("dp", "ctx"), 0, 0), axis=(0, 1))
    return (
        mixed[None],
        feature_grad[None],
        write_grad[None],
        read_grad[None],
        step_grad[None],
        sums[:heads],
        sums[heads : 2 * heads],
        sums[2 * heads : 3 * heads],
    )


def solution(mesh):
    by_tokens = P("dp", "ctx", None)
    by_heads = P("dp", None, "ctx")
    in_specs = (by_tokens, by_tokens, by_tokens, by_heads, P(), P(), P(), P("dp", None), by_tokens)
    out_specs = (by_tokens, by_tokens, by_tokens, by_tokens, by_heads, P(), P(), P())
    return jax.shard_map(local, mesh=mesh, in_specs=in_specs, out_specs=out_specs, check_vma=False)
```

```python
import functools

import jax
import jax.numpy as jnp
import numpy as np
from jax import lax
from jax.experimental import pallas as pl
from jax.experimental.pallas import tpu as pltpu
from jax.sharding import PartitionSpec as P

F32 = jnp.float32
BF16 = jnp.bfloat16
QUARTERS = 4
HALVES = 2
GROUP = QUARTERS * HALVES
DISTANCES = (1, 2, 3, 4, 5, 6, 7)
LANES = 128
LOG2E = 1.4426950408889634
FAR = -1e30
VMEM = pl.BlockSpec(memory_space=pltpu.VMEM)
SMEM = pl.BlockSpec(memory_space=pltpu.SMEM)
ANY = pl.BlockSpec(memory_space=pl.ANY)
INNER_AFTER = 2


def iota(shape, axis):
    return lax.broadcasted_iota(jnp.int32, shape, axis)


def matmul(left, right):
    return lax.dot_general(left, right, (((1,), (0,)), ((), ())), preferred_element_type=F32)


def matmul_nt(left, right):
    return lax.dot_general(left, right, (((1,), (1,)), ((), ())), preferred_element_type=F32)


def split2(value):
    high = value.astype(BF16)
    return high, (value - high.astype(F32)).astype(BF16)


def split3(value):
    high = value.astype(BF16)
    rest = value - high.astype(F32)
    middle = rest.astype(BF16)
    return high, middle, (rest - middle.astype(F32)).astype(BF16)


def column(row):
    count = row.shape[1]
    eye = iota((count, count), 0) == iota((count, count), 1)
    return jnp.sum(jnp.where(eye, row, 0.0), axis=1, keepdims=True)


def stacked_columns(rows):
    parts = [part.astype(F32) for part in split3(rows)]
    spare = LANES - 3 * rows.shape[0]
    if spare:
        parts.append(jnp.zeros((spare, rows.shape[1]), F32))
    return jnp.concatenate(parts, axis=0).T.astype(BF16)


def spread_table(heads, head_dim):
    table = np.zeros((LANES, heads * head_dim), np.float32)
    for head in range(heads):
        for part in range(3):
            table[part * heads + head, head * head_dim : (head + 1) * head_dim] = 1.0
    return jnp.asarray(table, BF16)


def softplus(value):
    return jnp.maximum(value, 0.0) + jnp.log1p(jnp.exp(-jnp.abs(value)))


def document_at(starts_ref, position):
    total = jnp.zeros_like(position)
    for entry in range(starts_ref.shape[1]):
        total = total + (starts_ref[0, entry] <= position).astype(jnp.int32)
    return total


def group_place():
    return lax.rem(lax.axis_index("ctx"), GROUP)


def share_out(own, quarter_of_state, places, scratch):
    mine = lax.div(own, QUARTERS)
    part = scratch.shape[0] // HALVES
    for distance in range(QUARTERS):
        scratch[...] = quarter_of_state(lax.rem(own ^ distance, QUARTERS))
        for half in range(HALVES):
            rows = pl.ds(pl.multiple_of((mine ^ half) * part, part), part)
            places[half * QUARTERS + distance][...] = scratch[rows]


def states_kernel(starts, logits, bias, decay, spread_ref, features, writes, cotangent, reads, *refs):
    sends = refs[:GROUP]
    weight_cols, factor_cols, cum_cols, cum_rows, stride_out, log_out, scratch = refs[GROUP:]
    heads, length = logits.shape
    state = writes.shape[1]
    width = features.shape[1] // QUARTERS
    part = state // HALVES
    first = lax.axis_index("ctx") * length
    own = group_place()
    stride = softplus(logits[...] + column(bias[...]))
    log_decay = stride * column(-jnp.exp(decay[...]))
    upto = jnp.where(iota((length, length), 0) <= iota((length, length), 1), 1.0, 0.0).astype(BF16)
    parts = matmul(jnp.concatenate(split3(log_decay), axis=0), upto)
    cum = parts[:heads] + parts[heads : 2 * heads] + parts[2 * heads :]
    segment = document_at(starts, first + iota((1, length), 1))
    entry = document_at(starts, jnp.full((1, 1), first - 1, jnp.int32))
    leave = document_at(starts, jnp.full((1, 1), first + length - 1, jnp.int32))
    own_last = jnp.where(segment == leave, 1.0, 0.0)
    keep_in = jnp.where(segment == entry, 1.0, 0.0)
    weight_stack = stacked_columns(own_last * jnp.exp(cum[:, length - 1 :] - cum) * stride)
    factor_stack = stacked_columns(keep_in * jnp.exp(cum))
    write_t = writes[...].astype(F32).T.astype(BF16)

    def quarter_of_state(quarter):
        cols = pl.ds(pl.multiple_of(quarter * width, LANES), width)
        high, low = split2(features[:, cols].astype(F32) * matmul(weight_stack, spread_ref[:, cols]))
        return matmul(write_t, high) + matmul(write_t, low)

    share_out(own, quarter_of_state, [send.at[0:part] for send in sends], scratch)
    read_t = reads[...].astype(F32).T.astype(BF16)

    keeps = []

    def back_quarter(quarter):
        cols = pl.ds(pl.multiple_of(quarter * width, LANES), width)
        wide = matmul(factor_stack, spread_ref[:, cols])
        keeps.append(jnp.broadcast_to(wide[length - 1 :], (8, width)))
        high, low = split2(cotangent[:, cols].astype(F32) * wide)
        return matmul(read_t, high) + matmul(read_t, low)

    share_out(own, back_quarter, [send.at[part + 8 :] for send in sends], scratch)
    for distance, send in enumerate(sends):
        send[part : part + 8] = keeps[distance % QUARTERS]
    weight_cols[...] = weight_stack
    factor_cols[...] = factor_stack
    cum_cols[...] = stacked_columns(cum * LOG2E)
    cum_rows[...] = cum * LOG2E - jnp.log2(stride)
    stride_out[...] = stride
    log_out[...] = log_decay


def inner_kernel(
    starts, cum_cols, cum_rows, features, cotangent, writes, reads, weight_cols, factor_cols, spread_ref, *refs
):
    refs = refs[INNER_AFTER:]
    inside, feature_part, skip_part, write_part, read_part, write_high, write_low, read_high, read_low = refs[:9]
    scores_ref, mask_ref, grad_ref = refs[9:]
    length, width = features.shape
    heads = cum_rows.shape[0]
    here = heads // QUARTERS
    head_dim = width // here
    pair = 2 * head_dim
    step = pl.program_id(0)

    @pl.when(step == 0)
    def _():
        first = lax.axis_index("ctx") * length
        segment_row = document_at(starts, first + iota((1, length), 1))
        segment_col = document_at(starts, first + iota((length, 1), 0))
        causal = iota((length, length), 0) >= iota((length, length), 1)
        mask_ref[...] = jnp.where((segment_row == segment_col) & causal, 0.0, FAR)
        scores_ref[...] = matmul_nt(reads[...], writes[...])
        grad_ref[...] = jnp.zeros_like(grad_ref)

    write_high[...], write_low[...] = split2(matmul(weight_cols[...], spread_ref[...]) * features[...].astype(F32))
    read_high[...], read_low[...] = split2(matmul(factor_cols[...], spread_ref[...]) * cotangent[...].astype(F32))

    def one_pair(at, carry):
        cols = pl.ds(pl.multiple_of(at * pair, LANES), pair)
        feature = features[:, cols]
        grad = cotangent[:, cols]
        grad_f32 = grad.astype(F32)
        grad_t = grad_f32.T.astype(BF16)
        skip_part[:, cols] = jnp.sum(grad_f32 * feature.astype(F32), axis=0, keepdims=True)
        head = step * here + at * 2
        lane = iota((LANES, 2 * LANES), 0)
        wanted = head + lax.div(iota((LANES, 2 * LANES), 1), LANES)
        pick = (lane == wanted) | (lane == wanted + heads) | (lane == wanted + 2 * heads)
        upper = matmul(cum_cols[...], jnp.where(pick, 1.0, 0.0).astype(BF16))
        second = iota((LANES, pair), 1) >= head_dim
        back = [None, None]
        for block in range(length // LANES):
            rows = slice(block * LANES, (block + 1) * LANES)
            reach = (block + 1) * LANES
            values = []
            for side in range(2):
                high_row = jnp.concatenate([upper[rows, side * LANES : (side + 1) * LANES]] * (block + 1), axis=1)
                low_row = cum_rows[pl.ds(head + side, 1), :][:, 0:reach]
                weight = jnp.exp2(high_row - low_row + mask_ref[rows, 0:reach])
                high, low = split2(weight * scores_ref[rows, 0:reach])
                values.append(matmul(high, feature[0:reach]) + matmul(low, feature[0:reach]))
                grad_rows = grad_t[side * head_dim : (side + 1) * head_dim, rows]
                found = matmul(grad_rows, high) + matmul(grad_rows, low)
                if block:
                    found = jnp.concatenate([found[:, : reach - LANES] + back[side], found[:, reach - LANES :]], axis=1)
                back[side] = found
                only = jnp.where(second == (side == 1), grad_f32[rows], 0.0).astype(BF16)
                grad_ref[rows, 0:reach] += matmul_nt(only, feature[0:reach]) * weight
            inside[rows, cols] = jnp.where(second, values[1], values[0])
        feature_part[:, cols] = jnp.concatenate(back, axis=0).T
        return carry

    lax.fori_loop(0, here // 2, one_pair, 0)

    @pl.when(step == QUARTERS - 1)
    def _():
        score_grad = grad_ref[...]
        high, low = split2(score_grad)
        read_part[...] = matmul(high, writes[...]) + matmul(low, writes[...])
        high, low = split2(score_grad.T)
        write_part[...] = matmul(high, reads[...]) + matmul(low, reads[...])


def in_order(refs, scratch, back=False):
    own = group_place()
    rows = scratch.shape[1]
    for distance, ref in enumerate(refs):
        first = ref.shape[0] - rows if back else 0
        scratch[own ^ distance] = ref[first : first + rows]


def group_kernel(part, *refs):
    keeps, came, back_came = refs[-3:]
    sums = refs[GROUP + 1 : -3]
    up, down = sums[0], sums[-1]
    in_order(refs[:GROUP], came)
    total = came[0, 0:part]
    keep = came[0, part:]
    for j in range(1, GROUP):
        total = total * came[j, part : part + 1] + came[j, 0:part]
        keep = keep * came[j, part:]
    up[0:part] = total
    up[part:] = keep
    for j in range(GROUP):
        keeps[j : j + 1] = came[j, part : part + 1]
    in_order(refs[:GROUP], back_came, back=True)

    def downward():
        total = back_came[GROUP - 1]
        for j in reversed(range(GROUP - 1)):
            total = total * keeps[j : j + 1] + back_came[j]
        down[0:part] = total
        down[part:] = keep

    if len(sums) == 1:
        pl.when(lax.axis_index("ctx") >= GROUP)(downward)
    else:
        downward()


def arrived(part, came):
    total, keep = came[0][0:part], came[0][part : part + 1]
    for ref in came[1:]:
        total = total + keep * ref[0:part]
        keep = keep * ref[part : part + 1]
    return total, keep


def link_kernel(part, own, *refs):
    total, keep = arrived(part, refs[:-1])
    refs[-1][0:part] = own[0:part] + own[part : part + 1] * total
    refs[-1][part:] = own[part:] * keep


def spread_kernel(part, count, back_count, *refs):
    ups, downs = refs[GROUP : GROUP + count], refs[GROUP + count : GROUP + count + back_count]
    keeps = refs[GROUP + count + back_count]
    outs = refs[GROUP + count + back_count + 1 : -3]
    came, back_came, give = refs[-3:]
    in_order(refs[:GROUP], came)
    if downs:
        entering, returning = arrived(part, ups)[0], arrived(part, downs)[0]
    else:
        upper = jnp.full((1, 1), lax.axis_index("ctx")) >= GROUP
        entering = jnp.where(upper, ups[0][0:part], 0.0)
        returning = jnp.where(upper, 0.0, ups[0][0:part])
    total = entering
    for j in range(GROUP):
        give[j, 0:part] = total
        if j < GROUP - 1:
            total = total * keeps[j : j + 1] + came[j, 0:part]
    in_order(refs[:GROUP], back_came, back=True)
    total = returning
    for j in reversed(range(GROUP)):
        give[j, part:] = total
        if j > 0:
            total = total * keeps[j : j + 1] + back_came[j]
    own = group_place()
    for distance, out in enumerate(outs):
        out[...] = give[own ^ distance]


def head_sums(ref, value, spread):
    high, low = split2(value)
    ref[...] += matmul_nt(high, spread) + matmul_nt(low, spread)


def wide_skip(skip, heads, spread):
    stack = stacked_columns(jnp.broadcast_to(column(skip[...]), (heads, LANES)))
    return matmul(stack[0:16], spread)[0:1]


def quarter_rows(have, step, back):
    part = have.shape[1] // 2
    return jnp.concatenate([have[half * QUARTERS + step, back * part : (back + 1) * part] for half in range(HALVES)], axis=0)


def finish_kernel(
    logits, bias, decay, skip, weight_cols, factor_cols, stride_ref, log_ref, spread_ref,
    features, cotangent, writes, reads, inside, feature_part, skip_part, *refs,
):
    haves = refs[:GROUP]
    mixed, feature_grad, step_grad, sums, row_acc, col_acc, last_acc, skip_acc, have = refs[GROUP:]
    heads, length = logits.shape
    state = writes.shape[1]
    width = features.shape[1]
    step = pl.program_id(0)

    @pl.when(step == 0)
    def _():
        for ref in (row_acc, col_acc, last_acc, skip_acc):
            ref[...] = jnp.zeros_like(ref)
        in_order(haves, have)

    spread = spread_ref[...]
    skips = wide_skip(skip, heads, spread)
    feature = features[...].astype(F32)
    grad = cotangent[...].astype(F32)
    factor = matmul(factor_cols[...], spread)
    entering = quarter_rows(have, step, 0)
    stack = jnp.concatenate(split2(entering), axis=0)
    total = inside[...] + factor * matmul(jnp.concatenate([reads[...]] * 2, axis=1), stack)
    mixed[...] = (total + skips * feature).astype(BF16)
    head_sums(row_acc, grad * total, spread)
    returning = quarter_rows(have, step, 1)
    stack = jnp.concatenate(split2(returning), axis=0)
    carried = matmul(weight_cols[...], spread) * matmul(jnp.concatenate([writes[...]] * 2, axis=1), stack)
    total = feature_part[...] + carried
    feature_grad[...] = (total + skips * grad).astype(BF16)
    head_sums(col_acc, feature * total, spread)
    leaving = jnp.sum((returning * entering).reshape(state // 8, 8, width), axis=0) * factor[length - 1 :]
    leaving = leaving + jnp.sum((feature * carried).reshape(length // 8, 8, width), axis=0)
    head_sums(last_acc, leaving, spread)
    head_sums(skip_acc, jnp.broadcast_to(skip_part[...], (8, width)), spread)

    @pl.when(step == QUARTERS - 1)
    def _():
        rows = row_acc[...].T[:heads]
        cols = col_acc[...].T[:heads]
        last = column(jnp.sum(last_acc[...], axis=0, keepdims=True))[:heads]
        stride = stride_ref[...]
        gap_grad = rows - cols + jnp.where(iota((heads, length), 1) == length - 1, last, 0.0)
        onward = jnp.where(iota((length, length), 0) >= iota((length, length), 1), 1.0, 0.0).astype(BF16)
        parts = matmul(jnp.concatenate(split3(gap_grad), axis=0), onward)
        log_grad = parts[:heads] + parts[heads : 2 * heads] + parts[2 * heads :]
        rate = column(-jnp.exp(decay[...]))
        slope = 1.0 / (1.0 + jnp.exp(-(logits[...] + column(bias[...]))))
        step_value = (cols / stride + rate * log_grad) * slope
        step_grad[...] = step_value
        bias_sum = jnp.sum(step_value, axis=1, keepdims=True)
        decay_sum = jnp.sum(log_grad * log_ref[...], axis=1, keepdims=True)
        skip_sum = column(skip_acc[0:1])[:heads]
        spare = jnp.zeros((LANES - 3 * heads, 1), F32)
        table = jnp.concatenate([bias_sum, decay_sum, skip_sum, spare], axis=0)
        eye = iota((LANES, LANES), 0) == iota((LANES, LANES), 1)
        table = jnp.sum(jnp.where(eye, table, 0.0), axis=0, keepdims=True)
        sums[...] = jnp.broadcast_to(table[None], sums.shape)


def keys_kernel(write_part, read_part, write_high, write_low, read_high, read_low, *refs):
    write_grad, read_grad, write_acc, read_acc, have = refs[GROUP + 1 :]
    state = write_part.shape[1]
    step = pl.program_id(0)

    @pl.when(step == 0)
    def _():
        write_acc[...] = jnp.zeros_like(write_acc)
        read_acc[...] = jnp.zeros_like(read_acc)
        in_order(refs[:GROUP], have)

    for back, high, low, acc in ((0, read_high, read_low, read_acc), (1, write_high, write_low, write_acc)):
        stack = jnp.concatenate(split2(quarter_rows(have, step, back)), axis=0)
        acc[...] += matmul_nt(high[...], stack) + matmul_nt(low[...], stack)

    @pl.when(step == QUARTERS - 1)
    def _():
        write_grad[...] = (write_part[...] + write_acc[:, :state] + write_acc[:, state:]).astype(BF16)
        read_grad[...] = (read_part[...] + read_acc[:, :state] + read_acc[:, state:]).astype(BF16)


def call(kernel, name, outs, in_specs, work, mib, **more):
    return pl.pallas_call(
        kernel,
        out_shape=outs,
        in_specs=in_specs,
        out_specs=more.pop("out_specs", [VMEM] * len(outs)),
        compiler_params=pltpu.CompilerParams(vmem_limit_bytes=mib * 2**20),
        cost_estimate=pl.CostEstimate(flops=work * 10**9, bytes_accessed=10**6, transcendentals=0),
        name=name,
        **more,
    )


def struct(shape, dtype=F32):
    return jax.ShapeDtypeStruct(shape, dtype)


def local(
    features, write_keys, read_queries, step_logits, step_bias, decay_log, skip_gain, doc_starts, out_grad
):
    features, writes, reads, logits, cotangent = (
        features[0], write_keys[0], read_queries[0], step_logits[0], out_grad[0]
    )
    length, wide = features.shape
    heads = logits.shape[0]
    state = writes.shape[1]
    head_dim = wide // heads
    width = wide // QUARTERS
    part = state // HALVES
    bias, decay, skip = step_bias[None], decay_log[None], skip_gain[None]
    blocks, members = lax.axis_size("ctx"), lax.axis_size("dp")
    spread = spread_table(heads, head_dim)

    def exchange(value, distance):
        return lax.ppermute(value, "ctx", [(k, k ^ distance) for k in range(blocks)])

    def swap(values):
        came = {d: exchange(values[d], d) for d in DISTANCES}
        return [came.get(d, values[0]) for d in range(GROUP)]

    def shift(value, distance):
        pairs = [(k, k + distance) for k in range(blocks) if 0 <= k + distance < blocks]
        return lax.ppermute(value, "ctx", pairs)

    def scan(own, sign):
        came, near, reach = [], own, 1
        while reach < blocks // GROUP:
            came.append(shift(near, sign * GROUP * reach))
            reach *= 2
            if reach < blocks // GROUP:
                near = call(
                    functools.partial(link_kernel, part), "link", [group_sum], [VMEM] * (1 + len(came)), 1, 8
                )(own, *came)[0]
        return came

    def all_of(*shape):
        return pl.BlockSpec(shape, lambda step: (0,) * len(shape))

    def quarter_of(rows, offset=0):
        return pl.BlockSpec((rows, width), lambda step: (0, step + offset))

    stack = struct((length, LANES), BF16)
    small = struct((heads, length))
    result = struct((length, wide), BF16)
    tokens_result = struct((length, state), BF16)
    group_sum = struct((part + 8, width))
    tokens = all_of(length, state)
    columns = all_of(length, LANES)
    by_heads = all_of(heads, length)
    row = all_of(1, heads)
    by_quarter = quarter_of(length)
    spread_quarter = quarter_of(LANES)
    shares = pltpu.VMEM((GROUP, part, width), F32)
    long_shares = pltpu.VMEM((GROUP, part + 8, width), F32)
    both_shares = pltpu.VMEM((GROUP, 2 * part, width), F32)

    both = struct((2 * part + 8, width))
    out = call(
        states_kernel,
        "states",
        [both] * GROUP + [stack] * 3 + [small] * 3,
        [SMEM] + [VMEM] * 8,
        4,
        60,
        scratch_shapes=[pltpu.VMEM((state, width), F32)],
    )(doc_starts, logits, bias, decay, spread, features, writes, cotangent, reads)
    came = swap(out[:GROUP])
    weight_cols, factor_cols, cum_cols, cum_rows, stride, log_decay = out[GROUP:]

    wide_part, wide_piece = struct((length, wide)), struct((length, wide), BF16)
    inside, feature_part, skip_part, write_part, read_part, *pieces = call(
        inner_kernel,
        "inner",
        [wide_part] * 2 + [struct((1, wide))] + [struct((length, state))] * 2 + [wide_piece] * 4,
        [SMEM, columns, by_heads, by_quarter, by_quarter, tokens, tokens, columns, columns, spread_quarter]
        + [ANY] * INNER_AFTER,
        10,
        24,
        grid=(QUARTERS,),
        out_specs=[by_quarter, by_quarter, quarter_of(1), tokens, tokens] + [by_quarter] * 4,
        scratch_shapes=[pltpu.VMEM((length, length), F32)] * 3,
    )(
        doc_starts, cum_cols, cum_rows, features, cotangent, writes, reads, weight_cols, factor_cols, spread,
        *[came[d] for d in DISTANCES[:INNER_AFTER]],
    )
    two = blocks == 2 * GROUP
    *sums, keeps = call(
        functools.partial(group_kernel, part),
        "group",
        [group_sum] * (1 if two else 2) + [struct((GROUP, width))],
        [VMEM] * GROUP + [ANY],
        2,
        12,
        scratch_shapes=[long_shares, shares],
    )(*came, write_part)
    if two:
        ups, downs = [exchange(sums[0], GROUP)], []
    else:
        ups, downs = scan(sums[0], 1), scan(sums[1], -1)
    give = call(
        functools.partial(spread_kernel, part, len(ups), len(downs)),
        "spread",
        [struct((2 * part, width))] * GROUP,
        [VMEM] * (GROUP + len(ups) + len(downs) + 1),
        2,
        16,
        scratch_shapes=[long_shares, shares, both_shares],
    )(*came, *ups, *downs, keeps)
    have = swap(give)
    devices = blocks * members
    whole_shares = [all_of(2 * part, width)] * GROUP
    mixed, feature_grad, step_grad, sums = call(
        finish_kernel,
        "finish",
        [result, result, small, struct((devices, 1, LANES))],
        [by_heads, row, row, row, columns, columns, by_heads, by_heads, spread_quarter]
        + [by_quarter, by_quarter, tokens, tokens, by_quarter, by_quarter, quarter_of(1)]
        + whole_shares,
        8,
        24,
        grid=(QUARTERS,),
        out_specs=[by_quarter, by_quarter, by_heads, all_of(devices, 1, LANES)],
        scratch_shapes=[pltpu.VMEM((length, LANES), F32)] * 2 + [pltpu.VMEM((8, LANES), F32)] * 2 + [both_shares],
    )(
        logits, bias, decay, skip, weight_cols, factor_cols, stride, log_decay, spread,
        features, cotangent, writes, reads, inside, feature_part, skip_part, *have,
    )
    write_grad, read_grad = call(
        keys_kernel,
        "keys",
        [tokens_result] * 2,
        [tokens] * 2 + [by_quarter] * 4 + whole_shares + [ANY],
        6,
        60,
        grid=(QUARTERS,),
        out_specs=[tokens] * 2,
        scratch_shapes=[pltpu.VMEM((length, 2 * state), F32)] * 2 + [both_shares],
    )(write_part, read_part, *pieces, *have, step_grad)
    sums = jnp.sum(lax.all_to_all(sums, ("dp", "ctx"), 0, 0), axis=(0, 1))
    return (
        mixed[None],
        feature_grad[None],
        write_grad[None],
        read_grad[None],
        step_grad[None],
        sums[:heads],
        sums[heads : 2 * heads],
        sums[2 * heads : 3 * heads],
    )


def solution(mesh):
    by_tokens = P("dp", "ctx", None)
    by_heads = P("dp", None, "ctx")
    in_specs = (by_tokens, by_tokens, by_tokens, by_heads, P(), P(), P(), P("dp", None), by_tokens)
    out_specs = (by_tokens, by_tokens, by_tokens, by_tokens, by_heads, P(), P(), P())
    return jax.shard_map(local, mesh=mesh, in_specs=in_specs, out_specs=out_specs, check_vma=False)
```

```python
import functools

import jax
import jax.numpy as jnp
import numpy as np
from jax import lax
from jax.experimental import pallas as pl
from jax.experimental.pallas import tpu as pltpu
from jax.sharding import PartitionSpec as P

F32 = jnp.float32
BF16 = jnp.bfloat16
QUARTERS = 4
HALVES = 2
GROUP = QUARTERS * HALVES
DISTANCES = (1, 2, 3, 4, 5, 6, 7)
LANES = 128
LOG2E = 1.4426950408889634
FAR = -1e30
VMEM = pl.BlockSpec(memory_space=pltpu.VMEM)
SMEM = pl.BlockSpec(memory_space=pltpu.SMEM)
ANY = pl.BlockSpec(memory_space=pl.ANY)
WIDE_PARTS = 7
AFTER = 2
CUM, WEIGHT, FACTOR = 0, 1, 2
STRIDE, LOG = 1, 2


def iota(shape, axis):
    return lax.broadcasted_iota(jnp.int32, shape, axis)


def matmul(left, right):
    return lax.dot_general(left, right, (((1,), (0,)), ((), ())), preferred_element_type=F32)


def matmul_nt(left, right):
    return lax.dot_general(left, right, (((1,), (1,)), ((), ())), preferred_element_type=F32)


def split2(value):
    high = value.astype(BF16)
    return high, (value - high.astype(F32)).astype(BF16)


def split3(value):
    high = value.astype(BF16)
    rest = value - high.astype(F32)
    middle = rest.astype(BF16)
    return high, middle, (rest - middle.astype(F32)).astype(BF16)


def column(row):
    count = row.shape[1]
    eye = iota((count, count), 0) == iota((count, count), 1)
    return jnp.sum(jnp.where(eye, row, 0.0), axis=1, keepdims=True)


def stacked_columns(rows):
    parts = [part.astype(F32) for part in split3(rows)]
    spare = LANES - 3 * rows.shape[0]
    if spare:
        parts.append(jnp.zeros((spare, rows.shape[1]), F32))
    return jnp.concatenate(parts, axis=0).T.astype(BF16)


def spread_table(heads, head_dim):
    table = np.zeros((LANES, heads * head_dim), np.float32)
    for head in range(heads):
        for part in range(3):
            table[part * heads + head, head * head_dim : (head + 1) * head_dim] = 1.0
    return jnp.asarray(table, BF16)


def softplus(value):
    return jnp.maximum(value, 0.0) + jnp.log1p(jnp.exp(-jnp.abs(value)))


def document_at(starts_ref, position):
    total = jnp.zeros_like(position)
    for entry in range(starts_ref.shape[1]):
        total = total + (starts_ref[0, entry] <= position).astype(jnp.int32)
    return total


def group_place():
    return lax.rem(lax.axis_index("ctx"), GROUP)


def share_out(own, quarter_of_state, places, scratch):
    mine = lax.div(own, QUARTERS)
    part = scratch.shape[0] // HALVES
    for distance in range(QUARTERS):
        scratch[...] = quarter_of_state(lax.rem(own ^ distance, QUARTERS))
        for half in range(HALVES):
            rows = pl.ds(pl.multiple_of((mine ^ half) * part, part), part)
            places[half * QUARTERS + distance][...] = scratch[rows]


def states_kernel(starts, logits, bias, decay, spread_ref, features, writes, cotangent, reads, *refs):
    sends, back_sends = refs[:GROUP], refs[GROUP : 2 * GROUP]
    cols_out, rows_out, scratch = refs[2 * GROUP :]
    heads, length = logits.shape
    state = writes.shape[1]
    width = features.shape[1] // QUARTERS
    part = state // HALVES
    first = lax.axis_index("ctx") * length
    own = group_place()
    stride = softplus(logits[...] + column(bias[...]))
    log_decay = stride * column(-jnp.exp(decay[...]))
    upto = jnp.where(iota((length, length), 0) <= iota((length, length), 1), 1.0, 0.0).astype(BF16)
    parts = matmul(jnp.concatenate(split3(log_decay), axis=0), upto)
    cum = parts[:heads] + parts[heads : 2 * heads] + parts[2 * heads :]
    segment = document_at(starts, first + iota((1, length), 1))
    entry = document_at(starts, jnp.full((1, 1), first - 1, jnp.int32))
    leave = document_at(starts, jnp.full((1, 1), first + length - 1, jnp.int32))
    own_last = jnp.where(segment == leave, 1.0, 0.0)
    keep_in = jnp.where(segment == entry, 1.0, 0.0)
    weight_stack = stacked_columns(own_last * jnp.exp(cum[:, length - 1 :] - cum) * stride)
    factor_stack = stacked_columns(keep_in * jnp.exp(cum))
    write_t = writes[...].astype(F32).T.astype(BF16)

    def quarter_of_state(quarter):
        cols = pl.ds(pl.multiple_of(quarter * width, LANES), width)
        high, low = split2(features[:, cols].astype(F32) * matmul(weight_stack, spread_ref[:, cols]))
        return matmul(write_t, high) + matmul(write_t, low)

    share_out(own, quarter_of_state, [send.at[0:part] for send in sends], scratch)
    read_t = reads[...].astype(F32).T.astype(BF16)

    keeps = []

    def back_quarter(quarter):
        cols = pl.ds(pl.multiple_of(quarter * width, LANES), width)
        wide = matmul(factor_stack, spread_ref[:, cols])
        keeps.append(jnp.broadcast_to(wide[length - 1 :], (8, width)))
        high, low = split2(cotangent[:, cols].astype(F32) * wide)
        return matmul(read_t, high) + matmul(read_t, low)

    share_out(own, back_quarter, back_sends, scratch)
    for distance, send in enumerate(sends):
        send[part:] = keeps[distance % QUARTERS]
    cols_out[CUM] = stacked_columns(cum * LOG2E)
    cols_out[WEIGHT] = weight_stack
    cols_out[FACTOR] = factor_stack
    rows_out[CUM] = cum * LOG2E - jnp.log2(stride)
    rows_out[STRIDE] = stride
    rows_out[LOG] = log_decay


def inner_kernel(
    offset, last, starts, cols_ref, rows_ref, features, cotangent, writes, reads, spread_ref, *refs
):
    if offset:
        before, refs = refs[0], refs[1 + WIDE_PARTS + AFTER :]
    else:
        refs = refs[AFTER:]
    inside, feature_part, skip_part, write_high, write_low, read_high, read_low = refs[:WIDE_PARTS]
    results = refs[WIDE_PARTS:-3]
    scores_ref, mask_ref, grad_ref = refs[-3:]
    length, width = features.shape
    heads = rows_ref.shape[1]
    here = heads // QUARTERS
    head_dim = width // here
    pair = 2 * head_dim
    step = pl.program_id(0)

    @pl.when(step == 0)
    def _():
        first = lax.axis_index("ctx") * length
        segment_row = document_at(starts, first + iota((1, length), 1))
        segment_col = document_at(starts, first + iota((length, 1), 0))
        causal = iota((length, length), 0) >= iota((length, length), 1)
        mask_ref[...] = jnp.where((segment_row == segment_col) & causal, 0.0, FAR)
        scores_ref[...] = matmul_nt(reads[...], writes[...])
        grad_ref[...] = before[...] if offset else jnp.zeros_like(grad_ref)

    write_high[...], write_low[...] = split2(matmul(cols_ref[WEIGHT], spread_ref[...]) * features[...].astype(F32))
    read_high[...], read_low[...] = split2(matmul(cols_ref[FACTOR], spread_ref[...]) * cotangent[...].astype(F32))

    def one_pair(at, carry):
        cols = pl.ds(pl.multiple_of(at * pair, LANES), pair)
        feature = features[:, cols]
        grad = cotangent[:, cols]
        grad_f32 = grad.astype(F32)
        grad_t = grad_f32.T.astype(BF16)
        skip_part[:, cols] = jnp.sum(grad_f32 * feature.astype(F32), axis=0, keepdims=True)
        head = (offset + step) * here + at * 2
        lane = iota((LANES, 2 * LANES), 0)
        wanted = head + lax.div(iota((LANES, 2 * LANES), 1), LANES)
        pick = (lane == wanted) | (lane == wanted + heads) | (lane == wanted + 2 * heads)
        upper = matmul(cols_ref[CUM], jnp.where(pick, 1.0, 0.0).astype(BF16))
        second = iota((LANES, pair), 1) >= head_dim
        back = [None, None]
        for block in range(length // LANES):
            rows = slice(block * LANES, (block + 1) * LANES)
            reach = (block + 1) * LANES
            values = []
            for side in range(2):
                high_row = jnp.concatenate([upper[rows, side * LANES : (side + 1) * LANES]] * (block + 1), axis=1)
                low_row = rows_ref[CUM, pl.ds(head + side, 1), :][:, 0:reach]
                weight = jnp.exp2(high_row - low_row + mask_ref[rows, 0:reach])
                pieces = split2(weight * scores_ref[rows, 0:reach])
                values.append(matmul(jnp.concatenate(pieces, axis=1), jnp.concatenate([feature[0:reach]] * 2, axis=0)))
                grad_rows = grad_t[side * head_dim : (side + 1) * head_dim, rows]
                found = matmul(jnp.concatenate([grad_rows] * 2, axis=1), jnp.concatenate(pieces, axis=0))
                if block:
                    found = jnp.concatenate([found[:, : reach - LANES] + back[side], found[:, reach - LANES :]], axis=1)
                back[side] = found
                only = jnp.where(second == (side == 1), grad_f32[rows], 0.0).astype(BF16)
                grad_ref[rows, 0:reach] += matmul_nt(only, feature[0:reach]) * weight
            inside[rows, cols] = jnp.where(second, values[1], values[0])
        feature_part[:, cols] = jnp.concatenate(back, axis=0).T
        return carry

    lax.fori_loop(0, here // 2, one_pair, 0)

    @pl.when(step == pl.num_programs(0) - 1)
    def _():
        score_grad = grad_ref[...]
        if last:
            write_part, read_part = results
            high, low = split2(score_grad)
            read_part[...] = matmul(high, writes[...]) + matmul(low, writes[...])
            high, low = split2(score_grad.T)
            write_part[...] = matmul(high, reads[...]) + matmul(low, reads[...])
        else:
            results[0][...] = score_grad


def in_order(refs, scratch):
    own = group_place()
    for distance, ref in enumerate(refs):
        scratch[own ^ distance] = ref[...]


def hold_kernel(*refs):
    count = len(refs) // 2
    for value, out in zip(refs[:count], refs[count + 1 :]):
        out[...] = value[...]


def group_kernel(part, *refs):
    up, keeps, came = refs[-3:]
    in_order(refs[:GROUP], came)
    total = came[0, 0:part]
    keep = came[0, part:]
    for j in range(1, GROUP):
        total = total * came[j, part : part + 1] + came[j, 0:part]
        keep = keep * came[j, part:]
    up[0:part] = total
    up[part:] = keep
    for j in range(GROUP):
        keeps[j : j + 1] = came[j, part : part + 1]


def back_group_kernel(part, two, *refs):
    up, keeps = refs[GROUP : GROUP + 2]
    out, came = refs[-2:]
    in_order(refs[:GROUP], came)
    out[part:] = up[part:]

    def downward():
        total = came[GROUP - 1]
        for j in reversed(range(GROUP - 1)):
            total = total * keeps[j : j + 1] + came[j]
        out[0:part] = total

    if two:
        out[0:part] = up[0:part]
        pl.when(lax.axis_index("ctx") >= GROUP)(downward)
    else:
        downward()


def arrived(part, came):
    total, keep = came[0][0:part], came[0][part : part + 1]
    for ref in came[1:]:
        total = total + keep * ref[0:part]
        keep = keep * ref[part : part + 1]
    return total, keep


def link_kernel(part, own, *refs):
    total, keep = arrived(part, refs[:-1])
    refs[-1][0:part] = own[0:part] + own[part : part + 1] * total
    refs[-1][part:] = own[part:] * keep


def spread_kernel(part, count, back_count, *refs):
    first = 2 * GROUP
    ups, downs = refs[first : first + count], refs[first + count : first + count + back_count]
    keeps = refs[first + count + back_count]
    outs = refs[first + count + back_count + 2 : -4]
    came, back_came, give, back_give = refs[-4:]
    in_order(refs[:GROUP], came)
    if downs:
        entering, returning = arrived(part, ups)[0], arrived(part, downs)[0]
    else:
        upper = jnp.full((1, 1), lax.axis_index("ctx")) >= GROUP
        entering = jnp.where(upper, ups[0][0:part], 0.0)
        returning = jnp.where(upper, 0.0, ups[0][0:part])
    total = entering
    for j in range(GROUP):
        give[j] = total
        if j < GROUP - 1:
            total = total * keeps[j : j + 1] + came[j, 0:part]
    in_order(refs[GROUP : 2 * GROUP], back_came)
    total = returning
    for j in reversed(range(GROUP)):
        back_give[j] = total
        if j > 0:
            total = total * keeps[j : j + 1] + back_came[j]
    own = group_place()
    for distance in range(GROUP):
        outs[distance][...] = give[own ^ distance]
        outs[GROUP + distance][...] = back_give[own ^ distance]


def head_sums(ref, value, spread):
    high, low = split2(value)
    ref[...] += matmul_nt(high, spread) + matmul_nt(low, spread)


def wide_skip(skip, heads, spread):
    stack = stacked_columns(jnp.broadcast_to(column(skip[...]), (heads, LANES)))
    return matmul(stack[0:16], spread)[0:1]


def quarter_rows(have, step):
    return jnp.concatenate([have[half * QUARTERS + step] for half in range(HALVES)], axis=0)


def finish_kernel(skip, cols_ref, spread_ref, features, cotangent, reads, inside, *refs):
    mixed, rows, kept, have = refs[GROUP + 1 :]
    length = reads.shape[0]
    heads = skip.shape[1]
    step = pl.program_id(0)

    @pl.when(step == 0)
    def _():
        rows[...] = jnp.zeros_like(rows)
        in_order(refs[:GROUP], have)

    spread = spread_ref[...]
    factor = matmul(cols_ref[FACTOR], spread)
    entering = quarter_rows(have, step)
    kept[...] = entering * factor[length - 1 :]
    stack = jnp.concatenate(split2(entering), axis=0)
    total = inside[...] + factor * matmul(jnp.concatenate([reads[...]] * 2, axis=1), stack)
    mixed[...] = (total + wide_skip(skip, heads, spread) * features[...].astype(F32)).astype(BF16)
    head_sums(rows, cotangent[...].astype(F32) * total, spread)


def back_finish_kernel(
    logits, bias, decay, skip, cols_ref, rows_ref, spread_ref,
    features, cotangent, writes, feature_part, skip_part, row_ref, kept, *refs,
):
    haves = refs[:GROUP]
    feature_grad, step_grad, sums, col_acc, last_acc, skip_acc, have = refs[GROUP:]
    heads, length = logits.shape
    state = writes.shape[1]
    width = features.shape[1]
    step = pl.program_id(0)

    @pl.when(step == 0)
    def _():
        for ref in (col_acc, last_acc, skip_acc):
            ref[...] = jnp.zeros_like(ref)
        in_order(haves, have)

    spread = spread_ref[...]
    weight = matmul(cols_ref[WEIGHT], spread)
    feature = features[...].astype(F32)
    returning = quarter_rows(have, step)
    stack = jnp.concatenate(split2(returning), axis=0)
    writes2 = jnp.concatenate([writes[...]] * 2, axis=1)
    carried = weight * matmul(writes2, stack)
    total = feature_part[...] + carried
    feature_grad[...] = (total + wide_skip(skip, heads, spread) * cotangent[...].astype(F32)).astype(BF16)
    head_sums(col_acc, feature * total, spread)
    leaving = jnp.sum((returning * kept[...]).reshape(state // 8, 8, width), axis=0)
    leaving = leaving + jnp.sum((feature * carried).reshape(length // 8, 8, width), axis=0)
    head_sums(last_acc, leaving, spread)
    head_sums(skip_acc, jnp.broadcast_to(skip_part[...], (8, width)), spread)

    @pl.when(step == QUARTERS - 1)
    def _():
        rows = row_ref[...].T[:heads]
        cols = col_acc[...].T[:heads]
        last = column(jnp.sum(last_acc[...], axis=0, keepdims=True))[:heads]
        stride = rows_ref[STRIDE]
        gap_grad = rows - cols + jnp.where(iota((heads, length), 1) == length - 1, last, 0.0)
        onward = jnp.where(iota((length, length), 0) >= iota((length, length), 1), 1.0, 0.0).astype(BF16)
        parts = matmul(jnp.concatenate(split3(gap_grad), axis=0), onward)
        log_grad = parts[:heads] + parts[heads : 2 * heads] + parts[2 * heads :]
        rate = column(-jnp.exp(decay[...]))
        slope = 1.0 / (1.0 + jnp.exp(-(logits[...] + column(bias[...]))))
        step_value = (cols / stride + rate * log_grad) * slope
        step_grad[...] = step_value
        bias_sum = jnp.sum(step_value, axis=1, keepdims=True)
        decay_sum = jnp.sum(log_grad * rows_ref[LOG], axis=1, keepdims=True)
        skip_sum = column(skip_acc[0:1])[:heads]
        spare = jnp.zeros((LANES - 3 * heads, 1), F32)
        table = jnp.concatenate([bias_sum, decay_sum, skip_sum, spare], axis=0)
        eye = iota((LANES, LANES), 0) == iota((LANES, LANES), 1)
        table = jnp.sum(jnp.where(eye, table, 0.0), axis=0, keepdims=True)
        sums[...] = jnp.broadcast_to(table[None], sums.shape)


def keys_kernel(write_part, read_part, write_high, write_low, read_high, read_low, *refs):
    write_grad, read_grad, write_acc, read_acc, have, back_have = refs[2 * GROUP + 1 :]
    state = write_part.shape[1]
    step = pl.program_id(0)

    @pl.when(step == 0)
    def _():
        write_acc[...] = jnp.zeros_like(write_acc)
        read_acc[...] = jnp.zeros_like(read_acc)
        in_order(refs[:GROUP], have)
        in_order(refs[GROUP : 2 * GROUP], back_have)

    for states, high, low, acc in (
        (have, read_high, read_low, read_acc),
        (back_have, write_high, write_low, write_acc),
    ):
        stack = jnp.concatenate(split2(quarter_rows(states, step)), axis=0)
        acc[...] += matmul_nt(high[...], stack) + matmul_nt(low[...], stack)

    @pl.when(step == QUARTERS - 1)
    def _():
        write_grad[...] = (write_part[...] + write_acc[:, :state] + write_acc[:, state:]).astype(BF16)
        read_grad[...] = (read_part[...] + read_acc[:, :state] + read_acc[:, state:]).astype(BF16)


def call(kernel, name, outs, in_specs, work, mib, **more):
    return pl.pallas_call(
        kernel,
        out_shape=outs,
        in_specs=in_specs,
        out_specs=more.pop("out_specs", [VMEM] * len(outs)),
        compiler_params=pltpu.CompilerParams(vmem_limit_bytes=mib * 2**20),
        cost_estimate=pl.CostEstimate(flops=work * 10**9, bytes_accessed=10**6, transcendentals=0),
        name=name,
        **more,
    )


def struct(shape, dtype=F32):
    return jax.ShapeDtypeStruct(shape, dtype)


def local(
    features, write_keys, read_queries, step_logits, step_bias, decay_log, skip_gain, doc_starts, out_grad
):
    features, writes, reads, logits, cotangent = (
        features[0], write_keys[0], read_queries[0], step_logits[0], out_grad[0]
    )
    length, wide = features.shape
    heads = logits.shape[0]
    state = writes.shape[1]
    head_dim = wide // heads
    width = wide // QUARTERS
    part = state // HALVES
    bias, decay, skip = step_bias[None], decay_log[None], skip_gain[None]
    blocks, members = lax.axis_size("ctx"), lax.axis_size("dp")
    spread = spread_table(heads, head_dim)

    def exchange(value, distance):
        return lax.ppermute(value, "ctx", [(k, k ^ distance) for k in range(blocks)])

    def swap(values):
        came = {d: exchange(values[d], d) for d in DISTANCES}
        return [came.get(d, values[0]) for d in range(GROUP)]

    def shift(value, distance):
        pairs = [(k, k + distance) for k in range(blocks) if 0 <= k + distance < blocks]
        return lax.ppermute(value, "ctx", pairs)

    def scan(own, sign):
        came, near, reach = [], own, 1
        while reach < blocks // GROUP:
            came.append(shift(near, sign * GROUP * reach))
            reach *= 2
            if reach < blocks // GROUP:
                near = call(
                    functools.partial(link_kernel, part), "link", [group_sum], [VMEM] * (1 + len(came)), 1, 8
                )(own, *came)[0]
        return came

    def all_of(*shape):
        return pl.BlockSpec(shape, lambda step: (0,) * len(shape))

    def quarter_of(rows, offset=0):
        return pl.BlockSpec((rows, width), lambda step: (0, step + offset))

    small = struct((heads, length))
    result = struct((length, wide), BF16)
    tokens_result = struct((length, state), BF16)
    group_sum = struct((part + 8, width))
    tokens = all_of(length, state)
    columns = all_of(length, LANES)
    by_heads = all_of(heads, length)
    all_cols, all_rows = all_of(3, length, LANES), all_of(3, heads, length)
    row = all_of(1, heads)
    by_quarter = quarter_of(length)
    spread_quarter = quarter_of(LANES)
    shares = pltpu.VMEM((GROUP, part, width), F32)
    long_shares = pltpu.VMEM((GROUP, part + 8, width), F32)

    share = struct((part, width))
    out = call(
        states_kernel,
        "states",
        [group_sum] * GROUP + [share] * GROUP + [struct((3, length, LANES), BF16), struct((3, heads, length))],
        [SMEM] + [VMEM] * 8,
        4,
        60,
        scratch_shapes=[pltpu.VMEM((state, width), F32)],
    )(doc_starts, logits, bias, decay, spread, features, writes, cotangent, reads)
    came = swap(out[:GROUP])
    back_sends = out[GROUP : 2 * GROUP]
    cols, head_rows = out[2 * GROUP :]

    wide_part, wide_piece = struct((length, wide)), struct((length, wide), BF16)
    wide_parts = [wide_part] * 2 + [struct((1, wide))] + [wide_piece] * 4
    inner_args = (
        doc_starts, cols, head_rows, features, cotangent, writes, reads, spread
    )

    square = all_of(length, length)
    token_part = struct((length, state))

    def inner(offset, count, begun, after):
        mine = quarter_of(length, offset)
        last = offset + count == QUARTERS
        n_args = len(inner_args) + 1
        return call(
            functools.partial(inner_kernel, offset, last),
            "inner_" + str(offset),
            wide_parts + ([token_part] * 2 if last else [struct((length, length))]),
            [SMEM, all_cols, all_rows, mine, mine, tokens, tokens, quarter_of(LANES, offset)]
            + ([square] + [ANY] * WIDE_PARTS if offset else [])
            + [ANY] * AFTER,
            5 * count,
            24,
            grid=(count,),
            out_specs=[mine, mine, quarter_of(1, offset)] + [mine] * 4 + ([tokens] * 2 if last else [square]),
            scratch_shapes=[pltpu.VMEM((length, length), F32)] * 3,
            input_output_aliases={n_args + at: at for at in range(WIDE_PARTS)} if offset else {},
        )(*inner_args, *begun, *after)

    def hold(values, distances, until):
        chosen = [values[d] for d in distances]
        count = len(chosen)
        held = call(hold_kernel, "hold", [share] * count, [VMEM] * count + [ANY], 1, 12)(*chosen, until)
        return dict(zip(distances, held))

    *begun, score_grad = inner(0, 1, [], [came[1], came[2]])
    early = hold(back_sends, (1, 2, 3), score_grad)
    back_came = [back_sends[0]] + [exchange(early[d], d) for d in (1, 2, 3)]
    up, keeps = call(
        functools.partial(group_kernel, part),
        "group",
        [group_sum, struct((GROUP, width))],
        [VMEM] * GROUP + [ANY],
        2,
        12,
        scratch_shapes=[long_shares],
    )(*came, score_grad)
    *begun, score_grad = inner(1, 1, [score_grad, *begun], [up, back_came[1]])
    late = hold(back_sends, (4, 5, 6, 7), score_grad)
    back_came += [exchange(late[d], d) for d in (4, 5, 6, 7)]
    two = blocks == 2 * GROUP
    (cross,) = call(
        functools.partial(back_group_kernel, part, two),
        "back_group",
        [group_sum],
        [VMEM] * (GROUP + 2) + [ANY],
        2,
        12,
        scratch_shapes=[shares],
    )(*back_came, up, keeps, score_grad)
    if two:
        ups, downs = [exchange(cross, GROUP)], []
    else:
        ups, downs = scan(up, 1), scan(cross, -1)
    *done, write_part, read_part = inner(2, QUARTERS - 2, [score_grad, *begun], [cross] * AFTER)
    inside, feature_part, skip_part, *pieces = done
    give = call(
        functools.partial(spread_kernel, part, len(ups), len(downs)),
        "spread",
        [share] * 2 * GROUP,
        [VMEM] * (2 * GROUP + len(ups) + len(downs) + 1) + [ANY],
        2,
        16,
        scratch_shapes=[long_shares, shares, shares, shares],
    )(*came, *back_came, *ups, *downs, keeps, write_part)
    have, back_have = swap(give[:GROUP]), swap(give[GROUP:])
    devices = blocks * members
    whole_shares = [all_of(part, width)] * GROUP
    mixed, rows, kept = call(
        finish_kernel,
        "finish",
        [result, struct((length, LANES)), struct((state, wide))],
        [row, all_cols, spread_quarter, by_quarter, by_quarter, tokens, by_quarter] + whole_shares + [ANY],
        8,
        24,
        grid=(QUARTERS,),
        out_specs=[by_quarter, columns, quarter_of(state)],
        scratch_shapes=[shares],
    )(skip, cols, spread, features, cotangent, reads, inside, *have, back_have[DISTANCES[1]])
    feature_grad, step_grad, sums = call(
        back_finish_kernel,
        "back_finish",
        [result, small, struct((devices, 1, LANES))],
        [by_heads, row, row, row, all_cols, all_rows, spread_quarter]
        + [by_quarter, by_quarter, tokens, by_quarter]
        + [quarter_of(1), columns, quarter_of(state)]
        + whole_shares,
        8,
        24,
        grid=(QUARTERS,),
        out_specs=[by_quarter, by_heads, all_of(devices, 1, LANES)],
        scratch_shapes=[pltpu.VMEM((length, LANES), F32)] + [pltpu.VMEM((8, LANES), F32)] * 2 + [shares],
    )(
        logits, bias, decay, skip, cols, head_rows, spread, features, cotangent, writes,
        feature_part, skip_part, rows, kept, *back_have,
    )
    write_grad, read_grad = call(
        keys_kernel,
        "keys",
        [tokens_result] * 2,
        [tokens] * 2 + [by_quarter] * 4 + whole_shares * 2 + [ANY],
        6,
        60,
        grid=(QUARTERS,),
        out_specs=[tokens] * 2,
        scratch_shapes=[pltpu.VMEM((length, 2 * state), F32)] * 2 + [shares] * 2,
    )(write_part, read_part, *pieces, *have, *back_have, step_grad)
    sums = jnp.sum(lax.all_to_all(sums, ("dp", "ctx"), 0, 0), axis=(0, 1))
    return (
        mixed[None],
        feature_grad[None],
        write_grad[None],
        read_grad[None],
        step_grad[None],
        sums[:heads],
        sums[heads : 2 * heads],
        sums[2 * heads : 3 * heads],
    )


def solution(mesh):
    by_tokens = P("dp", "ctx", None)
    by_heads = P("dp", None, "ctx")
    in_specs = (by_tokens, by_tokens, by_tokens, by_heads, P(), P(), P(), P("dp", None), by_tokens)
    out_specs = (by_tokens, by_tokens, by_tokens, by_tokens, by_heads, P(), P(), P())
    return jax.shard_map(local, mesh=mesh, in_specs=in_specs, out_specs=out_specs, check_vma=False)
```

```python
import functools

import jax
import jax.numpy as jnp
import numpy as np
from jax import lax
from jax.experimental import pallas as pl
from jax.experimental.pallas import tpu as pltpu
from jax.sharding import PartitionSpec as P

F32 = jnp.float32
BF16 = jnp.bfloat16
QUARTERS = 4
HALVES = 2
GROUP = QUARTERS * HALVES
DISTANCES = (7, 1, 6, 2, 5, 3, 4)
LANES = 128
LOG2E = 1.4426950408889634
FAR = -1e30
VMEM = pl.BlockSpec(memory_space=pltpu.VMEM)
SMEM = pl.BlockSpec(memory_space=pltpu.SMEM)
ANY = pl.BlockSpec(memory_space=pl.ANY)
WIDE_PARTS = 7
AFTER = 2
CUM, WEIGHT, FACTOR = 0, 1, 2
STRIDE, LOG = 1, 2


def iota(shape, axis):
    return lax.broadcasted_iota(jnp.int32, shape, axis)


def matmul(left, right):
    return lax.dot_general(left, right, (((1,), (0,)), ((), ())), preferred_element_type=F32)


def matmul_nt(left, right):
    return lax.dot_general(left, right, (((1,), (1,)), ((), ())), preferred_element_type=F32)


def split2(value):
    high = value.astype(BF16)
    return high, (value - high.astype(F32)).astype(BF16)


def split3(value):
    high = value.astype(BF16)
    rest = value - high.astype(F32)
    middle = rest.astype(BF16)
    return high, middle, (rest - middle.astype(F32)).astype(BF16)


def column(row):
    count = row.shape[1]
    eye = iota((count, count), 0) == iota((count, count), 1)
    return jnp.sum(jnp.where(eye, row, 0.0), axis=1, keepdims=True)


def stacked_columns(rows):
    parts = [part.astype(F32) for part in split3(rows)]
    spare = LANES - 3 * rows.shape[0]
    if spare:
        parts.append(jnp.zeros((spare, rows.shape[1]), F32))
    return jnp.concatenate(parts, axis=0).T.astype(BF16)


def spread_table(heads, head_dim):
    table = np.zeros((LANES, heads * head_dim), np.float32)
    for head in range(heads):
        for part in range(3):
            table[part * heads + head, head * head_dim : (head + 1) * head_dim] = 1.0
    return jnp.asarray(table, BF16)


def softplus(value):
    return jnp.maximum(value, 0.0) + jnp.log1p(jnp.exp(-jnp.abs(value)))


def document_at(starts_ref, position):
    total = jnp.zeros_like(position)
    for entry in range(starts_ref.shape[1]):
        total = total + (starts_ref[0, entry] <= position).astype(jnp.int32)
    return total


def group_place():
    return lax.rem(lax.axis_index("ctx"), GROUP)


def share_out(own, quarter_of_state, places, scratch):
    mine = lax.div(own, QUARTERS)
    part = scratch.shape[0] // HALVES
    for distance in range(QUARTERS):
        scratch[...] = quarter_of_state(lax.rem(own ^ distance, QUARTERS))
        for half in range(HALVES):
            rows = pl.ds(pl.multiple_of((mine ^ half) * part, part), part)
            places[half * QUARTERS + distance][...] = scratch[rows]


def states_kernel(starts, logits, bias, decay, spread_ref, features, writes, cotangent, reads, *refs):
    sends = refs[:GROUP]
    cols_out, rows_out, scratch = refs[GROUP:]
    heads, length = logits.shape
    state = writes.shape[1]
    width = features.shape[1] // QUARTERS
    part = state // HALVES
    first = lax.axis_index("ctx") * length
    own = group_place()
    stride = softplus(logits[...] + column(bias[...]))
    log_decay = stride * column(-jnp.exp(decay[...]))
    upto = jnp.where(iota((length, length), 0) <= iota((length, length), 1), 1.0, 0.0).astype(BF16)
    parts = matmul(jnp.concatenate(split3(log_decay), axis=0), upto)
    cum = parts[:heads] + parts[heads : 2 * heads] + parts[2 * heads :]
    segment = document_at(starts, first + iota((1, length), 1))
    entry = document_at(starts, jnp.full((1, 1), first - 1, jnp.int32))
    leave = document_at(starts, jnp.full((1, 1), first + length - 1, jnp.int32))
    own_last = jnp.where(segment == leave, 1.0, 0.0)
    keep_in = jnp.where(segment == entry, 1.0, 0.0)
    weight_stack = stacked_columns(own_last * jnp.exp(cum[:, length - 1 :] - cum) * stride)
    factor_stack = stacked_columns(keep_in * jnp.exp(cum))
    write_t = writes[...].astype(F32).T.astype(BF16)

    def quarter_of_state(quarter):
        cols = pl.ds(pl.multiple_of(quarter * width, LANES), width)
        high, low = split2(features[:, cols].astype(F32) * matmul(weight_stack, spread_ref[:, cols]))
        return matmul(write_t, high) + matmul(write_t, low)

    share_out(own, quarter_of_state, [send.at[0:part] for send in sends], scratch)
    read_t = reads[...].astype(F32).T.astype(BF16)

    keeps = []

    def back_quarter(quarter):
        cols = pl.ds(pl.multiple_of(quarter * width, LANES), width)
        wide = matmul(factor_stack, spread_ref[:, cols])
        keeps.append(jnp.broadcast_to(wide[length - 1 :], (8, width)))
        high, low = split2(cotangent[:, cols].astype(F32) * wide)
        return matmul(read_t, high) + matmul(read_t, low)

    share_out(own, back_quarter, [send.at[part + 8 :] for send in sends], scratch)
    for distance, send in enumerate(sends):
        send[part : part + 8] = keeps[distance % QUARTERS]
    cols_out[CUM] = stacked_columns(cum * LOG2E)
    cols_out[WEIGHT] = weight_stack
    cols_out[FACTOR] = factor_stack
    rows_out[CUM] = cum * LOG2E - jnp.log2(stride)
    rows_out[STRIDE] = stride
    rows_out[LOG] = log_decay


def inner_kernel(
    starts, cols_ref, rows_ref, features, cotangent, writes, reads, spread_ref, *refs
):
    refs = refs[AFTER:]
    inside, feature_part, skip_part, write_high, write_low, read_high, read_low = refs[:WIDE_PARTS]
    write_part, read_part = refs[WIDE_PARTS:-3]
    scores_ref, mask_ref, grad_ref = refs[-3:]
    length, width = features.shape
    heads = rows_ref.shape[1]
    here = heads // QUARTERS
    head_dim = width // here
    pair = 2 * head_dim
    step = pl.program_id(0)

    @pl.when(step == 0)
    def _():
        first = lax.axis_index("ctx") * length
        segment_row = document_at(starts, first + iota((1, length), 1))
        segment_col = document_at(starts, first + iota((length, 1), 0))
        causal = iota((length, length), 0) >= iota((length, length), 1)
        mask_ref[...] = jnp.where((segment_row == segment_col) & causal, 0.0, FAR)
        scores_ref[...] = matmul_nt(reads[...], writes[...])
        grad_ref[...] = jnp.zeros_like(grad_ref)

    write_high[...], write_low[...] = split2(matmul(cols_ref[WEIGHT], spread_ref[...]) * features[...].astype(F32))
    read_high[...], read_low[...] = split2(matmul(cols_ref[FACTOR], spread_ref[...]) * cotangent[...].astype(F32))

    def one_pair(at, carry):
        cols = pl.ds(pl.multiple_of(at * pair, LANES), pair)
        feature = features[:, cols]
        grad = cotangent[:, cols]
        grad_f32 = grad.astype(F32)
        grad_t = grad_f32.T.astype(BF16)
        skip_part[:, cols] = jnp.sum(grad_f32 * feature.astype(F32), axis=0, keepdims=True)
        head = step * here + at * 2
        lane = iota((LANES, 2 * LANES), 0)
        wanted = head + lax.div(iota((LANES, 2 * LANES), 1), LANES)
        pick = (lane == wanted) | (lane == wanted + heads) | (lane == wanted + 2 * heads)
        upper = matmul(cols_ref[CUM], jnp.where(pick, 1.0, 0.0).astype(BF16))
        second = iota((LANES, pair), 1) >= head_dim
        back = [None, None]
        for block in range(length // LANES):
            rows = slice(block * LANES, (block + 1) * LANES)
            reach = (block + 1) * LANES
            values = []
            for side in range(2):
                high_row = jnp.concatenate([upper[rows, side * LANES : (side + 1) * LANES]] * (block + 1), axis=1)
                low_row = rows_ref[CUM, pl.ds(head + side, 1), :][:, 0:reach]
                weight = jnp.exp2(high_row - low_row + mask_ref[rows, 0:reach])
                pieces = split2(weight * scores_ref[rows, 0:reach])
                values.append(matmul(jnp.concatenate(pieces, axis=1), jnp.concatenate([feature[0:reach]] * 2, axis=0)))
                grad_rows = grad_t[side * head_dim : (side + 1) * head_dim, rows]
                found = matmul(jnp.concatenate([grad_rows] * 2, axis=1), jnp.concatenate(pieces, axis=0))
                if block:
                    found = jnp.concatenate([found[:, : reach - LANES] + back[side], found[:, reach - LANES :]], axis=1)
                back[side] = found
                only = jnp.where(second == (side == 1), grad_f32[rows], 0.0).astype(BF16)
                grad_ref[rows, 0:reach] += matmul_nt(only, feature[0:reach]) * weight
            inside[rows, cols] = jnp.where(second, values[1], values[0])
        feature_part[:, cols] = jnp.concatenate(back, axis=0).T
        return carry

    lax.fori_loop(0, here // 2, one_pair, 0)

    @pl.when(step == QUARTERS - 1)
    def _():
        score_grad = grad_ref[...]
        high, low = split2(score_grad)
        read_part[...] = matmul(high, writes[...]) + matmul(low, writes[...])
        high, low = split2(score_grad.T)
        write_part[...] = matmul(high, reads[...]) + matmul(low, reads[...])


def in_order(refs, scratch, back=False):
    own = group_place()
    rows = scratch.shape[1]
    for distance, ref in enumerate(refs):
        first = ref.shape[0] - rows if back else 0
        scratch[own ^ distance] = ref[first : first + rows]


def group_kernel(part, *refs):
    keeps, came, back_came = refs[-3:]
    sums = refs[GROUP + 1 : -3]
    up, down = sums[0], sums[-1]
    in_order(refs[:GROUP], came)
    total = came[0, 0:part]
    keep = came[0, part:]
    for j in range(1, GROUP):
        total = total * came[j, part : part + 1] + came[j, 0:part]
        keep = keep * came[j, part:]
    up[0:part] = total
    up[part:] = keep
    for j in range(GROUP):
        keeps[j : j + 1] = came[j, part : part + 1]
    in_order(refs[:GROUP], back_came, back=True)

    def downward():
        total = back_came[GROUP - 1]
        for j in reversed(range(GROUP - 1)):
            total = total * keeps[j : j + 1] + back_came[j]
        down[0:part] = total
        down[part:] = keep

    if len(sums) == 1:
        pl.when(lax.axis_index("ctx") >= GROUP)(downward)
    else:
        downward()


def arrived(part, came):
    total, keep = came[0][0:part], came[0][part : part + 1]
    for ref in came[1:]:
        total = total + keep * ref[0:part]
        keep = keep * ref[part : part + 1]
    return total, keep


def link_kernel(part, own, *refs):
    total, keep = arrived(part, refs[:-1])
    refs[-1][0:part] = own[0:part] + own[part : part + 1] * total
    refs[-1][part:] = own[part:] * keep


def spread_kernel(part, count, back_count, *refs):
    first = GROUP
    ups, downs = refs[first : first + count], refs[first + count : first + count + back_count]
    keeps = refs[first + count + back_count]
    outs = refs[first + count + back_count + 2 : -4]
    came, back_came, give, back_give = refs[-4:]
    in_order(refs[:GROUP], came)
    if downs:
        entering, returning = arrived(part, ups)[0], arrived(part, downs)[0]
    else:
        upper = jnp.full((1, 1), lax.axis_index("ctx")) >= GROUP
        entering = jnp.where(upper, ups[0][0:part], 0.0)
        returning = jnp.where(upper, 0.0, ups[0][0:part])
    total = entering
    for j in range(GROUP):
        give[j] = total
        if j < GROUP - 1:
            total = total * keeps[j : j + 1] + came[j, 0:part]
    in_order(refs[:GROUP], back_came, back=True)
    total = returning
    for j in reversed(range(GROUP)):
        back_give[j] = total
        if j > 0:
            total = total * keeps[j : j + 1] + back_came[j]
    own = group_place()
    for distance in range(GROUP):
        outs[distance][...] = give[own ^ distance]
        outs[GROUP + distance][...] = back_give[own ^ distance]


def head_sums(ref, value, spread):
    high, low = split2(value)
    ref[...] += matmul_nt(high, spread) + matmul_nt(low, spread)


def wide_skip(skip, heads, spread):
    stack = stacked_columns(jnp.broadcast_to(column(skip[...]), (heads, LANES)))
    return matmul(stack[0:16], spread)[0:1]


def quarter_rows(have, step):
    return jnp.concatenate([have[half * QUARTERS + step] for half in range(HALVES)], axis=0)


def finish_kernel(skip, cols_ref, spread_ref, features, cotangent, reads, inside, *refs):
    mixed, rows, kept, have = refs[GROUP + 1 :]
    length = reads.shape[0]
    heads = skip.shape[1]
    step = pl.program_id(0)

    @pl.when(step == 0)
    def _():
        rows[...] = jnp.zeros_like(rows)
        in_order(refs[:GROUP], have)

    spread = spread_ref[...]
    factor = matmul(cols_ref[FACTOR], spread)
    entering = quarter_rows(have, step)
    kept[...] = entering * factor[length - 1 :]
    stack = jnp.concatenate(split2(entering), axis=0)
    total = inside[...] + factor * matmul(jnp.concatenate([reads[...]] * 2, axis=1), stack)
    mixed[...] = (total + wide_skip(skip, heads, spread) * features[...].astype(F32)).astype(BF16)
    head_sums(rows, cotangent[...].astype(F32) * total, spread)


def back_finish_kernel(
    logits, bias, decay, skip, cols_ref, rows_ref, spread_ref,
    features, cotangent, writes, feature_part, skip_part, row_ref, kept, *refs,
):
    haves = refs[:GROUP]
    feature_grad, step_grad, sums, col_acc, last_acc, skip_acc, have = refs[GROUP:]
    heads, length = logits.shape
    state = writes.shape[1]
    width = features.shape[1]
    step = pl.program_id(0)

    @pl.when(step == 0)
    def _():
        for ref in (col_acc, last_acc, skip_acc):
            ref[...] = jnp.zeros_like(ref)
        in_order(haves, have)

    spread = spread_ref[...]
    weight = matmul(cols_ref[WEIGHT], spread)
    feature = features[...].astype(F32)
    returning = quarter_rows(have, step)
    stack = jnp.concatenate(split2(returning), axis=0)
    writes2 = jnp.concatenate([writes[...]] * 2, axis=1)
    carried = weight * matmul(writes2, stack)
    total = feature_part[...] + carried
    feature_grad[...] = (total + wide_skip(skip, heads, spread) * cotangent[...].astype(F32)).astype(BF16)
    head_sums(col_acc, feature * total, spread)
    leaving = jnp.sum((returning * kept[...]).reshape(state // 8, 8, width), axis=0)
    leaving = leaving + jnp.sum((feature * carried).reshape(length // 8, 8, width), axis=0)
    head_sums(last_acc, leaving, spread)
    head_sums(skip_acc, jnp.broadcast_to(skip_part[...], (8, width)), spread)

    @pl.when(step == QUARTERS - 1)
    def _():
        rows = row_ref[...].T[:heads]
        cols = col_acc[...].T[:heads]
        last = column(jnp.sum(last_acc[...], axis=0, keepdims=True))[:heads]
        stride = rows_ref[STRIDE]
        gap_grad = rows - cols + jnp.where(iota((heads, length), 1) == length - 1, last, 0.0)
        onward = jnp.where(iota((length, length), 0) >= iota((length, length), 1), 1.0, 0.0).astype(BF16)
        parts = matmul(jnp.concatenate(split3(gap_grad), axis=0), onward)
        log_grad = parts[:heads] + parts[heads : 2 * heads] + parts[2 * heads :]
        rate = column(-jnp.exp(decay[...]))
        slope = 1.0 / (1.0 + jnp.exp(-(logits[...] + column(bias[...]))))
        step_value = (cols / stride + rate * log_grad) * slope
        step_grad[...] = step_value
        bias_sum = jnp.sum(step_value, axis=1, keepdims=True)
        decay_sum = jnp.sum(log_grad * rows_ref[LOG], axis=1, keepdims=True)
        skip_sum = column(skip_acc[0:1])[:heads]
        spare = jnp.zeros((LANES - 3 * heads, 1), F32)
        table = jnp.concatenate([bias_sum, decay_sum, skip_sum, spare], axis=0)
        eye = iota((LANES, LANES), 0) == iota((LANES, LANES), 1)
        table = jnp.sum(jnp.where(eye, table, 0.0), axis=0, keepdims=True)
        sums[...] = jnp.broadcast_to(table[None], sums.shape)


def keys_kernel(write_part, read_part, write_high, write_low, read_high, read_low, *refs):
    write_grad, read_grad, write_acc, read_acc, have, back_have = refs[2 * GROUP + 1 :]
    state = write_part.shape[1]
    step = pl.program_id(0)

    @pl.when(step == 0)
    def _():
        write_acc[...] = jnp.zeros_like(write_acc)
        read_acc[...] = jnp.zeros_like(read_acc)
        in_order(refs[:GROUP], have)
        in_order(refs[GROUP : 2 * GROUP], back_have)

    for states, high, low, acc in (
        (have, read_high, read_low, read_acc),
        (back_have, write_high, write_low, write_acc),
    ):
        stack = jnp.concatenate(split2(quarter_rows(states, step)), axis=0)
        acc[...] += matmul_nt(high[...], stack) + matmul_nt(low[...], stack)

    @pl.when(step == QUARTERS - 1)
    def _():
        write_grad[...] = (write_part[...] + write_acc[:, :state] + write_acc[:, state:]).astype(BF16)
        read_grad[...] = (read_part[...] + read_acc[:, :state] + read_acc[:, state:]).astype(BF16)


def call(kernel, name, outs, in_specs, work, mib, **more):
    return pl.pallas_call(
        kernel,
        out_shape=outs,
        in_specs=in_specs,
        out_specs=more.pop("out_specs", [VMEM] * len(outs)),
        compiler_params=pltpu.CompilerParams(vmem_limit_bytes=mib * 2**20),
        cost_estimate=pl.CostEstimate(flops=work * 10**9, bytes_accessed=10**6, transcendentals=0),
        name=name,
        **more,
    )


def struct(shape, dtype=F32):
    return jax.ShapeDtypeStruct(shape, dtype)


def local(
    features, write_keys, read_queries, step_logits, step_bias, decay_log, skip_gain, doc_starts, out_grad
):
    features, writes, reads, logits, cotangent = (
        features[0], write_keys[0], read_queries[0], step_logits[0], out_grad[0]
    )
    length, wide = features.shape
    heads = logits.shape[0]
    state = writes.shape[1]
    head_dim = wide // heads
    width = wide // QUARTERS
    part = state // HALVES
    bias, decay, skip = step_bias[None], decay_log[None], skip_gain[None]
    blocks, members = lax.axis_size("ctx"), lax.axis_size("dp")
    spread = spread_table(heads, head_dim)

    def exchange(value, distance):
        return lax.ppermute(value, "ctx", [(k, k ^ distance) for k in range(blocks)])

    def swap(values):
        came = {d: exchange(values[d], d) for d in DISTANCES}
        return [came.get(d, values[0]) for d in range(GROUP)]

    def shift(value, distance):
        pairs = [(k, k + distance) for k in range(blocks) if 0 <= k + distance < blocks]
        return lax.ppermute(value, "ctx", pairs)

    def scan(own, sign):
        came, near, reach = [], own, 1
        while reach < blocks // GROUP:
            came.append(shift(near, sign * GROUP * reach))
            reach *= 2
            if reach < blocks // GROUP:
                near = call(
                    functools.partial(link_kernel, part), "link", [group_sum], [VMEM] * (1 + len(came)), 1, 8
                )(own, *came)[0]
        return came

    def all_of(*shape):
        return pl.BlockSpec(shape, lambda step: (0,) * len(shape))

    def quarter_of(rows, offset=0):
        return pl.BlockSpec((rows, width), lambda step: (0, step + offset))

    small = struct((heads, length))
    result = struct((length, wide), BF16)
    tokens_result = struct((length, state), BF16)
    group_sum = struct((part + 8, width))
    tokens = all_of(length, state)
    columns = all_of(length, LANES)
    by_heads = all_of(heads, length)
    all_cols, all_rows = all_of(3, length, LANES), all_of(3, heads, length)
    row = all_of(1, heads)
    by_quarter = quarter_of(length)
    spread_quarter = quarter_of(LANES)
    shares = pltpu.VMEM((GROUP, part, width), F32)
    long_shares = pltpu.VMEM((GROUP, part + 8, width), F32)

    share = struct((part, width))
    out = call(
        states_kernel,
        "states",
        [struct((2 * part + 8, width))] * GROUP + [struct((3, length, LANES), BF16), struct((3, heads, length))],
        [SMEM] + [VMEM] * 8,
        4,
        60,
        scratch_shapes=[pltpu.VMEM((state, width), F32)],
    )(doc_starts, logits, bias, decay, spread, features, writes, cotangent, reads)
    came = swap(out[:GROUP])
    cols, head_rows = out[GROUP:]

    wide_part, wide_piece = struct((length, wide)), struct((length, wide), BF16)
    wide_parts = [wide_part] * 2 + [struct((1, wide))] + [wide_piece] * 4
    token_part = struct((length, state))
    inside, feature_part, skip_part, *pieces, write_part, read_part = call(
        inner_kernel,
        "inner",
        wide_parts + [token_part] * 2,
        [SMEM, all_cols, all_rows, by_quarter, by_quarter, tokens, tokens, spread_quarter] + [ANY] * AFTER,
        10,
        24,
        grid=(QUARTERS,),
        out_specs=[by_quarter, by_quarter, quarter_of(1)] + [by_quarter] * 4 + [tokens] * 2,
        scratch_shapes=[pltpu.VMEM((length, length), F32)] * 3,
    )(
        doc_starts, cols, head_rows, features, cotangent, writes, reads, spread,
        *[came[d] for d in DISTANCES[1 : 1 + AFTER]],
    )
    two = blocks == 2 * GROUP
    *group_sums, keeps = call(
        functools.partial(group_kernel, part),
        "group",
        [group_sum] * (1 if two else 2) + [struct((GROUP, width))],
        [VMEM] * GROUP + [ANY],
        2,
        12,
        scratch_shapes=[long_shares, shares],
    )(*came, write_part)
    if two:
        ups, downs = [exchange(group_sums[0], GROUP)], []
    else:
        ups, downs = scan(group_sums[0], 1), scan(group_sums[1], -1)
    give = call(
        functools.partial(spread_kernel, part, len(ups), len(downs)),
        "spread",
        [share] * 2 * GROUP,
        [VMEM] * (GROUP + len(ups) + len(downs) + 1) + [ANY],
        2,
        16,
        scratch_shapes=[long_shares, shares, shares, shares],
    )(*came, *ups, *downs, keeps, write_part)
    have, back_have = swap(give[:GROUP]), swap(give[GROUP:])
    devices = blocks * members
    whole_shares = [all_of(part, width)] * GROUP
    mixed, rows, kept = call(
        finish_kernel,
        "finish",
        [result, struct((length, LANES)), struct((state, wide))],
        [row, all_cols, spread_quarter, by_quarter, by_quarter, tokens, by_quarter] + whole_shares + [ANY],
        8,
        24,
        grid=(QUARTERS,),
        out_specs=[by_quarter, columns, quarter_of(state)],
        scratch_shapes=[shares],
    )(skip, cols, spread, features, cotangent, reads, inside, *have, back_have[DISTANCES[1]])
    feature_grad, step_grad, sums = call(
        back_finish_kernel,
        "back_finish",
        [result, small, struct((devices, 1, LANES))],
        [by_heads, row, row, row, all_cols, all_rows, spread_quarter]
        + [by_quarter, by_quarter, tokens, by_quarter]
        + [quarter_of(1), columns, quarter_of(state)]
        + whole_shares,
        8,
        24,
        grid=(QUARTERS,),
        out_specs=[by_quarter, by_heads, all_of(devices, 1, LANES)],
        scratch_shapes=[pltpu.VMEM((length, LANES), F32)] + [pltpu.VMEM((8, LANES), F32)] * 2 + [shares],
    )(
        logits, bias, decay, skip, cols, head_rows, spread, features, cotangent, writes,
        feature_part, skip_part, rows, kept, *back_have,
    )
    write_grad, read_grad = call(
        keys_kernel,
        "keys",
        [tokens_result] * 2,
        [tokens] * 2 + [by_quarter] * 4 + whole_shares * 2 + [ANY],
        6,
        60,
        grid=(QUARTERS,),
        out_specs=[tokens] * 2,
        scratch_shapes=[pltpu.VMEM((length, 2 * state), F32)] * 2 + [shares] * 2,
    )(write_part, read_part, *pieces, *have, *back_have, step_grad)
    sums = jnp.sum(lax.all_to_all(sums, ("dp", "ctx"), 0, 0), axis=(0, 1))
    return (
        mixed[None],
        feature_grad[None],
        write_grad[None],
        read_grad[None],
        step_grad[None],
        sums[:heads],
        sums[heads : 2 * heads],
        sums[2 * heads : 3 * heads],
    )


def solution(mesh):
    by_tokens = P("dp", "ctx", None)
    by_heads = P("dp", None, "ctx")
    in_specs = (by_tokens, by_tokens, by_tokens, by_heads, P(), P(), P(), P("dp", None), by_tokens)
    out_specs = (by_tokens, by_tokens, by_tokens, by_tokens, by_heads, P(), P(), P())
    return jax.shard_map(local, mesh=mesh, in_specs=in_specs, out_specs=out_specs, check_vma=False)
```

```python
import functools

import jax
import jax.numpy as jnp
import numpy as np
from jax import lax
from jax.experimental import pallas as pl
from jax.experimental.pallas import tpu as pltpu
from jax.sharding import PartitionSpec as P

F32 = jnp.float32
BF16 = jnp.bfloat16
QUARTERS = 4
HALVES = 2
GROUP = QUARTERS * HALVES
DISTANCES = (1, 2, 3, 4, 5, 6, 7)
ARRIVALS = (0, *DISTANCES)
LANES = 128
LOG2E = 1.4426950408889634
FAR = -1e30
VMEM = pl.BlockSpec(memory_space=pltpu.VMEM)
SMEM = pl.BlockSpec(memory_space=pltpu.SMEM)
ANY = pl.BlockSpec(memory_space=pl.ANY)
WIDE_PARTS = 8
AFTER = 2
CUM, WEIGHT, FACTOR = 0, 1, 2
STRIDE, LOG = 1, 2


def iota(shape, axis):
    return lax.broadcasted_iota(jnp.int32, shape, axis)


def matmul(left, right):
    return lax.dot_general(left, right, (((1,), (0,)), ((), ())), preferred_element_type=F32)


def matmul_nt(left, right):
    return lax.dot_general(left, right, (((1,), (1,)), ((), ())), preferred_element_type=F32)


def split2(value):
    high = value.astype(BF16)
    return high, (value - high.astype(F32)).astype(BF16)


def split3(value):
    high = value.astype(BF16)
    rest = value - high.astype(F32)
    middle = rest.astype(BF16)
    return high, middle, (rest - middle.astype(F32)).astype(BF16)


def column(row):
    count = row.shape[1]
    eye = iota((count, count), 0) == iota((count, count), 1)
    return jnp.sum(jnp.where(eye, row, 0.0), axis=1, keepdims=True)


def stacked_columns(rows):
    parts = [part.astype(F32) for part in split3(rows)]
    spare = LANES - 3 * rows.shape[0]
    if spare:
        parts.append(jnp.zeros((spare, rows.shape[1]), F32))
    return jnp.concatenate(parts, axis=0).T.astype(BF16)


def spread_table(heads, head_dim):
    table = np.zeros((LANES, heads * head_dim), np.float32)
    for head in range(heads):
        for part in range(3):
            table[part * heads + head, head * head_dim : (head + 1) * head_dim] = 1.0
    return jnp.asarray(table, BF16)


def softplus(value):
    return jnp.maximum(value, 0.0) + jnp.log1p(jnp.exp(-jnp.abs(value)))


def document_at(starts_ref, position):
    total = jnp.zeros_like(position)
    for entry in range(starts_ref.shape[1]):
        total = total + (starts_ref[0, entry] <= position).astype(jnp.int32)
    return total


def group_place():
    return lax.rem(lax.axis_index("ctx"), GROUP)


def share_out(own, quarter_of_state, places, scratch):
    mine = lax.div(own, QUARTERS)
    part = scratch.shape[0] // HALVES
    for distance in range(QUARTERS):
        scratch[...] = quarter_of_state(lax.rem(own ^ distance, QUARTERS))
        for half in range(HALVES):
            rows = pl.ds(pl.multiple_of((mine ^ half) * part, part), part)
            places[half * QUARTERS + distance][...] = scratch[rows]


def states_kernel(starts, logits, bias, decay, spread_ref, features, writes, cotangent, reads, *refs):
    sends = refs[:GROUP]
    cols_out, rows_out, scratch = refs[GROUP:]
    heads, length = logits.shape
    state = writes.shape[1]
    width = features.shape[1] // QUARTERS
    part = state // HALVES
    first = lax.axis_index("ctx") * length
    own = group_place()
    stride = softplus(logits[...] + column(bias[...]))
    log_decay = stride * column(-jnp.exp(decay[...]))
    upto = jnp.where(iota((length, length), 0) <= iota((length, length), 1), 1.0, 0.0).astype(BF16)
    parts = matmul(jnp.concatenate(split3(log_decay), axis=0), upto)
    cum = parts[:heads] + parts[heads : 2 * heads] + parts[2 * heads :]
    segment = document_at(starts, first + iota((1, length), 1))
    entry = document_at(starts, jnp.full((1, 1), first - 1, jnp.int32))
    leave = document_at(starts, jnp.full((1, 1), first + length - 1, jnp.int32))
    own_last = jnp.where(segment == leave, 1.0, 0.0)
    keep_in = jnp.where(segment == entry, 1.0, 0.0)
    weight_stack = stacked_columns(own_last * jnp.exp(cum[:, length - 1 :] - cum) * stride)
    factor_stack = stacked_columns(keep_in * jnp.exp(cum))
    write_t = writes[...].astype(F32).T.astype(BF16)

    def quarter_of_state(quarter):
        cols = pl.ds(pl.multiple_of(quarter * width, LANES), width)
        high, low = split2(features[:, cols].astype(F32) * matmul(weight_stack, spread_ref[:, cols]))
        return matmul(write_t, high) + matmul(write_t, low)

    share_out(own, quarter_of_state, [send.at[0:part] for send in sends], scratch)
    read_t = reads[...].astype(F32).T.astype(BF16)

    keeps = []

    def back_quarter(quarter):
        cols = pl.ds(pl.multiple_of(quarter * width, LANES), width)
        wide = matmul(factor_stack, spread_ref[:, cols])
        keeps.append(jnp.broadcast_to(wide[length - 1 :], (8, width)))
        high, low = split2(cotangent[:, cols].astype(F32) * wide)
        return matmul(read_t, high) + matmul(read_t, low)

    share_out(own, back_quarter, [send.at[part + 8 :] for send in sends], scratch)
    for distance, send in enumerate(sends):
        send[part : part + 8] = keeps[distance % QUARTERS]
    cols_out[CUM] = stacked_columns(cum * LOG2E)
    cols_out[WEIGHT] = weight_stack
    cols_out[FACTOR] = factor_stack
    rows_out[CUM] = cum * LOG2E - jnp.log2(stride)
    rows_out[STRIDE] = stride
    rows_out[LOG] = log_decay


def inner_kernel(
    offset, last, starts, cols_ref, rows_ref, features, cotangent, writes, reads, skip, spread_ref, *refs
):
    if offset:
        before, refs = refs[0], refs[1 + WIDE_PARTS + AFTER :]
    else:
        refs = refs[AFTER:]
    inside, feature_part, skip_part, skip_wide, write_high, write_low, read_high, read_low = refs[:WIDE_PARTS]
    results = refs[WIDE_PARTS:-3]
    scores_ref, mask_ref, grad_ref = refs[-3:]
    length, width = features.shape
    heads = rows_ref.shape[1]
    here = heads // QUARTERS
    head_dim = width // here
    pair = 2 * head_dim
    step = pl.program_id(0)

    @pl.when(step == 0)
    def _():
        first = lax.axis_index("ctx") * length
        segment_row = document_at(starts, first + iota((1, length), 1))
        segment_col = document_at(starts, first + iota((length, 1), 0))
        causal = iota((length, length), 0) >= iota((length, length), 1)
        mask_ref[...] = jnp.where((segment_row == segment_col) & causal, 0.0, FAR)
        scores_ref[...] = matmul_nt(reads[...], writes[...])
        grad_ref[...] = before[...] if offset else jnp.zeros_like(grad_ref)

    skip_wide[...] = wide_skip(skip, heads, spread_ref[...])
    write_high[...], write_low[...] = split2(matmul(cols_ref[WEIGHT], spread_ref[...]) * features[...].astype(F32))
    read_high[...], read_low[...] = split2(matmul(cols_ref[FACTOR], spread_ref[...]) * cotangent[...].astype(F32))

    def one_pair(at, carry):
        cols = pl.ds(pl.multiple_of(at * pair, LANES), pair)
        feature = features[:, cols]
        grad = cotangent[:, cols]
        grad_f32 = grad.astype(F32)
        grad_t = grad_f32.T.astype(BF16)
        skip_part[:, cols] = jnp.sum(grad_f32 * feature.astype(F32), axis=0, keepdims=True)
        head = (offset + step) * here + at * 2
        lane = iota((LANES, 2 * LANES), 0)
        wanted = head + lax.div(iota((LANES, 2 * LANES), 1), LANES)
        pick = (lane == wanted) | (lane == wanted + heads) | (lane == wanted + 2 * heads)
        upper = matmul(cols_ref[CUM], jnp.where(pick, 1.0, 0.0).astype(BF16))
        second = iota((LANES, pair), 1) >= head_dim
        back = [None, None]
        for block in range(length // LANES):
            rows = slice(block * LANES, (block + 1) * LANES)
            reach = (block + 1) * LANES
            values = []
            for side in range(2):
                high_row = jnp.concatenate([upper[rows, side * LANES : (side + 1) * LANES]] * (block + 1), axis=1)
                low_row = rows_ref[CUM, pl.ds(head + side, 1), :][:, 0:reach]
                weight = jnp.exp2(high_row - low_row + mask_ref[rows, 0:reach])
                pieces = split2(weight * scores_ref[rows, 0:reach])
                values.append(matmul(jnp.concatenate(pieces, axis=1), jnp.concatenate([feature[0:reach]] * 2, axis=0)))
                grad_rows = grad_t[side * head_dim : (side + 1) * head_dim, rows]
                found = matmul(jnp.concatenate([grad_rows] * 2, axis=1), jnp.concatenate(pieces, axis=0))
                if block:
                    found = jnp.concatenate([found[:, : reach - LANES] + back[side], found[:, reach - LANES :]], axis=1)
                back[side] = found
                only = jnp.where(second == (side == 1), grad_f32[rows], 0.0).astype(BF16)
                grad_ref[rows, 0:reach] += matmul_nt(only, feature[0:reach]) * weight
            inside[rows, cols] = jnp.where(second, values[1], values[0])
        feature_part[:, cols] = jnp.concatenate(back, axis=0).T
        return carry

    lax.fori_loop(0, here // 2, one_pair, 0)

    @pl.when(step == pl.num_programs(0) - 1)
    def _():
        score_grad = grad_ref[...]
        if last:
            write_part, read_part = results
            high, low = split2(score_grad)
            read_part[...] = matmul(high, writes[...]) + matmul(low, writes[...])
            high, low = split2(score_grad.T)
            write_part[...] = matmul(high, reads[...]) + matmul(low, reads[...])
        else:
            results[0][...] = score_grad


def in_order(refs, scratch, back=False):
    own = group_place()
    rows = scratch.shape[1]
    for distance, ref in zip(ARRIVALS, refs):
        first = ref.shape[0] - rows if back else 0
        scratch[own ^ distance] = ref[first : first + rows]


def group_kernel(part, *refs):
    keeps, came, back_came = refs[-3:]
    sums = refs[GROUP + 1 : -3]
    up, down = sums[0], sums[-1]
    in_order(refs[:GROUP], came)
    total = came[0, 0:part]
    keep = came[0, part:]
    for j in range(1, GROUP):
        total = total * came[j, part : part + 1] + came[j, 0:part]
        keep = keep * came[j, part:]
    up[0:part] = total
    up[part:] = keep
    for j in range(GROUP):
        keeps[j : j + 1] = came[j, part : part + 1]
    in_order(refs[:GROUP], back_came, back=True)

    def downward():
        total = back_came[GROUP - 1]
        for j in reversed(range(GROUP - 1)):
            total = total * keeps[j : j + 1] + back_came[j]
        down[0:part] = total
        down[part:] = keep

    if len(sums) == 1:
        pl.when(lax.axis_index("ctx") >= GROUP)(downward)
    else:
        downward()


def arrived(part, came):
    total, keep = came[0][0:part], came[0][part : part + 1]
    for ref in came[1:]:
        total = total + keep * ref[0:part]
        keep = keep * ref[part : part + 1]
    return total, keep


def link_kernel(part, own, *refs):
    total, keep = arrived(part, refs[:-1])
    refs[-1][0:part] = own[0:part] + own[part : part + 1] * total
    refs[-1][part:] = own[part:] * keep


def in_upper():
    return lax.axis_index("ctx") >= GROUP


def spread_kernel(part, two, second, *refs):
    keeps = refs[GROUP]
    arrivals = refs[GROUP + 1 : -3 - GROUP]
    outs = refs[-3 - GROUP : -3]
    came, back_came, give = refs[-3:]

    def start():
        return arrived(part, arrivals)[0] if arrivals else jnp.zeros(give.shape[1:], F32)

    def forward():
        in_order(refs[:GROUP], came)
        total = start()
        for j in range(GROUP):
            give[j] = total
            if j < GROUP - 1:
                total = total * keeps[j : j + 1] + came[j, 0:part]

    def backward():
        in_order(refs[:GROUP], back_came, back=True)
        total = start()
        for j in reversed(range(GROUP)):
            give[j] = total
            if j > 0:
                total = total * keeps[j : j + 1] + back_came[j]

    if two:
        upper = in_upper()
        pl.when(upper == second)(forward)
        pl.when(upper != second)(backward)
    else:
        (backward if second else forward)()
    own = group_place()
    for distance, out in enumerate(outs):
        out[...] = give[own ^ distance]


def both_sets(two, refs, have, back_have):
    sets = refs[:GROUP], refs[GROUP : 2 * GROUP]

    def straight():
        in_order(sets[0], have)
        in_order(sets[1], back_have)

    def crossed():
        in_order(sets[1], have)
        in_order(sets[0], back_have)

    if two:
        upper = in_upper()
        pl.when(upper)(crossed)
        pl.when(jnp.logical_not(upper))(straight)
    else:
        straight()


def head_sums(ref, value, spread):
    high, low = split2(value)
    ref[...] += matmul_nt(high, spread) + matmul_nt(low, spread)


def wide_skip(skip, heads, spread):
    stack = stacked_columns(jnp.broadcast_to(column(skip[...]), (heads, LANES)))
    return matmul(stack[0:16], spread)[0:1]


def quarter_rows(have, step):
    return jnp.concatenate([have[half * QUARTERS + step] for half in range(HALVES)], axis=0)


def summed_onward(value):
    count, length = value.shape
    onward = jnp.where(iota((length, length), 0) >= iota((length, length), 1), 1.0, 0.0).astype(BF16)
    parts = matmul(jnp.concatenate(split3(value), axis=0), onward)
    return parts[:count] + parts[count : 2 * count] + parts[2 * count :]


def finish_kernel(
    two, logits, bias, decay, cols_ref, rows_ref, spread_ref, features, cotangent, writes, reads,
    inside, feature_part, skip_part, skip_wide, *refs,
):
    mixed, feature_grad, step_grad, sums, row_acc, col_acc, last_acc, skip_acc, have, back_have = refs[2 * GROUP :]
    heads, length = logits.shape
    state = writes.shape[1]
    width = features.shape[1]
    step = pl.program_id(0)

    @pl.when(step == 0)
    def _():
        for ref in (row_acc, col_acc, last_acc, skip_acc):
            ref[...] = jnp.zeros_like(ref)
        both_sets(two, refs, have, back_have)

    spread = spread_ref[...]
    feature = features[...].astype(F32)
    grad = cotangent[...].astype(F32)
    factor = matmul(cols_ref[FACTOR], spread)
    entering = quarter_rows(have, step)
    stack = jnp.concatenate(split2(entering), axis=0)
    total = inside[...] + factor * matmul(jnp.concatenate([reads[...]] * 2, axis=1), stack)
    mixed[...] = (total + skip_wide[...] * feature).astype(BF16)
    head_sums(row_acc, grad * total, spread)
    returning = quarter_rows(back_have, step)
    stack = jnp.concatenate(split2(returning), axis=0)
    carried = matmul(cols_ref[WEIGHT], spread) * matmul(jnp.concatenate([writes[...]] * 2, axis=1), stack)
    total = feature_part[...] + carried
    feature_grad[...] = (total + skip_wide[...] * grad).astype(BF16)
    head_sums(col_acc, feature * total, spread)
    leaving = jnp.sum((returning * entering).reshape(state // 8, 8, width), axis=0) * factor[length - 1 :]
    leaving = leaving + jnp.sum((feature * carried).reshape(length // 8, 8, width), axis=0)
    head_sums(last_acc, leaving, spread)
    head_sums(skip_acc, jnp.broadcast_to(skip_part[...], (8, width)), spread)

    @pl.when(step == QUARTERS - 1)
    def _():
        cols = col_acc[...].T[:heads]
        last = column(jnp.sum(last_acc[...], axis=0, keepdims=True))[:heads]
        log_grad = last + summed_onward(row_acc[...].T[:heads] - cols)
        slope = 1.0 / (1.0 + jnp.exp(-(logits[...] + column(bias[...]))))
        step_value = (cols / rows_ref[STRIDE] + column(-jnp.exp(decay[...])) * log_grad) * slope
        step_grad[...] = step_value
        bias_sum = jnp.sum(step_value, axis=1, keepdims=True)
        decay_sum = jnp.sum(log_grad * rows_ref[LOG], axis=1, keepdims=True)
        skip_sum = column(skip_acc[0:1])[:heads]
        spare = jnp.zeros((LANES - 3 * heads, 1), F32)
        table = jnp.concatenate([bias_sum, decay_sum, skip_sum, spare], axis=0)
        eye = iota((LANES, LANES), 0) == iota((LANES, LANES), 1)
        table = jnp.sum(jnp.where(eye, table, 0.0), axis=0, keepdims=True)
        sums[...] = jnp.broadcast_to(table[None], sums.shape)


def keys_kernel(two, write_part, read_part, write_high, write_low, read_high, read_low, *refs):
    write_grad, read_grad, write_acc, read_acc, have, back_have = refs[2 * GROUP + 1 :]
    state = write_part.shape[1]
    step = pl.program_id(0)

    @pl.when(step == 0)
    def _():
        write_acc[...] = jnp.zeros_like(write_acc)
        read_acc[...] = jnp.zeros_like(read_acc)
        both_sets(two, refs, have, back_have)

    for states, high, low, acc in (
        (have, read_high, read_low, read_acc),
        (back_have, write_high, write_low, write_acc),
    ):
        stack = jnp.concatenate(split2(quarter_rows(states, step)), axis=0)
        acc[...] += matmul_nt(high[...], stack) + matmul_nt(low[...], stack)

    @pl.when(step == QUARTERS - 1)
    def _():
        write_grad[...] = (write_part[...] + write_acc[:, :state] + write_acc[:, state:]).astype(BF16)
        read_grad[...] = (read_part[...] + read_acc[:, :state] + read_acc[:, state:]).astype(BF16)


def call(kernel, name, outs, in_specs, work, mib, **more):
    return pl.pallas_call(
        kernel,
        out_shape=outs,
        in_specs=in_specs,
        out_specs=more.pop("out_specs", [VMEM] * len(outs)),
        compiler_params=pltpu.CompilerParams(vmem_limit_bytes=mib * 2**20),
        cost_estimate=pl.CostEstimate(flops=work * 10**9, bytes_accessed=10**6, transcendentals=0),
        name=name,
        **more,
    )


def struct(shape, dtype=F32):
    return jax.ShapeDtypeStruct(shape, dtype)


def local(
    features, write_keys, read_queries, step_logits, step_bias, decay_log, skip_gain, doc_starts, out_grad
):
    features, writes, reads, logits, cotangent = (
        features[0], write_keys[0], read_queries[0], step_logits[0], out_grad[0]
    )
    length, wide = features.shape
    heads = logits.shape[0]
    state = writes.shape[1]
    head_dim = wide // heads
    width = wide // QUARTERS
    part = state // HALVES
    bias, decay, skip = step_bias[None], decay_log[None], skip_gain[None]
    blocks, members = lax.axis_size("ctx"), lax.axis_size("dp")
    spread = spread_table(heads, head_dim)

    def exchange(value, distance):
        return lax.ppermute(value, "ctx", [(k, k ^ distance) for k in range(blocks)])

    def swap(values):
        return [values[0]] + [exchange(values[d], d) for d in DISTANCES]

    def shift(value, distance):
        pairs = [(k, k + distance) for k in range(blocks) if 0 <= k + distance < blocks]
        return lax.ppermute(value, "ctx", pairs)

    def scan(own, sign):
        came, near, reach = [], own, 1
        while reach < blocks // GROUP:
            came.append(shift(near, sign * GROUP * reach))
            reach *= 2
            if reach < blocks // GROUP:
                near = call(
                    functools.partial(link_kernel, part), "link", [group_sum], [VMEM] * (1 + len(came)), 1, 8
                )(own, *came)[0]
        return came

    def all_of(*shape):
        return pl.BlockSpec(shape, lambda step: (0,) * len(shape))

    def quarter_of(rows, offset=0):
        return pl.BlockSpec((rows, width), lambda step: (0, step + offset))

    small = struct((heads, length))
    result = struct((length, wide), BF16)
    tokens_result = struct((length, state), BF16)
    group_sum = struct((part + 8, width))
    tokens = all_of(length, state)
    columns = all_of(length, LANES)
    by_heads = all_of(heads, length)
    all_cols, all_rows = all_of(3, length, LANES), all_of(3, heads, length)
    row = all_of(1, heads)
    by_quarter = quarter_of(length)
    spread_quarter = quarter_of(LANES)
    shares = pltpu.VMEM((GROUP, part, width), F32)
    long_shares = pltpu.VMEM((GROUP, part + 8, width), F32)

    share = struct((part, width))
    out = call(
        states_kernel,
        "states",
        [struct((2 * part + 8, width))] * GROUP + [struct((3, length, LANES), BF16), struct((3, heads, length))],
        [SMEM] + [VMEM] * 8,
        4,
        60,
        scratch_shapes=[pltpu.VMEM((state, width), F32)],
    )(doc_starts, logits, bias, decay, spread, features, writes, cotangent, reads)
    came = swap(out[:GROUP])
    cols, head_rows = out[GROUP:]

    wide_part, wide_piece = struct((length, wide)), struct((length, wide), BF16)
    wide_parts = [wide_part] * 2 + [struct((1, wide))] * 2 + [wide_piece] * 4
    token_part = struct((length, state))
    square = all_of(length, length)
    inner_args = (doc_starts, cols, head_rows, features, cotangent, writes, reads, skip, spread)

    def inner(offset, count, begun, after):
        mine, thin = quarter_of(length, offset), quarter_of(1, offset)
        last = offset + count == QUARTERS
        n_args = len(inner_args) + 1
        return call(
            functools.partial(inner_kernel, offset, last),
            "inner_" + str(offset),
            wide_parts + ([token_part] * 2 if last else [struct((length, length))]),
            [SMEM, all_cols, all_rows, mine, mine, tokens, tokens, row, quarter_of(LANES, offset)]
            + ([square] + [ANY] * WIDE_PARTS if offset else [])
            + [ANY] * AFTER,
            5 * count,
            24,
            grid=(count,),
            out_specs=[mine, mine, thin, thin] + [mine] * 4 + ([tokens] * 2 if last else [square]),
            scratch_shapes=[pltpu.VMEM((length, length), F32)] * 3,
            input_output_aliases={n_args + at: at for at in range(WIDE_PARTS)} if offset else {},
        )(*inner_args, *begun, *after)

    inside, feature_part, skip_part, skip_wide, *pieces, write_part, read_part = inner(
        0, QUARTERS, [], came[1 : 1 + AFTER]
    )
    two = blocks == 2 * GROUP
    *group_sums, keeps = call(
        functools.partial(group_kernel, part),
        "group",
        [group_sum] * (1 if two else 2) + [struct((GROUP, width))],
        [VMEM] * GROUP + [ANY],
        2,
        12,
        scratch_shapes=[long_shares, shares],
    )(*came, write_part)
    if two:
        near, far = [], [exchange(group_sums[0], GROUP)]
    else:
        near, far = scan(group_sums[0], 1), scan(group_sums[1], -1)

    def give_back(second, arrivals):
        return swap(
            call(
                functools.partial(spread_kernel, part, two, second),
                "spread",
                [share] * GROUP,
                [VMEM] * (GROUP + 1 + len(arrivals)),
                2,
                12,
                scratch_shapes=[long_shares, shares, shares],
            )(*came, keeps, *arrivals)
        )

    sets = [*give_back(False, near), *give_back(True, far)]
    devices = blocks * members
    whole_shares = [all_of(part, width)] * GROUP
    mixed, feature_grad, step_grad, sums = call(
        functools.partial(finish_kernel, two),
        "finish",
        [result, result, small, struct((devices, 1, LANES))],
        [by_heads, row, row, all_cols, all_rows, spread_quarter, by_quarter, by_quarter, tokens, tokens]
        + [by_quarter] * 2
        + [quarter_of(1)] * 2
        + whole_shares * 2,
        8,
        24,
        grid=(QUARTERS,),
        out_specs=[by_quarter, by_quarter, by_heads, all_of(devices, 1, LANES)],
        scratch_shapes=[pltpu.VMEM((length, LANES), F32)] * 2 + [pltpu.VMEM((8, LANES), F32)] * 2 + [shares] * 2,
    )(
        logits, bias, decay, cols, head_rows, spread, features, cotangent, writes, reads,
        inside, feature_part, skip_part, skip_wide, *sets,
    )
    write_grad, read_grad = call(
        functools.partial(keys_kernel, two),
        "keys",
        [tokens_result] * 2,
        [tokens] * 2 + [by_quarter] * 4 + whole_shares * 2 + [ANY],
        6,
        60,
        grid=(QUARTERS,),
        out_specs=[tokens] * 2,
        scratch_shapes=[pltpu.VMEM((length, 2 * state), F32)] * 2 + [shares] * 2,
    )(write_part, read_part, *pieces, *sets, step_grad)
    sums = jnp.sum(lax.all_to_all(sums, ("dp", "ctx"), 0, 0), axis=(0, 1))
    return (
        mixed[None],
        feature_grad[None],
        write_grad[None],
        read_grad[None],
        step_grad[None],
        sums[:heads],
        sums[heads : 2 * heads],
        sums[2 * heads : 3 * heads],
    )


def solution(mesh):
    by_tokens = P("dp", "ctx", None)
    by_heads = P("dp", None, "ctx")
    in_specs = (by_tokens, by_tokens, by_tokens, by_heads, P(), P(), P(), P("dp", None), by_tokens)
    out_specs = (by_tokens, by_tokens, by_tokens, by_tokens, by_heads, P(), P(), P())
    return jax.shard_map(local, mesh=mesh, in_specs=in_specs, out_specs=out_specs, check_vma=False)
```

```python
import functools

import jax
import jax.numpy as jnp
import numpy as np
from jax import lax
from jax.experimental import pallas as pl
from jax.experimental.pallas import tpu as pltpu
from jax.sharding import PartitionSpec as P

F32 = jnp.float32
BF16 = jnp.bfloat16
QUARTERS = 4
HALVES = 2
GROUP = QUARTERS * HALVES
DISTANCES = (1, 2, 3, 4, 5, 6, 7)
ARRIVALS = (0, *DISTANCES)
LANES = 128
LOG2E = 1.4426950408889634
FAR = -1e30
VMEM = pl.BlockSpec(memory_space=pltpu.VMEM)
SMEM = pl.BlockSpec(memory_space=pltpu.SMEM)
ANY = pl.BlockSpec(memory_space=pl.ANY)
WIDE_PARTS = 8
AFTER = 2
CUM, WEIGHT, FACTOR = 0, 1, 2
STRIDE, LOG = 1, 2


def iota(shape, axis):
    return lax.broadcasted_iota(jnp.int32, shape, axis)


def matmul(left, right):
    return lax.dot_general(left, right, (((1,), (0,)), ((), ())), preferred_element_type=F32)


def matmul_nt(left, right):
    return lax.dot_general(left, right, (((1,), (1,)), ((), ())), preferred_element_type=F32)


def split2(value):
    high = value.astype(BF16)
    return high, (value - high.astype(F32)).astype(BF16)


def split3(value):
    high = value.astype(BF16)
    rest = value - high.astype(F32)
    middle = rest.astype(BF16)
    return high, middle, (rest - middle.astype(F32)).astype(BF16)


def column(row):
    count = row.shape[1]
    eye = iota((count, count), 0) == iota((count, count), 1)
    return jnp.sum(jnp.where(eye, row, 0.0), axis=1, keepdims=True)


def stacked_columns(rows):
    parts = [part.astype(F32) for part in split3(rows)]
    spare = LANES - 3 * rows.shape[0]
    if spare:
        parts.append(jnp.zeros((spare, rows.shape[1]), F32))
    return jnp.concatenate(parts, axis=0).T.astype(BF16)


def spread_table(heads, head_dim):
    table = np.zeros((LANES, heads * head_dim), np.float32)
    for head in range(heads):
        for part in range(3):
            table[part * heads + head, head * head_dim : (head + 1) * head_dim] = 1.0
    return jnp.asarray(table, BF16)


def softplus(value):
    return jnp.maximum(value, 0.0) + jnp.log1p(jnp.exp(-jnp.abs(value)))


def document_at(starts_ref, position):
    total = jnp.zeros_like(position)
    for entry in range(starts_ref.shape[1]):
        total = total + (starts_ref[0, entry] <= position).astype(jnp.int32)
    return total


def group_place():
    return lax.rem(lax.axis_index("ctx"), GROUP)


def share_out(own, quarter_of_state, places, scratch):
    mine = lax.div(own, QUARTERS)
    part = scratch.shape[0] // HALVES
    for distance in range(QUARTERS):
        scratch[...] = quarter_of_state(lax.rem(own ^ distance, QUARTERS))
        for half in range(HALVES):
            rows = pl.ds(pl.multiple_of((mine ^ half) * part, part), part)
            places[half * QUARTERS + distance][...] = scratch[rows]


def states_kernel(starts, logits, bias, decay, spread_ref, features, writes, cotangent, reads, *refs):
    sends = refs[:GROUP]
    cols_out, rows_out, scratch = refs[GROUP:]
    heads, length = logits.shape
    state = writes.shape[1]
    width = features.shape[1] // QUARTERS
    part = state // HALVES
    first = lax.axis_index("ctx") * length
    own = group_place()
    stride = softplus(logits[...] + column(bias[...]))
    log_decay = stride * column(-jnp.exp(decay[...]))
    upto = jnp.where(iota((length, length), 0) <= iota((length, length), 1), 1.0, 0.0).astype(BF16)
    parts = matmul(jnp.concatenate(split3(log_decay), axis=0), upto)
    cum = parts[:heads] + parts[heads : 2 * heads] + parts[2 * heads :]
    segment = document_at(starts, first + iota((1, length), 1))
    entry = document_at(starts, jnp.full((1, 1), first - 1, jnp.int32))
    leave = document_at(starts, jnp.full((1, 1), first + length - 1, jnp.int32))
    own_last = jnp.where(segment == leave, 1.0, 0.0)
    keep_in = jnp.where(segment == entry, 1.0, 0.0)
    weight_stack = stacked_columns(own_last * jnp.exp(cum[:, length - 1 :] - cum) * stride)
    factor_stack = stacked_columns(keep_in * jnp.exp(cum))
    write_t = writes[...].astype(F32).T.astype(BF16)

    def quarter_of_state(quarter):
        cols = pl.ds(pl.multiple_of(quarter * width, LANES), width)
        high, low = split2(features[:, cols].astype(F32) * matmul(weight_stack, spread_ref[:, cols]))
        return matmul(write_t, high) + matmul(write_t, low)

    share_out(own, quarter_of_state, [send.at[0:part] for send in sends], scratch)
    read_t = reads[...].astype(F32).T.astype(BF16)

    keeps = []

    def back_quarter(quarter):
        cols = pl.ds(pl.multiple_of(quarter * width, LANES), width)
        wide = matmul(factor_stack, spread_ref[:, cols])
        keeps.append(jnp.broadcast_to(wide[length - 1 :], (8, width)))
        high, low = split2(cotangent[:, cols].astype(F32) * wide)
        return matmul(read_t, high) + matmul(read_t, low)

    share_out(own, back_quarter, [send.at[part + 8 :] for send in sends], scratch)
    for distance, send in enumerate(sends):
        send[part : part + 8] = keeps[distance % QUARTERS]
    cols_out[CUM] = stacked_columns(cum * LOG2E)
    cols_out[WEIGHT] = weight_stack
    cols_out[FACTOR] = factor_stack
    rows_out[CUM] = cum * LOG2E - jnp.log2(stride)
    rows_out[STRIDE] = stride
    rows_out[LOG] = log_decay


def inner_kernel(
    offset, last, starts, cols_ref, rows_ref, features, cotangent, writes, reads, skip, spread_ref, *refs
):
    if offset:
        before, refs = refs[0], refs[1 + WIDE_PARTS + AFTER :]
    else:
        refs = refs[AFTER:]
    inside, feature_part, skip_part, skip_wide, write_high, write_low, read_high, read_low = refs[:WIDE_PARTS]
    results = refs[WIDE_PARTS:-3]
    scores_ref, mask_ref, grad_ref = refs[-3:]
    length, width = features.shape
    heads = rows_ref.shape[1]
    here = heads // QUARTERS
    head_dim = width // here
    pair = 2 * head_dim
    step = pl.program_id(0)

    @pl.when(step == 0)
    def _():
        first = lax.axis_index("ctx") * length
        segment_row = document_at(starts, first + iota((1, length), 1))
        segment_col = document_at(starts, first + iota((length, 1), 0))
        causal = iota((length, length), 0) >= iota((length, length), 1)
        mask_ref[...] = jnp.where((segment_row == segment_col) & causal, 0.0, FAR)
        scores_ref[...] = matmul_nt(reads[...], writes[...])
        grad_ref[...] = before[...] if offset else jnp.zeros_like(grad_ref)

    skip_wide[...] = wide_skip(skip, heads, spread_ref[...])
    write_high[...], write_low[...] = split2(matmul(cols_ref[WEIGHT], spread_ref[...]) * features[...].astype(F32))
    read_high[...], read_low[...] = split2(matmul(cols_ref[FACTOR], spread_ref[...]) * cotangent[...].astype(F32))

    def one_pair(at, carry):
        cols = pl.ds(pl.multiple_of(at * pair, LANES), pair)
        feature = features[:, cols]
        grad = cotangent[:, cols]
        grad_f32 = grad.astype(F32)
        grad_t = grad_f32.T.astype(BF16)
        skip_part[:, cols] = jnp.sum(grad_f32 * feature.astype(F32), axis=0, keepdims=True)
        head = (offset + step) * here + at * 2
        lane = iota((LANES, 2 * LANES), 0)
        wanted = head + lax.div(iota((LANES, 2 * LANES), 1), LANES)
        pick = (lane == wanted) | (lane == wanted + heads) | (lane == wanted + 2 * heads)
        upper = matmul(cols_ref[CUM], jnp.where(pick, 1.0, 0.0).astype(BF16))
        second = iota((LANES, pair), 1) >= head_dim
        back = [None, None]
        for block in range(length // LANES):
            rows = slice(block * LANES, (block + 1) * LANES)
            reach = (block + 1) * LANES
            values = []
            for side in range(2):
                high_row = jnp.concatenate([upper[rows, side * LANES : (side + 1) * LANES]] * (block + 1), axis=1)
                low_row = rows_ref[CUM, pl.ds(head + side, 1), :][:, 0:reach]
                weight = jnp.exp2(high_row - low_row + mask_ref[rows, 0:reach])
                pieces = split2(weight * scores_ref[rows, 0:reach])
                values.append(matmul(jnp.concatenate(pieces, axis=1), jnp.concatenate([feature[0:reach]] * 2, axis=0)))
                grad_rows = grad_t[side * head_dim : (side + 1) * head_dim, rows]
                found = matmul(jnp.concatenate([grad_rows] * 2, axis=1), jnp.concatenate(pieces, axis=0))
                if block:
                    found = jnp.concatenate([found[:, : reach - LANES] + back[side], found[:, reach - LANES :]], axis=1)
                back[side] = found
                only = jnp.where(second == (side == 1), grad_f32[rows], 0.0).astype(BF16)
                grad_ref[rows, 0:reach] += matmul_nt(only, feature[0:reach]) * weight
            inside[rows, cols] = jnp.where(second, values[1], values[0])
        feature_part[:, cols] = jnp.concatenate(back, axis=0).T
        return carry

    lax.fori_loop(0, here // 2, one_pair, 0)

    @pl.when(step == pl.num_programs(0) - 1)
    def _():
        score_grad = grad_ref[...]
        if last:
            write_part, read_part = results
            high, low = split2(score_grad)
            read_part[...] = matmul(high, writes[...]) + matmul(low, writes[...])
            high, low = split2(score_grad.T)
            write_part[...] = matmul(high, reads[...]) + matmul(low, reads[...])
        else:
            results[0][...] = score_grad


def in_order(refs, scratch, back=False):
    own = group_place()
    rows = scratch.shape[1]
    for distance, ref in zip(ARRIVALS, refs):
        first = ref.shape[0] - rows if back else 0
        scratch[own ^ distance] = ref[first : first + rows]


def group_kernel(part, *refs):
    keeps, came, back_came = refs[-3:]
    sums = refs[GROUP + 1 : -3]
    up, down = sums[0], sums[-1]
    in_order(refs[:GROUP], came)
    total = came[0, 0:part]
    keep = came[0, part:]
    for j in range(1, GROUP):
        total = total * came[j, part : part + 1] + came[j, 0:part]
        keep = keep * came[j, part:]
    up[0:part] = total
    up[part:] = keep
    for j in range(GROUP):
        keeps[j : j + 1] = came[j, part : part + 1]
    in_order(refs[:GROUP], back_came, back=True)

    def downward():
        total = back_came[GROUP - 1]
        for j in reversed(range(GROUP - 1)):
            total = total * keeps[j : j + 1] + back_came[j]
        down[0:part] = total
        down[part:] = keep

    if len(sums) == 1:
        pl.when(lax.axis_index("ctx") >= GROUP)(downward)
    else:
        downward()


def arrived(part, came):
    total, keep = came[0][0:part], came[0][part : part + 1]
    for ref in came[1:]:
        total = total + keep * ref[0:part]
        keep = keep * ref[part : part + 1]
    return total, keep


def link_kernel(part, own, *refs):
    total, keep = arrived(part, refs[:-1])
    refs[-1][0:part] = own[0:part] + own[part : part + 1] * total
    refs[-1][part:] = own[part:] * keep


def in_upper():
    return lax.axis_index("ctx") >= GROUP


def spread_kernel(part, two, second, *refs):
    keeps = refs[GROUP]
    arrivals = refs[GROUP + 1 : -3 - GROUP]
    outs = refs[-3 - GROUP : -3]
    came, back_came, give = refs[-3:]

    def start():
        return arrived(part, arrivals)[0] if arrivals else jnp.zeros(give.shape[1:], F32)

    def forward():
        in_order(refs[:GROUP], came)
        total = start()
        for j in range(GROUP):
            give[j] = total
            if j < GROUP - 1:
                total = total * keeps[j : j + 1] + came[j, 0:part]

    def backward():
        in_order(refs[:GROUP], back_came, back=True)
        total = start()
        for j in reversed(range(GROUP)):
            give[j] = total
            if j > 0:
                total = total * keeps[j : j + 1] + back_came[j]

    if two:
        upper = in_upper()
        pl.when(upper == second)(forward)
        pl.when(upper != second)(backward)
    else:
        (backward if second else forward)()
    own = group_place()
    for distance, out in enumerate(outs):
        out[...] = give[own ^ distance]


def both_sets(two, refs, have, back_have):
    sets = refs[:GROUP], refs[GROUP : 2 * GROUP]

    def straight():
        in_order(sets[0], have)
        in_order(sets[1], back_have)

    def crossed():
        in_order(sets[1], have)
        in_order(sets[0], back_have)

    if two:
        upper = in_upper()
        pl.when(upper)(crossed)
        pl.when(jnp.logical_not(upper))(straight)
    else:
        straight()


def head_sums(ref, value, spread):
    high, low = split2(value)
    ref[...] += matmul_nt(high, spread) + matmul_nt(low, spread)


def wide_skip(skip, heads, spread):
    stack = stacked_columns(jnp.broadcast_to(column(skip[...]), (heads, LANES)))
    return matmul(stack[0:16], spread)[0:1]


def quarter_rows(have, step):
    return jnp.concatenate([have[half * QUARTERS + step] for half in range(HALVES)], axis=0)


def summed_onward(value):
    count, length = value.shape
    onward = jnp.where(iota((length, length), 0) >= iota((length, length), 1), 1.0, 0.0).astype(BF16)
    parts = matmul(jnp.concatenate(split3(value), axis=0), onward)
    return parts[:count] + parts[count : 2 * count] + parts[2 * count :]


def finish_kernel(
    two, logits, bias, decay, cols_ref, rows_ref, spread_ref, features, cotangent, writes, reads,
    inside, feature_part, skip_part, skip_wide, *refs,
):
    mixed, feature_grad, step_grad, sums, row_acc, col_acc, last_acc, skip_acc, have, back_have = refs[2 * GROUP :]
    heads, length = logits.shape
    state = writes.shape[1]
    width = features.shape[1]
    step = pl.program_id(0)

    @pl.when(step == 0)
    def _():
        for ref in (row_acc, col_acc, last_acc, skip_acc):
            ref[...] = jnp.zeros_like(ref)
        both_sets(two, refs, have, back_have)

    spread = spread_ref[...]
    feature = features[...].astype(F32)
    grad = cotangent[...].astype(F32)
    factor = matmul(cols_ref[FACTOR], spread)
    entering = quarter_rows(have, step)
    stack = jnp.concatenate(split2(entering), axis=0)
    total = inside[...] + factor * matmul(jnp.concatenate([reads[...]] * 2, axis=1), stack)
    mixed[...] = (total + skip_wide[...] * feature).astype(BF16)
    head_sums(row_acc, grad * total, spread)
    returning = quarter_rows(back_have, step)
    stack = jnp.concatenate(split2(returning), axis=0)
    carried = matmul(cols_ref[WEIGHT], spread) * matmul(jnp.concatenate([writes[...]] * 2, axis=1), stack)
    total = feature_part[...] + carried
    feature_grad[...] = (total + skip_wide[...] * grad).astype(BF16)
    head_sums(col_acc, feature * total, spread)
    leaving = jnp.sum((returning * entering).reshape(state // 8, 8, width), axis=0) * factor[length - 1 :]
    leaving = leaving + jnp.sum((feature * carried).reshape(length // 8, 8, width), axis=0)
    head_sums(last_acc, leaving, spread)
    head_sums(skip_acc, jnp.broadcast_to(skip_part[...], (8, width)), spread)

    @pl.when(step == QUARTERS - 1)
    def _():
        cols = col_acc[...].T[:heads]
        last = column(jnp.sum(last_acc[...], axis=0, keepdims=True))[:heads]
        log_grad = last + summed_onward(row_acc[...].T[:heads] - cols)
        slope = 1.0 / (1.0 + jnp.exp(-(logits[...] + column(bias[...]))))
        step_value = (cols / rows_ref[STRIDE] + column(-jnp.exp(decay[...])) * log_grad) * slope
        step_grad[...] = step_value
        bias_sum = jnp.sum(step_value, axis=1, keepdims=True)
        decay_sum = jnp.sum(log_grad * rows_ref[LOG], axis=1, keepdims=True)
        skip_sum = column(skip_acc[0:1])[:heads]
        spare = jnp.zeros((LANES - 3 * heads, 1), F32)
        table = jnp.concatenate([bias_sum, decay_sum, skip_sum, spare], axis=0)
        eye = iota((LANES, LANES), 0) == iota((LANES, LANES), 1)
        table = jnp.sum(jnp.where(eye, table, 0.0), axis=0, keepdims=True)
        sums[...] = jnp.broadcast_to(table[None], sums.shape)


def keys_kernel(two, write_part, read_part, write_high, write_low, read_high, read_low, *refs):
    write_grad, read_grad, write_acc, read_acc, have, back_have = refs[2 * GROUP + 1 :]
    state = write_part.shape[1]
    step = pl.program_id(0)

    @pl.when(step == 0)
    def _():
        write_acc[...] = jnp.zeros_like(write_acc)
        read_acc[...] = jnp.zeros_like(read_acc)
        both_sets(two, refs, have, back_have)

    for states, high, low, acc in (
        (have, read_high, read_low, read_acc),
        (back_have, write_high, write_low, write_acc),
    ):
        stack = jnp.concatenate(split2(quarter_rows(states, step)), axis=0)
        acc[...] += matmul_nt(high[...], stack) + matmul_nt(low[...], stack)

    @pl.when(step == QUARTERS - 1)
    def _():
        write_grad[...] = (write_part[...] + write_acc[:, :state] + write_acc[:, state:]).astype(BF16)
        read_grad[...] = (read_part[...] + read_acc[:, :state] + read_acc[:, state:]).astype(BF16)


def call(kernel, name, outs, in_specs, work, mib, **more):
    return pl.pallas_call(
        kernel,
        out_shape=outs,
        in_specs=in_specs,
        out_specs=more.pop("out_specs", [VMEM] * len(outs)),
        compiler_params=pltpu.CompilerParams(vmem_limit_bytes=mib * 2**20),
        cost_estimate=pl.CostEstimate(flops=work * 10**9, bytes_accessed=10**6, transcendentals=0),
        name=name,
        **more,
    )


def struct(shape, dtype=F32):
    return jax.ShapeDtypeStruct(shape, dtype)


def local(
    features, write_keys, read_queries, step_logits, step_bias, decay_log, skip_gain, doc_starts, out_grad
):
    features, writes, reads, logits, cotangent = (
        features[0], write_keys[0], read_queries[0], step_logits[0], out_grad[0]
    )
    length, wide = features.shape
    heads = logits.shape[0]
    state = writes.shape[1]
    head_dim = wide // heads
    width = wide // QUARTERS
    part = state // HALVES
    bias, decay, skip = step_bias[None], decay_log[None], skip_gain[None]
    blocks, members = lax.axis_size("ctx"), lax.axis_size("dp")
    spread = spread_table(heads, head_dim)

    def exchange(value, distance):
        return lax.ppermute(value, "ctx", [(k, k ^ distance) for k in range(blocks)])

    def swap(values):
        return [values[0]] + [exchange(values[d], d) for d in DISTANCES]

    def shift(value, distance):
        pairs = [(k, k + distance) for k in range(blocks) if 0 <= k + distance < blocks]
        return lax.ppermute(value, "ctx", pairs)

    def scan(own, sign):
        came, near, reach = [], own, 1
        while reach < blocks // GROUP:
            came.append(shift(near, sign * GROUP * reach))
            reach *= 2
            if reach < blocks // GROUP:
                near = call(
                    functools.partial(link_kernel, part), "link", [group_sum], [VMEM] * (1 + len(came)), 1, 8
                )(own, *came)[0]
        return came

    def all_of(*shape):
        return pl.BlockSpec(shape, lambda step: (0,) * len(shape))

    def quarter_of(rows, offset=0):
        return pl.BlockSpec((rows, width), lambda step: (0, step + offset))

    small = struct((heads, length))
    result = struct((length, wide), BF16)
    tokens_result = struct((length, state), BF16)
    group_sum = struct((part + 8, width))
    tokens = all_of(length, state)
    columns = all_of(length, LANES)
    by_heads = all_of(heads, length)
    all_cols, all_rows = all_of(3, length, LANES), all_of(3, heads, length)
    row = all_of(1, heads)
    by_quarter = quarter_of(length)
    spread_quarter = quarter_of(LANES)
    shares = pltpu.VMEM((GROUP, part, width), F32)
    long_shares = pltpu.VMEM((GROUP, part + 8, width), F32)

    share = struct((part, width))
    out = call(
        states_kernel,
        "states",
        [struct((2 * part + 8, width))] * GROUP + [struct((3, length, LANES), BF16), struct((3, heads, length))],
        [SMEM] + [VMEM] * 8,
        4,
        60,
        scratch_shapes=[pltpu.VMEM((state, width), F32)],
    )(doc_starts, logits, bias, decay, spread, features, writes, cotangent, reads)
    came = swap(out[:GROUP])
    cols, head_rows = out[GROUP:]

    wide_part, wide_piece = struct((length, wide)), struct((length, wide), BF16)
    wide_parts = [wide_part] * 2 + [struct((1, wide))] * 2 + [wide_piece] * 4
    token_part = struct((length, state))
    square = all_of(length, length)
    inner_args = (doc_starts, cols, head_rows, features, cotangent, writes, reads, skip, spread)

    def inner(offset, count, begun, after):
        mine, thin = quarter_of(length, offset), quarter_of(1, offset)
        last = offset + count == QUARTERS
        n_args = len(inner_args) + 1
        return call(
            functools.partial(inner_kernel, offset, last),
            "inner_" + str(offset),
            wide_parts + ([token_part] * 2 if last else [struct((length, length))]),
            [SMEM, all_cols, all_rows, mine, mine, tokens, tokens, row, quarter_of(LANES, offset)]
            + ([square] + [ANY] * WIDE_PARTS if offset else [])
            + [ANY] * AFTER,
            5 * count,
            24,
            grid=(count,),
            out_specs=[mine, mine, thin, thin] + [mine] * 4 + ([tokens] * 2 if last else [square]),
            scratch_shapes=[pltpu.VMEM((length, length), F32)] * 3,
            input_output_aliases={n_args + at: at for at in range(WIDE_PARTS)} if offset else {},
        )(*inner_args, *begun, *after)

    inside, feature_part, skip_part, skip_wide, *pieces, write_part, read_part = inner(
        0, QUARTERS, [], [came[1], came[6]]
    )
    two = blocks == 2 * GROUP
    *group_sums, keeps = call(
        functools.partial(group_kernel, part),
        "group",
        [group_sum] * (1 if two else 2) + [struct((GROUP, width))],
        [VMEM] * GROUP + [ANY],
        2,
        12,
        scratch_shapes=[long_shares, shares],
    )(*came, write_part)
    if two:
        near, far = [], [exchange(group_sums[0], GROUP)]
    else:
        near, far = scan(group_sums[0], 1), scan(group_sums[1], -1)

    def give_back(second, arrivals):
        return swap(
            call(
                functools.partial(spread_kernel, part, two, second),
                "spread",
                [share] * GROUP,
                [VMEM] * (GROUP + 1 + len(arrivals)),
                2,
                12,
                scratch_shapes=[long_shares, shares, shares],
            )(*came, keeps, *arrivals)
        )

    sets = [*give_back(False, near), *give_back(True, far)]
    devices = blocks * members
    whole_shares = [all_of(part, width)] * GROUP
    mixed, feature_grad, step_grad, sums = call(
        functools.partial(finish_kernel, two),
        "finish",
        [result, result, small, struct((devices, 1, LANES))],
        [by_heads, row, row, all_cols, all_rows, spread_quarter, by_quarter, by_quarter, tokens, tokens]
        + [by_quarter] * 2
        + [quarter_of(1)] * 2
        + whole_shares * 2,
        8,
        24,
        grid=(QUARTERS,),
        out_specs=[by_quarter, by_quarter, by_heads, all_of(devices, 1, LANES)],
        scratch_shapes=[pltpu.VMEM((length, LANES), F32)] * 2 + [pltpu.VMEM((8, LANES), F32)] * 2 + [shares] * 2,
    )(
        logits, bias, decay, cols, head_rows, spread, features, cotangent, writes, reads,
        inside, feature_part, skip_part, skip_wide, *sets,
    )
    write_grad, read_grad = call(
        functools.partial(keys_kernel, two),
        "keys",
        [tokens_result] * 2,
        [tokens] * 2 + [by_quarter] * 4 + whole_shares * 2 + [ANY],
        6,
        60,
        grid=(QUARTERS,),
        out_specs=[tokens] * 2,
        scratch_shapes=[pltpu.VMEM((length, 2 * state), F32)] * 2 + [shares] * 2,
    )(write_part, read_part, *pieces, *sets, step_grad)
    sums = jnp.sum(lax.all_to_all(sums, ("dp", "ctx"), 0, 0), axis=(0, 1))
    return (
        mixed[None],
        feature_grad[None],
        write_grad[None],
        read_grad[None],
        step_grad[None],
        sums[:heads],
        sums[heads : 2 * heads],
        sums[2 * heads : 3 * heads],
    )


def solution(mesh):
    by_tokens = P("dp", "ctx", None)
    by_heads = P("dp", None, "ctx")
    in_specs = (by_tokens, by_tokens, by_tokens, by_heads, P(), P(), P(), P("dp", None), by_tokens)
    out_specs = (by_tokens, by_tokens, by_tokens, by_tokens, by_heads, P(), P(), P())
    return jax.shard_map(local, mesh=mesh, in_specs=in_specs, out_specs=out_specs, check_vma=False)
```

```python
import functools

import jax
import jax.numpy as jnp
import numpy as np
from jax import lax
from jax.experimental import pallas as pl
from jax.experimental.pallas import tpu as pltpu
from jax.sharding import PartitionSpec as P

F32 = jnp.float32
BF16 = jnp.bfloat16
QUARTERS = 4
HALVES = 2
GROUP = QUARTERS * HALVES
DISTANCES = (1, 2, 3, 4, 5, 6, 7)
ARRIVALS = (0, *DISTANCES)
LANES = 128
LOG2E = 1.4426950408889634
FAR = -1e30
VMEM = pl.BlockSpec(memory_space=pltpu.VMEM)
SMEM = pl.BlockSpec(memory_space=pltpu.SMEM)
ANY = pl.BlockSpec(memory_space=pl.ANY)
WIDE_PARTS = 4
AFTER = 2
CUM, WEIGHT, FACTOR = 0, 1, 2
STRIDE, LOG = 1, 2


def iota(shape, axis):
    return lax.broadcasted_iota(jnp.int32, shape, axis)


def matmul(left, right):
    return lax.dot_general(left, right, (((1,), (0,)), ((), ())), preferred_element_type=F32)


def matmul_nt(left, right):
    return lax.dot_general(left, right, (((1,), (1,)), ((), ())), preferred_element_type=F32)


def split2(value):
    high = value.astype(BF16)
    return high, (value - high.astype(F32)).astype(BF16)


def split3(value):
    high = value.astype(BF16)
    rest = value - high.astype(F32)
    middle = rest.astype(BF16)
    return high, middle, (rest - middle.astype(F32)).astype(BF16)


def column(row):
    count = row.shape[1]
    eye = iota((count, count), 0) == iota((count, count), 1)
    return jnp.sum(jnp.where(eye, row, 0.0), axis=1, keepdims=True)


def stacked_columns(rows):
    parts = [part.astype(F32) for part in split3(rows)]
    spare = LANES - 3 * rows.shape[0]
    if spare:
        parts.append(jnp.zeros((spare, rows.shape[1]), F32))
    return jnp.concatenate(parts, axis=0).T.astype(BF16)


def spread_table(heads, head_dim):
    table = np.zeros((LANES, heads * head_dim), np.float32)
    for head in range(heads):
        for part in range(3):
            table[part * heads + head, head * head_dim : (head + 1) * head_dim] = 1.0
    return jnp.asarray(table, BF16)


def softplus(value):
    return jnp.maximum(value, 0.0) + jnp.log1p(jnp.exp(-jnp.abs(value)))


def document_at(starts_ref, position):
    total = jnp.zeros_like(position)
    for entry in range(starts_ref.shape[1]):
        total = total + (starts_ref[0, entry] <= position).astype(jnp.int32)
    return total


def group_place():
    return lax.rem(lax.axis_index("ctx"), GROUP)


def share_out(own, quarter_of_state, places, scratch):
    mine = lax.div(own, QUARTERS)
    part = scratch.shape[0] // HALVES
    for distance in range(QUARTERS):
        scratch[...] = quarter_of_state(lax.rem(own ^ distance, QUARTERS))
        for half in range(HALVES):
            rows = pl.ds(pl.multiple_of((mine ^ half) * part, part), part)
            places[half * QUARTERS + distance][...] = scratch[rows]


def states_kernel(starts, logits, bias, decay, spread_ref, features, writes, cotangent, reads, *refs):
    sends = refs[:GROUP]
    cols_out, rows_out, scratch = refs[GROUP:]
    heads, length = logits.shape
    state = writes.shape[1]
    width = features.shape[1] // QUARTERS
    part = state // HALVES
    first = lax.axis_index("ctx") * length
    own = group_place()
    stride = softplus(logits[...] + column(bias[...]))
    log_decay = stride * column(-jnp.exp(decay[...]))
    upto = jnp.where(iota((length, length), 0) <= iota((length, length), 1), 1.0, 0.0).astype(BF16)
    parts = matmul(jnp.concatenate(split3(log_decay), axis=0), upto)
    cum = parts[:heads] + parts[heads : 2 * heads] + parts[2 * heads :]
    segment = document_at(starts, first + iota((1, length), 1))
    entry = document_at(starts, jnp.full((1, 1), first - 1, jnp.int32))
    leave = document_at(starts, jnp.full((1, 1), first + length - 1, jnp.int32))
    own_last = jnp.where(segment == leave, 1.0, 0.0)
    keep_in = jnp.where(segment == entry, 1.0, 0.0)
    weight_stack = stacked_columns(own_last * jnp.exp(cum[:, length - 1 :] - cum) * stride)
    factor_stack = stacked_columns(keep_in * jnp.exp(cum))
    write_t = writes[...].astype(F32).T.astype(BF16)

    def quarter_of_state(quarter):
        cols = pl.ds(pl.multiple_of(quarter * width, LANES), width)
        high, low = split2(features[:, cols].astype(F32) * matmul(weight_stack, spread_ref[:, cols]))
        return matmul(write_t, high) + matmul(write_t, low)

    share_out(own, quarter_of_state, [send.at[0:part] for send in sends], scratch)
    read_t = reads[...].astype(F32).T.astype(BF16)

    keeps = []

    def back_quarter(quarter):
        cols = pl.ds(pl.multiple_of(quarter * width, LANES), width)
        wide = matmul(factor_stack, spread_ref[:, cols])
        keeps.append(jnp.broadcast_to(wide[length - 1 :], (8, width)))
        high, low = split2(cotangent[:, cols].astype(F32) * wide)
        return matmul(read_t, high) + matmul(read_t, low)

    share_out(own, back_quarter, [send.at[part + 8 :] for send in sends], scratch)
    for distance, send in enumerate(sends):
        send[part : part + 8] = keeps[distance % QUARTERS]
    cols_out[CUM] = stacked_columns(cum * LOG2E)
    cols_out[WEIGHT] = weight_stack
    cols_out[FACTOR] = factor_stack
    rows_out[CUM] = cum * LOG2E - jnp.log2(stride)
    rows_out[STRIDE] = stride
    rows_out[LOG] = log_decay


def inner_kernel(
    offset, last, starts, cols_ref, rows_ref, features, cotangent, writes, reads, skip, spread_ref, *refs
):
    if offset:
        before, refs = refs[0], refs[1 + WIDE_PARTS + AFTER :]
    else:
        refs = refs[AFTER:]
    inside, feature_part, skip_part, skip_wide = refs[:WIDE_PARTS]
    results = refs[WIDE_PARTS:-3]
    scores_ref, mask_ref, grad_ref = refs[-3:]
    length, width = features.shape
    heads = rows_ref.shape[1]
    here = heads // QUARTERS
    head_dim = width // here
    pair = 2 * head_dim
    step = pl.program_id(0)

    @pl.when(step == 0)
    def _():
        first = lax.axis_index("ctx") * length
        segment_row = document_at(starts, first + iota((1, length), 1))
        segment_col = document_at(starts, first + iota((length, 1), 0))
        causal = iota((length, length), 0) >= iota((length, length), 1)
        mask_ref[...] = jnp.where((segment_row == segment_col) & causal, 0.0, FAR)
        scores_ref[...] = matmul_nt(reads[...], writes[...])
        grad_ref[...] = before[...] if offset else jnp.zeros_like(grad_ref)

    skip_wide[...] = wide_skip(skip, heads, spread_ref[...])
    def one_pair(at, carry):
        cols = pl.ds(pl.multiple_of(at * pair, LANES), pair)
        feature = features[:, cols]
        grad = cotangent[:, cols]
        grad_f32 = grad.astype(F32)
        grad_t = grad_f32.T.astype(BF16)
        skip_part[:, cols] = jnp.sum(grad_f32 * feature.astype(F32), axis=0, keepdims=True)
        head = (offset + step) * here + at * 2
        lane = iota((LANES, 2 * LANES), 0)
        wanted = head + lax.div(iota((LANES, 2 * LANES), 1), LANES)
        pick = (lane == wanted) | (lane == wanted + heads) | (lane == wanted + 2 * heads)
        upper = matmul(cols_ref[CUM], jnp.where(pick, 1.0, 0.0).astype(BF16))
        second = iota((LANES, pair), 1) >= head_dim
        back = [None, None]
        for block in range(length // LANES):
            rows = slice(block * LANES, (block + 1) * LANES)
            reach = (block + 1) * LANES
            values = []
            for side in range(2):
                high_row = jnp.concatenate([upper[rows, side * LANES : (side + 1) * LANES]] * (block + 1), axis=1)
                low_row = rows_ref[CUM, pl.ds(head + side, 1), :][:, 0:reach]
                weight = jnp.exp2(high_row - low_row + mask_ref[rows, 0:reach])
                pieces = split2(weight * scores_ref[rows, 0:reach])
                values.append(matmul(jnp.concatenate(pieces, axis=1), jnp.concatenate([feature[0:reach]] * 2, axis=0)))
                grad_rows = grad_t[side * head_dim : (side + 1) * head_dim, rows]
                found = matmul(jnp.concatenate([grad_rows] * 2, axis=1), jnp.concatenate(pieces, axis=0))
                if block:
                    found = jnp.concatenate([found[:, : reach - LANES] + back[side], found[:, reach - LANES :]], axis=1)
                back[side] = found
                only = jnp.where(second == (side == 1), grad_f32[rows], 0.0).astype(BF16)
                grad_ref[rows, 0:reach] += matmul_nt(only, feature[0:reach]) * weight
            inside[rows, cols] = jnp.where(second, values[1], values[0])
        feature_part[:, cols] = jnp.concatenate(back, axis=0).T
        return carry

    lax.fori_loop(0, here // 2, one_pair, 0)

    @pl.when(step == pl.num_programs(0) - 1)
    def _():
        score_grad = grad_ref[...]
        if last:
            write_part, read_part = results
            high, low = split2(score_grad)
            read_part[...] = matmul(high, writes[...]) + matmul(low, writes[...])
            high, low = split2(score_grad.T)
            write_part[...] = matmul(high, reads[...]) + matmul(low, reads[...])
        else:
            results[0][...] = score_grad


def in_order(refs, scratch, back=False):
    own = group_place()
    rows = scratch.shape[1]
    for distance, ref in zip(ARRIVALS, refs):
        first = ref.shape[0] - rows if back else 0
        scratch[own ^ distance] = ref[first : first + rows]


def group_kernel(part, *refs):
    keeps, came, back_came = refs[-3:]
    sums = refs[GROUP + 1 : -3]
    up, down = sums[0], sums[-1]
    in_order(refs[:GROUP], came)
    total = came[0, 0:part]
    keep = came[0, part:]
    for j in range(1, GROUP):
        total = total * came[j, part : part + 1] + came[j, 0:part]
        keep = keep * came[j, part:]
    up[0:part] = total
    up[part:] = keep
    for j in range(GROUP):
        keeps[j : j + 1] = came[j, part : part + 1]
    in_order(refs[:GROUP], back_came, back=True)

    def downward():
        total = back_came[GROUP - 1]
        for j in reversed(range(GROUP - 1)):
            total = total * keeps[j : j + 1] + back_came[j]
        down[0:part] = total
        down[part:] = keep

    if len(sums) == 1:
        pl.when(lax.axis_index("ctx") >= GROUP)(downward)
    else:
        downward()


def arrived(part, came):
    total, keep = came[0][0:part], came[0][part : part + 1]
    for ref in came[1:]:
        total = total + keep * ref[0:part]
        keep = keep * ref[part : part + 1]
    return total, keep


def link_kernel(part, own, *refs):
    total, keep = arrived(part, refs[:-1])
    refs[-1][0:part] = own[0:part] + own[part : part + 1] * total
    refs[-1][part:] = own[part:] * keep


def in_upper():
    return lax.axis_index("ctx") >= GROUP


def spread_kernel(part, two, second, *refs):
    keeps = refs[GROUP]
    arrivals = refs[GROUP + 1 : -3 - GROUP]
    outs = refs[-3 - GROUP : -3]
    came, back_came, give = refs[-3:]

    def start():
        return arrived(part, arrivals)[0] if arrivals else jnp.zeros(give.shape[1:], F32)

    def forward():
        in_order(refs[:GROUP], came)
        total = start()
        for j in range(GROUP):
            give[j] = total
            if j < GROUP - 1:
                total = total * keeps[j : j + 1] + came[j, 0:part]

    def backward():
        in_order(refs[:GROUP], back_came, back=True)
        total = start()
        for j in reversed(range(GROUP)):
            give[j] = total
            if j > 0:
                total = total * keeps[j : j + 1] + back_came[j]

    if two:
        upper = in_upper()
        pl.when(upper == second)(forward)
        pl.when(upper != second)(backward)
    else:
        (backward if second else forward)()
    own = group_place()
    for distance, out in enumerate(outs):
        out[...] = give[own ^ distance]


def both_sets(two, refs, have, back_have):
    sets = refs[:GROUP], refs[GROUP : 2 * GROUP]

    def straight():
        in_order(sets[0], have)
        in_order(sets[1], back_have)

    def crossed():
        in_order(sets[1], have)
        in_order(sets[0], back_have)

    if two:
        upper = in_upper()
        pl.when(upper)(crossed)
        pl.when(jnp.logical_not(upper))(straight)
    else:
        straight()


def head_sums(ref, value, spread):
    high, low = split2(value)
    ref[...] += matmul_nt(high, spread) + matmul_nt(low, spread)


def wide_skip(skip, heads, spread):
    stack = stacked_columns(jnp.broadcast_to(column(skip[...]), (heads, LANES)))
    return matmul(stack[0:16], spread)[0:1]


def quarter_rows(have, step):
    return jnp.concatenate([have[half * QUARTERS + step] for half in range(HALVES)], axis=0)


def summed_onward(value):
    count, length = value.shape
    onward = jnp.where(iota((length, length), 0) >= iota((length, length), 1), 1.0, 0.0).astype(BF16)
    parts = matmul(jnp.concatenate(split3(value), axis=0), onward)
    return parts[:count] + parts[count : 2 * count] + parts[2 * count :]


def finish_kernel(
    two, logits, bias, decay, cols_ref, rows_ref, spread_ref, features, cotangent, writes, reads,
    inside, feature_part, skip_part, skip_wide, *refs,
):
    mixed, feature_grad, step_grad, sums, row_acc, col_acc, last_acc, skip_acc, have, back_have = refs[2 * GROUP :]
    heads, length = logits.shape
    state = writes.shape[1]
    width = features.shape[1]
    step = pl.program_id(0)

    @pl.when(step == 0)
    def _():
        for ref in (row_acc, col_acc, last_acc, skip_acc):
            ref[...] = jnp.zeros_like(ref)
        both_sets(two, refs, have, back_have)

    spread = spread_ref[...]
    feature = features[...].astype(F32)
    grad = cotangent[...].astype(F32)
    factor = matmul(cols_ref[FACTOR], spread)
    entering = quarter_rows(have, step)
    stack = jnp.concatenate(split2(entering), axis=0)
    total = inside[...] + factor * matmul(jnp.concatenate([reads[...]] * 2, axis=1), stack)
    mixed[...] = (total + skip_wide[...] * feature).astype(BF16)
    head_sums(row_acc, grad * total, spread)
    returning = quarter_rows(back_have, step)
    stack = jnp.concatenate(split2(returning), axis=0)
    carried = matmul(cols_ref[WEIGHT], spread) * matmul(jnp.concatenate([writes[...]] * 2, axis=1), stack)
    total = feature_part[...] + carried
    feature_grad[...] = (total + skip_wide[...] * grad).astype(BF16)
    head_sums(col_acc, feature * total, spread)
    leaving = jnp.sum((returning * entering).reshape(state // 8, 8, width), axis=0) * factor[length - 1 :]
    leaving = leaving + jnp.sum((feature * carried).reshape(length // 8, 8, width), axis=0)
    head_sums(last_acc, leaving, spread)
    head_sums(skip_acc, jnp.broadcast_to(skip_part[...], (8, width)), spread)

    @pl.when(step == QUARTERS - 1)
    def _():
        cols = col_acc[...].T[:heads]
        last = column(jnp.sum(last_acc[...], axis=0, keepdims=True))[:heads]
        log_grad = last + summed_onward(row_acc[...].T[:heads] - cols)
        slope = 1.0 / (1.0 + jnp.exp(-(logits[...] + column(bias[...]))))
        step_value = (cols / rows_ref[STRIDE] + column(-jnp.exp(decay[...])) * log_grad) * slope
        step_grad[...] = step_value
        bias_sum = jnp.sum(step_value, axis=1, keepdims=True)
        decay_sum = jnp.sum(log_grad * rows_ref[LOG], axis=1, keepdims=True)
        skip_sum = column(skip_acc[0:1])[:heads]
        spare = jnp.zeros((LANES - 3 * heads, 1), F32)
        table = jnp.concatenate([bias_sum, decay_sum, skip_sum, spare], axis=0)
        eye = iota((LANES, LANES), 0) == iota((LANES, LANES), 1)
        table = jnp.sum(jnp.where(eye, table, 0.0), axis=0, keepdims=True)
        sums[...] = jnp.broadcast_to(table[None], sums.shape)


def keys_kernel(two, write_part, read_part, cols_ref, spread_ref, features, cotangent, *refs):
    write_grad, read_grad, write_acc, read_acc, have, back_have = refs[2 * GROUP + 1 :]
    state = write_part.shape[1]
    step = pl.program_id(0)

    @pl.when(step == 0)
    def _():
        write_acc[...] = jnp.zeros_like(write_acc)
        read_acc[...] = jnp.zeros_like(read_acc)
        both_sets(two, refs, have, back_have)

    for states, scale, wide, acc in (
        (have, FACTOR, cotangent, read_acc),
        (back_have, WEIGHT, features, write_acc),
    ):
        stack = jnp.concatenate(split2(quarter_rows(states, step)), axis=0)
        high, low = split2(matmul(cols_ref[scale], spread_ref[...]) * wide[...].astype(F32))
        acc[...] += matmul_nt(high, stack) + matmul_nt(low, stack)

    @pl.when(step == QUARTERS - 1)
    def _():
        write_grad[...] = (write_part[...] + write_acc[:, :state] + write_acc[:, state:]).astype(BF16)
        read_grad[...] = (read_part[...] + read_acc[:, :state] + read_acc[:, state:]).astype(BF16)


def call(kernel, name, outs, in_specs, work, mib, **more):
    return pl.pallas_call(
        kernel,
        out_shape=outs,
        in_specs=in_specs,
        out_specs=more.pop("out_specs", [VMEM] * len(outs)),
        compiler_params=pltpu.CompilerParams(vmem_limit_bytes=mib * 2**20),
        cost_estimate=pl.CostEstimate(flops=work * 10**9, bytes_accessed=10**6, transcendentals=0),
        name=name,
        **more,
    )


def struct(shape, dtype=F32):
    return jax.ShapeDtypeStruct(shape, dtype)


def local(
    features, write_keys, read_queries, step_logits, step_bias, decay_log, skip_gain, doc_starts, out_grad
):
    features, writes, reads, logits, cotangent = (
        features[0], write_keys[0], read_queries[0], step_logits[0], out_grad[0]
    )
    length, wide = features.shape
    heads = logits.shape[0]
    state = writes.shape[1]
    head_dim = wide // heads
    width = wide // QUARTERS
    part = state // HALVES
    bias, decay, skip = step_bias[None], decay_log[None], skip_gain[None]
    blocks, members = lax.axis_size("ctx"), lax.axis_size("dp")
    spread = spread_table(heads, head_dim)

    def exchange(value, distance):
        return lax.ppermute(value, "ctx", [(k, k ^ distance) for k in range(blocks)])

    def swap(values):
        return [values[0]] + [exchange(values[d], d) for d in DISTANCES]

    def shift(value, distance):
        pairs = [(k, k + distance) for k in range(blocks) if 0 <= k + distance < blocks]
        return lax.ppermute(value, "ctx", pairs)

    def scan(own, sign):
        came, near, reach = [], own, 1
        while reach < blocks // GROUP:
            came.append(shift(near, sign * GROUP * reach))
            reach *= 2
            if reach < blocks // GROUP:
                near = call(
                    functools.partial(link_kernel, part), "link", [group_sum], [VMEM] * (1 + len(came)), 1, 8
                )(own, *came)[0]
        return came

    def all_of(*shape):
        return pl.BlockSpec(shape, lambda step: (0,) * len(shape))

    def quarter_of(rows, offset=0):
        return pl.BlockSpec((rows, width), lambda step: (0, step + offset))

    small = struct((heads, length))
    result = struct((length, wide), BF16)
    tokens_result = struct((length, state), BF16)
    group_sum = struct((part + 8, width))
    tokens = all_of(length, state)
    columns = all_of(length, LANES)
    by_heads = all_of(heads, length)
    all_cols, all_rows = all_of(3, length, LANES), all_of(3, heads, length)
    row = all_of(1, heads)
    by_quarter = quarter_of(length)
    spread_quarter = quarter_of(LANES)
    shares = pltpu.VMEM((GROUP, part, width), F32)
    long_shares = pltpu.VMEM((GROUP, part + 8, width), F32)

    share = struct((part, width))
    out = call(
        states_kernel,
        "states",
        [struct((2 * part + 8, width))] * GROUP + [struct((3, length, LANES), BF16), struct((3, heads, length))],
        [SMEM] + [VMEM] * 8,
        4,
        60,
        scratch_shapes=[pltpu.VMEM((state, width), F32)],
    )(doc_starts, logits, bias, decay, spread, features, writes, cotangent, reads)
    came = swap(out[:GROUP])
    cols, head_rows = out[GROUP:]

    wide_parts = [struct((length, wide))] * 2 + [struct((1, wide))] * 2
    token_part = struct((length, state))
    square = all_of(length, length)
    inner_args = (doc_starts, cols, head_rows, features, cotangent, writes, reads, skip, spread)

    def inner(offset, count, begun, after):
        mine, thin = quarter_of(length, offset), quarter_of(1, offset)
        last = offset + count == QUARTERS
        n_args = len(inner_args) + 1
        return call(
            functools.partial(inner_kernel, offset, last),
            "inner_" + str(offset),
            wide_parts + ([token_part] * 2 if last else [struct((length, length))]),
            [SMEM, all_cols, all_rows, mine, mine, tokens, tokens, row, quarter_of(LANES, offset)]
            + ([square] + [ANY] * WIDE_PARTS if offset else [])
            + [ANY] * AFTER,
            5 * count,
            24,
            grid=(count,),
            out_specs=[mine, mine, thin, thin] + ([tokens] * 2 if last else [square]),
            scratch_shapes=[pltpu.VMEM((length, length), F32)] * 3,
            input_output_aliases={n_args + at: at for at in range(WIDE_PARTS)} if offset else {},
        )(*inner_args, *begun, *after)

    inside, feature_part, skip_part, skip_wide, write_part, read_part = inner(
        0, QUARTERS, [], [came[1], came[6]]
    )
    two = blocks == 2 * GROUP
    *group_sums, keeps = call(
        functools.partial(group_kernel, part),
        "group",
        [group_sum] * (1 if two else 2) + [struct((GROUP, width))],
        [VMEM] * GROUP + [ANY],
        2,
        12,
        scratch_shapes=[long_shares, shares],
    )(*came, write_part)
    if two:
        near, far = [], [exchange(group_sums[0], GROUP)]
    else:
        near, far = scan(group_sums[0], 1), scan(group_sums[1], -1)

    def give_back(second, arrivals):
        return swap(
            call(
                functools.partial(spread_kernel, part, two, second),
                "spread",
                [share] * GROUP,
                [VMEM] * (GROUP + 1 + len(arrivals)),
                2,
                12,
                scratch_shapes=[long_shares, shares, shares],
            )(*came, keeps, *arrivals)
        )

    sets = [*give_back(False, near), *give_back(True, far)]
    devices = blocks * members
    whole_shares = [all_of(part, width)] * GROUP
    mixed, feature_grad, step_grad, sums = call(
        functools.partial(finish_kernel, two),
        "finish",
        [result, result, small, struct((devices, 1, LANES))],
        [by_heads, row, row, all_cols, all_rows, spread_quarter, by_quarter, by_quarter, tokens, tokens]
        + [by_quarter] * 2
        + [quarter_of(1)] * 2
        + whole_shares * 2,
        8,
        24,
        grid=(QUARTERS,),
        out_specs=[by_quarter, by_quarter, by_heads, all_of(devices, 1, LANES)],
        scratch_shapes=[pltpu.VMEM((length, LANES), F32)] * 2 + [pltpu.VMEM((8, LANES), F32)] * 2 + [shares] * 2,
    )(
        logits, bias, decay, cols, head_rows, spread, features, cotangent, writes, reads,
        inside, feature_part, skip_part, skip_wide, *sets,
    )
    write_grad, read_grad = call(
        functools.partial(keys_kernel, two),
        "keys",
        [tokens_result] * 2,
        [tokens] * 2 + [all_cols, spread_quarter] + [by_quarter] * 2 + whole_shares * 2 + [ANY],
        6,
        60,
        grid=(QUARTERS,),
        out_specs=[tokens] * 2,
        scratch_shapes=[pltpu.VMEM((length, 2 * state), F32)] * 2 + [shares] * 2,
    )(write_part, read_part, cols, spread, features, cotangent, *sets, step_grad)
    sums = jnp.sum(lax.all_to_all(sums, ("dp", "ctx"), 0, 0), axis=(0, 1))
    return (
        mixed[None],
        feature_grad[None],
        write_grad[None],
        read_grad[None],
        step_grad[None],
        sums[:heads],
        sums[heads : 2 * heads],
        sums[2 * heads : 3 * heads],
    )


def solution(mesh):
    by_tokens = P("dp", "ctx", None)
    by_heads = P("dp", None, "ctx")
    in_specs = (by_tokens, by_tokens, by_tokens, by_heads, P(), P(), P(), P("dp", None), by_tokens)
    out_specs = (by_tokens, by_tokens, by_tokens, by_tokens, by_heads, P(), P(), P())
    return jax.shard_map(local, mesh=mesh, in_specs=in_specs, out_specs=out_specs, check_vma=False)
```

```python
import functools

import jax
import jax.numpy as jnp
import numpy as np
from jax import lax
from jax.experimental import pallas as pl
from jax.experimental.pallas import tpu as pltpu
from jax.sharding import PartitionSpec as P

F32 = jnp.float32
BF16 = jnp.bfloat16
QUARTERS = 4
HALVES = 2
GROUP = QUARTERS * HALVES
DISTANCES = (1, 6, 2, 5, 3, 4, 7)
ARRIVALS = (0, *DISTANCES)
LANES = 128
LOG2E = 1.4426950408889634
FAR = -1e30
VMEM = pl.BlockSpec(memory_space=pltpu.VMEM)
SMEM = pl.BlockSpec(memory_space=pltpu.SMEM)
ANY = pl.BlockSpec(memory_space=pl.ANY)
WIDE_PARTS = 8
AFTER = 2
CUM, WEIGHT, FACTOR = 0, 1, 2
STRIDE, LOG = 1, 2


def iota(shape, axis):
    return lax.broadcasted_iota(jnp.int32, shape, axis)


def matmul(left, right):
    return lax.dot_general(left, right, (((1,), (0,)), ((), ())), preferred_element_type=F32)


def matmul_nt(left, right):
    return lax.dot_general(left, right, (((1,), (1,)), ((), ())), preferred_element_type=F32)


def split2(value):
    high = value.astype(BF16)
    return high, (value - high.astype(F32)).astype(BF16)


def split3(value):
    high = value.astype(BF16)
    rest = value - high.astype(F32)
    middle = rest.astype(BF16)
    return high, middle, (rest - middle.astype(F32)).astype(BF16)


def column(row):
    count = row.shape[1]
    eye = iota((count, count), 0) == iota((count, count), 1)
    return jnp.sum(jnp.where(eye, row, 0.0), axis=1, keepdims=True)


def stacked_columns(rows):
    parts = [part.astype(F32) for part in split3(rows)]
    spare = LANES - 3 * rows.shape[0]
    if spare:
        parts.append(jnp.zeros((spare, rows.shape[1]), F32))
    return jnp.concatenate(parts, axis=0).T.astype(BF16)


def spread_table(heads, head_dim):
    table = np.zeros((LANES, heads * head_dim), np.float32)
    for head in range(heads):
        for part in range(3):
            table[part * heads + head, head * head_dim : (head + 1) * head_dim] = 1.0
    return jnp.asarray(table, BF16)


def softplus(value):
    return jnp.maximum(value, 0.0) + jnp.log1p(jnp.exp(-jnp.abs(value)))


def document_at(starts_ref, position):
    total = jnp.zeros_like(position)
    for entry in range(starts_ref.shape[1]):
        total = total + (starts_ref[0, entry] <= position).astype(jnp.int32)
    return total


def group_place():
    return lax.rem(lax.axis_index("ctx"), GROUP)


def share_out(own, quarter_of_state, places, scratch):
    mine = lax.div(own, QUARTERS)
    part = scratch.shape[0] // HALVES
    for distance in range(QUARTERS):
        scratch[...] = quarter_of_state(lax.rem(own ^ distance, QUARTERS))
        for half in range(HALVES):
            rows = pl.ds(pl.multiple_of((mine ^ half) * part, part), part)
            places[half * QUARTERS + distance][...] = scratch[rows]


def states_kernel(starts, logits, bias, decay, spread_ref, features, writes, cotangent, reads, *refs):
    sends = refs[:GROUP]
    cols_out, rows_out, scratch = refs[GROUP:]
    heads, length = logits.shape
    state = writes.shape[1]
    width = features.shape[1] // QUARTERS
    part = state // HALVES
    first = lax.axis_index("ctx") * length
    own = group_place()
    stride = softplus(logits[...] + column(bias[...]))
    log_decay = stride * column(-jnp.exp(decay[...]))
    upto = jnp.where(iota((length, length), 0) <= iota((length, length), 1), 1.0, 0.0).astype(BF16)
    parts = matmul(jnp.concatenate(split3(log_decay), axis=0), upto)
    cum = parts[:heads] + parts[heads : 2 * heads] + parts[2 * heads :]
    segment = document_at(starts, first + iota((1, length), 1))
    entry = document_at(starts, jnp.full((1, 1), first - 1, jnp.int32))
    leave = document_at(starts, jnp.full((1, 1), first + length - 1, jnp.int32))
    own_last = jnp.where(segment == leave, 1.0, 0.0)
    keep_in = jnp.where(segment == entry, 1.0, 0.0)
    weight_stack = stacked_columns(own_last * jnp.exp(cum[:, length - 1 :] - cum) * stride)
    factor_stack = stacked_columns(keep_in * jnp.exp(cum))
    write_t = writes[...].astype(F32).T.astype(BF16)

    def quarter_of_state(quarter):
        cols = pl.ds(pl.multiple_of(quarter * width, LANES), width)
        high, low = split2(features[:, cols].astype(F32) * matmul(weight_stack, spread_ref[:, cols]))
        return matmul(write_t, high) + matmul(write_t, low)

    share_out(own, quarter_of_state, [send.at[0:part] for send in sends], scratch)
    read_t = reads[...].astype(F32).T.astype(BF16)

    keeps = []

    def back_quarter(quarter):
        cols = pl.ds(pl.multiple_of(quarter * width, LANES), width)
        wide = matmul(factor_stack, spread_ref[:, cols])
        keeps.append(jnp.broadcast_to(wide[length - 1 :], (8, width)))
        high, low = split2(cotangent[:, cols].astype(F32) * wide)
        return matmul(read_t, high) + matmul(read_t, low)

    share_out(own, back_quarter, [send.at[part + 8 :] for send in sends], scratch)
    for distance, send in enumerate(sends):
        send[part : part + 8] = keeps[distance % QUARTERS]
    cols_out[CUM] = stacked_columns(cum * LOG2E)
    cols_out[WEIGHT] = weight_stack
    cols_out[FACTOR] = factor_stack
    rows_out[CUM] = cum * LOG2E - jnp.log2(stride)
    rows_out[STRIDE] = stride
    rows_out[LOG] = log_decay


def inner_kernel(
    offset, last, starts, cols_ref, rows_ref, features, cotangent, writes, reads, skip, spread_ref, *refs
):
    if offset:
        before, refs = refs[0], refs[1 + WIDE_PARTS + AFTER :]
    else:
        refs = refs[AFTER:]
    inside, feature_part, skip_part, skip_wide, write_high, write_low, read_high, read_low = refs[:WIDE_PARTS]
    results = refs[WIDE_PARTS:-3]
    scores_ref, mask_ref, grad_ref = refs[-3:]
    length, width = features.shape
    heads = rows_ref.shape[1]
    here = heads // QUARTERS
    head_dim = width // here
    pair = 2 * head_dim
    step = pl.program_id(0)

    @pl.when(step == 0)
    def _():
        first = lax.axis_index("ctx") * length
        segment_row = document_at(starts, first + iota((1, length), 1))
        segment_col = document_at(starts, first + iota((length, 1), 0))
        causal = iota((length, length), 0) >= iota((length, length), 1)
        mask_ref[...] = jnp.where((segment_row == segment_col) & causal, 0.0, FAR)
        scores_ref[...] = matmul_nt(reads[...], writes[...])
        grad_ref[...] = before[...] if offset else jnp.zeros_like(grad_ref)

    skip_wide[...] = wide_skip(skip, heads, spread_ref[...])
    write_high[...], write_low[...] = split2(matmul(cols_ref[WEIGHT], spread_ref[...]) * features[...].astype(F32))
    read_high[...], read_low[...] = split2(matmul(cols_ref[FACTOR], spread_ref[...]) * cotangent[...].astype(F32))

    def one_pair(at, carry):
        cols = pl.ds(pl.multiple_of(at * pair, LANES), pair)
        feature = features[:, cols]
        grad = cotangent[:, cols]
        grad_f32 = grad.astype(F32)
        grad_t = grad_f32.T.astype(BF16)
        skip_part[:, cols] = jnp.sum(grad_f32 * feature.astype(F32), axis=0, keepdims=True)
        head = (offset + step) * here + at * 2
        lane = iota((LANES, 2 * LANES), 0)
        wanted = head + lax.div(iota((LANES, 2 * LANES), 1), LANES)
        pick = (lane == wanted) | (lane == wanted + heads) | (lane == wanted + 2 * heads)
        upper = matmul(cols_ref[CUM], jnp.where(pick, 1.0, 0.0).astype(BF16))
        second = iota((LANES, pair), 1) >= head_dim
        back = [None, None]
        for block in range(length // LANES):
            rows = slice(block * LANES, (block + 1) * LANES)
            reach = (block + 1) * LANES
            values = []
            for side in range(2):
                high_row = jnp.concatenate([upper[rows, side * LANES : (side + 1) * LANES]] * (block + 1), axis=1)
                low_row = rows_ref[CUM, pl.ds(head + side, 1), :][:, 0:reach]
                weight = jnp.exp2(high_row - low_row + mask_ref[rows, 0:reach])
                pieces = split2(weight * scores_ref[rows, 0:reach])
                values.append(matmul(jnp.concatenate(pieces, axis=1), jnp.concatenate([feature[0:reach]] * 2, axis=0)))
                grad_rows = grad_t[side * head_dim : (side + 1) * head_dim, rows]
                found = matmul(jnp.concatenate([grad_rows] * 2, axis=1), jnp.concatenate(pieces, axis=0))
                if block:
                    found = jnp.concatenate([found[:, : reach - LANES] + back[side], found[:, reach - LANES :]], axis=1)
                back[side] = found
                only = jnp.where(second == (side == 1), grad_f32[rows], 0.0).astype(BF16)
                grad_ref[rows, 0:reach] += matmul_nt(only, feature[0:reach]) * weight
            inside[rows, cols] = jnp.where(second, values[1], values[0])
        feature_part[:, cols] = jnp.concatenate(back, axis=0).T
        return carry

    lax.fori_loop(0, here // 2, one_pair, 0)

    @pl.when(step == pl.num_programs(0) - 1)
    def _():
        score_grad = grad_ref[...]
        if last:
            write_part, read_part = results
            high, low = split2(score_grad)
            read_part[...] = matmul(high, writes[...]) + matmul(low, writes[...])
            high, low = split2(score_grad.T)
            write_part[...] = matmul(high, reads[...]) + matmul(low, reads[...])
        else:
            results[0][...] = score_grad


def in_order(refs, scratch, back=False):
    own = group_place()
    rows = scratch.shape[1]
    for distance, ref in zip(ARRIVALS, refs):
        first = ref.shape[0] - rows if back else 0
        scratch[own ^ distance] = ref[first : first + rows]


def group_kernel(part, *refs):
    keeps, came, back_came = refs[-3:]
    sums = refs[GROUP + 1 : -3]
    up, down = sums[0], sums[-1]
    in_order(refs[:GROUP], came)
    total = came[0, 0:part]
    keep = came[0, part:]
    for j in range(1, GROUP):
        total = total * came[j, part : part + 1] + came[j, 0:part]
        keep = keep * came[j, part:]
    up[0:part] = total
    up[part:] = keep
    for j in range(GROUP):
        keeps[j : j + 1] = came[j, part : part + 1]
    in_order(refs[:GROUP], back_came, back=True)

    def downward():
        total = back_came[GROUP - 1]
        for j in reversed(range(GROUP - 1)):
            total = total * keeps[j : j + 1] + back_came[j]
        down[0:part] = total
        down[part:] = keep

    if len(sums) == 1:
        pl.when(lax.axis_index("ctx") >= GROUP)(downward)
    else:
        downward()


def arrived(part, came):
    total, keep = came[0][0:part], came[0][part : part + 1]
    for ref in came[1:]:
        total = total + keep * ref[0:part]
        keep = keep * ref[part : part + 1]
    return total, keep


def link_kernel(part, own, *refs):
    total, keep = arrived(part, refs[:-1])
    refs[-1][0:part] = own[0:part] + own[part : part + 1] * total
    refs[-1][part:] = own[part:] * keep


def in_upper():
    return lax.axis_index("ctx") >= GROUP


def spread_kernel(part, two, second, *refs):
    keeps = refs[GROUP]
    arrivals = refs[GROUP + 1 : -3 - GROUP]
    outs = refs[-3 - GROUP : -3]
    came, back_came, give = refs[-3:]

    def start():
        return arrived(part, arrivals)[0] if arrivals else jnp.zeros(give.shape[1:], F32)

    def forward():
        in_order(refs[:GROUP], came)
        total = start()
        for j in range(GROUP):
            give[j] = total
            if j < GROUP - 1:
                total = total * keeps[j : j + 1] + came[j, 0:part]

    def backward():
        in_order(refs[:GROUP], back_came, back=True)
        total = start()
        for j in reversed(range(GROUP)):
            give[j] = total
            if j > 0:
                total = total * keeps[j : j + 1] + back_came[j]

    if two:
        upper = in_upper()
        pl.when(upper == second)(forward)
        pl.when(upper != second)(backward)
    else:
        (backward if second else forward)()
    own = group_place()
    for distance, out in enumerate(outs):
        out[...] = give[own ^ distance]


def both_sets(two, refs, have, back_have):
    sets = refs[:GROUP], refs[GROUP : 2 * GROUP]

    def straight():
        in_order(sets[0], have)
        in_order(sets[1], back_have)

    def crossed():
        in_order(sets[1], have)
        in_order(sets[0], back_have)

    if two:
        upper = in_upper()
        pl.when(upper)(crossed)
        pl.when(jnp.logical_not(upper))(straight)
    else:
        straight()


def head_sums(ref, value, spread):
    high, low = split2(value)
    ref[...] += matmul_nt(high, spread) + matmul_nt(low, spread)


def wide_skip(skip, heads, spread):
    stack = stacked_columns(jnp.broadcast_to(column(skip[...]), (heads, LANES)))
    return matmul(stack[0:16], spread)[0:1]


def quarter_rows(have, step):
    return jnp.concatenate([have[half * QUARTERS + step] for half in range(HALVES)], axis=0)


def summed_onward(value):
    count, length = value.shape
    onward = jnp.where(iota((length, length), 0) >= iota((length, length), 1), 1.0, 0.0).astype(BF16)
    parts = matmul(jnp.concatenate(split3(value), axis=0), onward)
    return parts[:count] + parts[count : 2 * count] + parts[2 * count :]


def finish_kernel(
    two, logits, bias, decay, cols_ref, rows_ref, spread_ref, features, cotangent, writes, reads,
    inside, feature_part, skip_part, skip_wide, *refs,
):
    mixed, feature_grad, step_grad, sums, row_acc, col_acc, last_acc, skip_acc, have, back_have = refs[2 * GROUP :]
    heads, length = logits.shape
    state = writes.shape[1]
    width = features.shape[1]
    step = pl.program_id(0)

    @pl.when(step == 0)
    def _():
        for ref in (row_acc, col_acc, last_acc, skip_acc):
            ref[...] = jnp.zeros_like(ref)
        both_sets(two, refs, have, back_have)

    spread = spread_ref[...]
    feature = features[...].astype(F32)
    grad = cotangent[...].astype(F32)
    factor = matmul(cols_ref[FACTOR], spread)
    entering = quarter_rows(have, step)
    stack = jnp.concatenate(split2(entering), axis=0)
    total = inside[...] + factor * matmul(jnp.concatenate([reads[...]] * 2, axis=1), stack)
    mixed[...] = (total + skip_wide[...] * feature).astype(BF16)
    head_sums(row_acc, grad * total, spread)
    returning = quarter_rows(back_have, step)
    stack = jnp.concatenate(split2(returning), axis=0)
    carried = matmul(cols_ref[WEIGHT], spread) * matmul(jnp.concatenate([writes[...]] * 2, axis=1), stack)
    total = feature_part[...] + carried
    feature_grad[...] = (total + skip_wide[...] * grad).astype(BF16)
    head_sums(col_acc, feature * total, spread)
    leaving = jnp.sum((returning * entering).reshape(state // 8, 8, width), axis=0) * factor[length - 1 :]
    leaving = leaving + jnp.sum((feature * carried).reshape(length // 8, 8, width), axis=0)
    head_sums(last_acc, leaving, spread)
    head_sums(skip_acc, jnp.broadcast_to(skip_part[...], (8, width)), spread)

    @pl.when(step == QUARTERS - 1)
    def _():
        cols = col_acc[...].T[:heads]
        last = column(jnp.sum(last_acc[...], axis=0, keepdims=True))[:heads]
        log_grad = last + summed_onward(row_acc[...].T[:heads] - cols)
        slope = 1.0 / (1.0 + jnp.exp(-(logits[...] + column(bias[...]))))
        step_value = (cols / rows_ref[STRIDE] + column(-jnp.exp(decay[...])) * log_grad) * slope
        step_grad[...] = step_value
        bias_sum = jnp.sum(step_value, axis=1, keepdims=True)
        decay_sum = jnp.sum(log_grad * rows_ref[LOG], axis=1, keepdims=True)
        skip_sum = column(skip_acc[0:1])[:heads]
        spare = jnp.zeros((LANES - 3 * heads, 1), F32)
        table = jnp.concatenate([bias_sum, decay_sum, skip_sum, spare], axis=0)
        eye = iota((LANES, LANES), 0) == iota((LANES, LANES), 1)
        table = jnp.sum(jnp.where(eye, table, 0.0), axis=0, keepdims=True)
        sums[...] = jnp.broadcast_to(table[None], sums.shape)


def keys_kernel(two, write_part, read_part, write_high, write_low, read_high, read_low, *refs):
    write_grad, read_grad, write_acc, read_acc, have, back_have = refs[2 * GROUP + 1 :]
    state = write_part.shape[1]
    step = pl.program_id(0)

    @pl.when(step == 0)
    def _():
        write_acc[...] = jnp.zeros_like(write_acc)
        read_acc[...] = jnp.zeros_like(read_acc)
        both_sets(two, refs, have, back_have)

    for states, high, low, acc in (
        (have, read_high, read_low, read_acc),
        (back_have, write_high, write_low, write_acc),
    ):
        stack = jnp.concatenate(split2(quarter_rows(states, step)), axis=0)
        acc[...] += matmul_nt(high[...], stack) + matmul_nt(low[...], stack)

    @pl.when(step == QUARTERS - 1)
    def _():
        write_grad[...] = (write_part[...] + write_acc[:, :state] + write_acc[:, state:]).astype(BF16)
        read_grad[...] = (read_part[...] + read_acc[:, :state] + read_acc[:, state:]).astype(BF16)


def call(kernel, name, outs, in_specs, work, mib, **more):
    return pl.pallas_call(
        kernel,
        out_shape=outs,
        in_specs=in_specs,
        out_specs=more.pop("out_specs", [VMEM] * len(outs)),
        compiler_params=pltpu.CompilerParams(vmem_limit_bytes=mib * 2**20),
        cost_estimate=pl.CostEstimate(flops=work * 10**9, bytes_accessed=10**6, transcendentals=0),
        name=name,
        **more,
    )


def struct(shape, dtype=F32):
    return jax.ShapeDtypeStruct(shape, dtype)


def local(
    features, write_keys, read_queries, step_logits, step_bias, decay_log, skip_gain, doc_starts, out_grad
):
    features, writes, reads, logits, cotangent = (
        features[0], write_keys[0], read_queries[0], step_logits[0], out_grad[0]
    )
    length, wide = features.shape
    heads = logits.shape[0]
    state = writes.shape[1]
    head_dim = wide // heads
    width = wide // QUARTERS
    part = state // HALVES
    bias, decay, skip = step_bias[None], decay_log[None], skip_gain[None]
    blocks, members = lax.axis_size("ctx"), lax.axis_size("dp")
    spread = spread_table(heads, head_dim)

    def exchange(value, distance):
        return lax.ppermute(value, "ctx", [(k, k ^ distance) for k in range(blocks)])

    def swap(values):
        return [values[0]] + [exchange(values[d], d) for d in DISTANCES]

    def shift(value, distance):
        pairs = [(k, k + distance) for k in range(blocks) if 0 <= k + distance < blocks]
        return lax.ppermute(value, "ctx", pairs)

    def scan(own, sign):
        came, near, reach = [], own, 1
        while reach < blocks // GROUP:
            came.append(shift(near, sign * GROUP * reach))
            reach *= 2
            if reach < blocks // GROUP:
                near = call(
                    functools.partial(link_kernel, part), "link", [group_sum], [VMEM] * (1 + len(came)), 1, 8
                )(own, *came)[0]
        return came

    def all_of(*shape):
        return pl.BlockSpec(shape, lambda step: (0,) * len(shape))

    def quarter_of(rows, offset=0):
        return pl.BlockSpec((rows, width), lambda step: (0, step + offset))

    small = struct((heads, length))
    result = struct((length, wide), BF16)
    tokens_result = struct((length, state), BF16)
    group_sum = struct((part + 8, width))
    tokens = all_of(length, state)
    columns = all_of(length, LANES)
    by_heads = all_of(heads, length)
    all_cols, all_rows = all_of(3, length, LANES), all_of(3, heads, length)
    row = all_of(1, heads)
    by_quarter = quarter_of(length)
    spread_quarter = quarter_of(LANES)
    shares = pltpu.VMEM((GROUP, part, width), F32)
    long_shares = pltpu.VMEM((GROUP, part + 8, width), F32)

    share = struct((part, width))
    out = call(
        states_kernel,
        "states",
        [struct((2 * part + 8, width))] * GROUP + [struct((3, length, LANES), BF16), struct((3, heads, length))],
        [SMEM] + [VMEM] * 8,
        4,
        60,
        scratch_shapes=[pltpu.VMEM((state, width), F32)],
    )(doc_starts, logits, bias, decay, spread, features, writes, cotangent, reads)
    came = swap(out[:GROUP])
    cols, head_rows = out[GROUP:]

    wide_part, wide_piece = struct((length, wide)), struct((length, wide), BF16)
    wide_parts = [wide_part] * 2 + [struct((1, wide))] * 2 + [wide_piece] * 4
    token_part = struct((length, state))
    square = all_of(length, length)
    inner_args = (doc_starts, cols, head_rows, features, cotangent, writes, reads, skip, spread)

    def inner(offset, count, begun, after):
        mine, thin = quarter_of(length, offset), quarter_of(1, offset)
        last = offset + count == QUARTERS
        n_args = len(inner_args) + 1
        return call(
            functools.partial(inner_kernel, offset, last),
            "inner_" + str(offset),
            wide_parts + ([token_part] * 2 if last else [struct((length, length))]),
            [SMEM, all_cols, all_rows, mine, mine, tokens, tokens, row, quarter_of(LANES, offset)]
            + ([square] + [ANY] * WIDE_PARTS if offset else [])
            + [ANY] * AFTER,
            5 * count,
            24,
            grid=(count,),
            out_specs=[mine, mine, thin, thin] + [mine] * 4 + ([tokens] * 2 if last else [square]),
            scratch_shapes=[pltpu.VMEM((length, length), F32)] * 3,
            input_output_aliases={n_args + at: at for at in range(WIDE_PARTS)} if offset else {},
        )(*inner_args, *begun, *after)

    inside, feature_part, skip_part, skip_wide, *pieces, write_part, read_part = inner(
        0, QUARTERS, [], [came[1], came[2]]
    )
    two = blocks == 2 * GROUP
    *group_sums, keeps = call(
        functools.partial(group_kernel, part),
        "group",
        [group_sum] * (1 if two else 2) + [struct((GROUP, width))],
        [VMEM] * GROUP + [ANY],
        2,
        12,
        scratch_shapes=[long_shares, shares],
    )(*came, write_part)
    if two:
        near, far = [], [exchange(group_sums[0], GROUP)]
    else:
        near, far = scan(group_sums[0], 1), scan(group_sums[1], -1)

    def give_back(second, arrivals):
        return swap(
            call(
                functools.partial(spread_kernel, part, two, second),
                "spread",
                [share] * GROUP,
                [VMEM] * (GROUP + 1 + len(arrivals)),
                2,
                12,
                scratch_shapes=[long_shares, shares, shares],
            )(*came, keeps, *arrivals)
        )

    sets = [*give_back(False, near), *give_back(True, far)]
    devices = blocks * members
    whole_shares = [all_of(part, width)] * GROUP
    mixed, feature_grad, step_grad, sums = call(
        functools.partial(finish_kernel, two),
        "finish",
        [result, result, small, struct((devices, 1, LANES))],
        [by_heads, row, row, all_cols, all_rows, spread_quarter, by_quarter, by_quarter, tokens, tokens]
        + [by_quarter] * 2
        + [quarter_of(1)] * 2
        + whole_shares * 2,
        8,
        24,
        grid=(QUARTERS,),
        out_specs=[by_quarter, by_quarter, by_heads, all_of(devices, 1, LANES)],
        scratch_shapes=[pltpu.VMEM((length, LANES), F32)] * 2 + [pltpu.VMEM((8, LANES), F32)] * 2 + [shares] * 2,
    )(
        logits, bias, decay, cols, head_rows, spread, features, cotangent, writes, reads,
        inside, feature_part, skip_part, skip_wide, *sets,
    )
    write_grad, read_grad = call(
        functools.partial(keys_kernel, two),
        "keys",
        [tokens_result] * 2,
        [tokens] * 2 + [by_quarter] * 4 + whole_shares * 2 + [ANY],
        6,
        60,
        grid=(QUARTERS,),
        out_specs=[tokens] * 2,
        scratch_shapes=[pltpu.VMEM((length, 2 * state), F32)] * 2 + [shares] * 2,
    )(write_part, read_part, *pieces, *sets, step_grad)
    sums = jnp.sum(lax.all_to_all(sums, ("dp", "ctx"), 0, 0), axis=(0, 1))
    return (
        mixed[None],
        feature_grad[None],
        write_grad[None],
        read_grad[None],
        step_grad[None],
        sums[:heads],
        sums[heads : 2 * heads],
        sums[2 * heads : 3 * heads],
    )


def solution(mesh):
    by_tokens = P("dp", "ctx", None)
    by_heads = P("dp", None, "ctx")
    in_specs = (by_tokens, by_tokens, by_tokens, by_heads, P(), P(), P(), P("dp", None), by_tokens)
    out_specs = (by_tokens, by_tokens, by_tokens, by_tokens, by_heads, P(), P(), P())
    return jax.shard_map(local, mesh=mesh, in_specs=in_specs, out_specs=out_specs, check_vma=False)
```
